32 devices in a mesh: dp: 4 (over y, x), depth: 2 (over core), mp: 4 (over z).
Axes of the slice: x: 2, y: 2, z: 4, core: 2. Of those that a mesh axis runs over, the one named last changes fastest.
Arguments:
- tokens: bfloat16 [4096, 2048], P(('dp', 'depth')), may hold values from -6 to 6
- cotangent: bfloat16 [4096, 2048], P(('dp', 'depth')), may hold values from -6 to 6
- lengths: int32 [4, 2, 4], P('dp'), may hold values from 0 to 512, as said below
- bucket_loop_index: int32 [4, 2], P('dp'), may hold values from 0 to 1, as said below
- query_weight: bfloat16 [2048, 2048], P(('dp', 'depth'), 'mp'), may hold values from -0.125 to 0.125
- key_value_weight: bfloat16 [2048, 512], P(('dp', 'depth'), 'mp'), may hold values from -0.125 to 0.125
- output_weight: bfloat16 [2048, 2048], P('mp', ('dp', 'depth')), may hold values from -0.5 to 0.5
- gate_up_weight: bfloat16 [2, 2048, 16384], P(None, ('dp', 'depth'), 'mp'), may hold values from -0.125 to 0.125
- down_weight: bfloat16 [16384, 2048], P('mp', ('dp', 'depth')), may hold values from -0.046875 to 0.046875
- gains: bfloat16 [2, 2048], P(None, ('dp', 'depth')), may hold values from 0.5 to 1.5
- adapter_input_down: bfloat16 [2, 5, 2048, 256], P('depth', None, 'dp'), may hold values from -0.125 to 0.125
- adapter_query_up: bfloat16 [2, 256, 2048], P('depth', 'dp', 'mp'), may hold values from -0.375 to 0.375
- adapter_key_value: bfloat16 [2, 256, 512], P('depth', 'dp', 'mp'), may hold values from -0.375 to 0.375
- adapter_output_down: bfloat16 [2, 256, 2048], P('depth', 'dp', 'mp'), may hold values from -0.5 to 0.5
- adapter_hidden_down: bfloat16 [2, 256, 16384], P('depth', 'dp', 'mp'), may hold values from -0.046875 to 0.046875
- adapter_model_up: bfloat16 [2, 2, 256, 2048], P('depth', None, 'dp'), may hold values from -0.375 to 0.375
- adapter_gate_up: bfloat16 [2, 2, 256, 16384], P('depth', None, 'dp', 'mp'), may hold values from -0.375 to 0.375
Outputs:
- mixed_rows: bfloat16 [4096, 2048], P(('dp', 'depth'))
- grad_tokens: bfloat16 [4096, 2048], P(('dp', 'depth'))
- grad_w_query: float32 [2048, 2048], P(('dp', 'depth'), 'mp')
- grad_w_keyval: float32 [2048, 512], P(('dp', 'depth'), 'mp')
- grad_w_output: float32 [2048, 2048], P('mp', ('dp', 'depth'))
- grad_w_gateup: float32 [2, 2048, 16384], P(None, ('dp', 'depth'), 'mp')
- grad_w_down: float32 [16384, 2048], P('mp', ('dp', 'depth'))
- grad_gains: float32 [2, 2048], P(None, ('dp', 'depth'))
- grad_lora_in: float32 [2, 5, 2048, 256], P('depth', None, 'dp')
- grad_lora_query: float32 [2, 256, 2048], P('depth', 'dp', 'mp')
- grad_lora_keyval: float32 [2, 256, 512], P('depth', 'dp', 'mp')
- grad_lora_out: float32 [2, 256, 2048], P('depth', 'dp', 'mp')
- grad_lora_hidden: float32 [2, 256, 16384], P('depth', 'dp', 'mp')
- grad_lora_model: float32 [2, 2, 256, 2048], P('depth', None, 'dp')
- grad_lora_gateup: float32 [2, 2, 256, 16384], P('depth', None, 'dp', 'mp')
The draws below stay inside these ranges and needn't reach their ends.
Inputs may be any that keep to these rules, and one draw needn't show every extreme that they name: The 4 entries of a bucket are the lengths of the sequences packed into it, in order; 0 marks an unused slot and every used length is at least 64; they sum to at most 512 and to at least half of it; in every draw some bucket holds a single sequence of 512 rows. `bucket_loop_index`: the 2 buckets of one dp index belong to different loops; in some dp index the bucket of depth 0 is of loop 1, and in another of loop 0.
All inputs are finite; a program needn't handle non-finite values.
Results may differ from the reference program's by a relative error of at most 0.025.
Values may be sent and summed in bfloat16 or wider, within the bound.
No kernel may reach another device: no remote copies, remote signals or barrier semaphores. Data moves between devices by JAX's collectives and lax.ppermute only.
A program may use at most 256 MiB of HBM per device.

```python
from functools import partial
import jax
import jax.numpy as jnp
from jax import lax

MODEL_WIDTH = 2048
QUERY_HEADS = 8
HEAD_SIZE = 256
FEED_HIDDEN = 16384
ADAPTER_RANK = 256
LOOP_COUNT = 2
NSEQ = 4
BUCKET = 512
MINSEQ = 64
GROUPS = 4
TOKENS = 4096


def draw_lengths(key, part):
    key = jax.random.fold_in(key, 11)
    subkeys = jax.random.split(key, 3)
    grid_shape = (GROUPS, LOOP_COUNT, NSEQ)
    first_draw = jax.random.randint(subkeys[0], grid_shape, 0, 4)
    second_draw = jax.random.randint(subkeys[1], grid_shape, 0, 4)
    exponent = jnp.minimum(first_draw, second_draw)
    wanted = MINSEQ * jnp.left_shift(jnp.ones(grid_shape, jnp.int32), exponent)
    room_left = jnp.full((GROUPS, LOOP_COUNT), BUCKET, jnp.int32)
    columns = []
    for slot_id in range(NSEQ):
        taken = jnp.where(room_left >= MINSEQ, jnp.minimum(wanted[..., slot_id], room_left), 0)
        columns.append(taken)
        room_left = room_left - taken
    flat_lens = jnp.stack(columns, axis=-1).reshape(GROUPS * LOOP_COUNT, NSEQ)
    chosen = jax.random.randint(subkeys[2], (), 0, GROUPS * LOOP_COUNT)
    single = (jnp.arange(NSEQ) == 0).astype(jnp.int32) * BUCKET
    marker = (jnp.arange(GROUPS * LOOP_COUNT) == chosen)[:, None]
    flat_lens = jnp.where(marker, single[None, :], flat_lens)
    return flat_lens.reshape(GROUPS, LOOP_COUNT, NSEQ).astype(jnp.int32)


def draw_bucket_loop_index(key, part):
    key = jax.random.fold_in(key, 23)
    subkeys = jax.random.split(key, 3)
    flip_bits = jax.random.randint(subkeys[0], (GROUPS,), 0, 2)
    first_group = jax.random.randint(subkeys[1], (), 0, GROUPS)
    other_group = (first_group + 1 + jax.random.randint(subkeys[2], (), 0, GROUPS - 1)) % GROUPS
    group_ids = jnp.arange(GROUPS)
    flip_bits = jnp.where(group_ids == first_group, 1, jnp.where(group_ids == other_group, 0, flip_bits))
    depth_ids = jnp.arange(LOOP_COUNT)
    return jnp.bitwise_xor(flip_bits[:, None], depth_ids[None, :]).astype(jnp.int32)


def level_of(key, extent, cuts, least, top_value):
    loudness, own = 1.0, jax.random.fold_in(key, 6)
    for axis_at, shards_of in cuts:
        draws = jnp.exp(jax.random.uniform(jax.random.fold_in(own, axis_at), (shards_of,), jnp.float32, least / len(cuts), top_value / len(cuts)))
        loudness = loudness * jnp.repeat(draws, extent[axis_at] // shards_of).reshape([-1 if axis == axis_at else 1 for axis in range(len(extent))])
    return loudness


def scatter_about(key, shape, scale, most, cuts=(), kind=jnp.bfloat16):
    result = scale * jax.random.normal(key, shape, jnp.float32)
    if cuts:
        result = result * level_of(key, shape, cuts, -0.22, 0.18)
    return jnp.clip(result, -most, most).astype(kind)


def setup_inputs(seed: int = 0) -> dict:
    keys = jax.random.split(jax.random.key(seed), 18)
    return {
        "tokens": scatter_about(keys[0], (TOKENS, MODEL_WIDTH), 1.0, 6.0, ((0, 8),)),
        "cotangent": scatter_about(keys[1], (TOKENS, MODEL_WIDTH), 1.0, 6.0, ((0, 8),)),
        "lengths": draw_lengths(jax.random.fold_in(keys[17], 71), 0),
        "bucket_loop_index": draw_bucket_loop_index(jax.random.fold_in(keys[17], 71), 0),
        "query_weight": scatter_about(keys[4], (MODEL_WIDTH, QUERY_HEADS * HEAD_SIZE), MODEL_WIDTH ** -0.5, 0.125, ((0, 8), (1, 4))),
        "key_value_weight": scatter_about(keys[5], (MODEL_WIDTH, 2 * HEAD_SIZE), MODEL_WIDTH ** -0.5, 0.125, ((0, 8), (1, 4))),
        "output_weight": scatter_about(keys[6], (QUERY_HEADS * HEAD_SIZE, MODEL_WIDTH), (QUERY_HEADS * HEAD_SIZE // 16) ** -0.5, 0.5, ((0, 4), (1, 8))),
        "gate_up_weight": scatter_about(keys[7], (2, MODEL_WIDTH, FEED_HIDDEN), MODEL_WIDTH ** -0.5, 0.125, ((1, 8), (2, 4))),
        "down_weight": scatter_about(keys[8], (FEED_HIDDEN, MODEL_WIDTH), FEED_HIDDEN ** -0.5, 0.046875, ((0, 4), (1, 8))),
        "gains": jnp.clip(1.0 + 0.1 * jax.random.normal(keys[9], (2, MODEL_WIDTH), jnp.float32), 0.5, 1.5).astype(jnp.bfloat16),
        "adapter_input_down": scatter_about(keys[10], (LOOP_COUNT, 5, MODEL_WIDTH, ADAPTER_RANK), MODEL_WIDTH ** -0.5, 0.125, ((0, 2), (2, 4))),
        "adapter_query_up": scatter_about(keys[11], (LOOP_COUNT, ADAPTER_RANK, QUERY_HEADS * HEAD_SIZE), ADAPTER_RANK ** -0.5, 0.375, ((0, 2), (1, 4), (2, 4))),
        "adapter_key_value": scatter_about(keys[12], (LOOP_COUNT, ADAPTER_RANK, 2 * HEAD_SIZE), ADAPTER_RANK ** -0.5, 0.375, ((0, 2), (1, 4), (2, 4))),
        "adapter_output_down": scatter_about(keys[13], (LOOP_COUNT, ADAPTER_RANK, QUERY_HEADS * HEAD_SIZE), (QUERY_HEADS * HEAD_SIZE // 16) ** -0.5, 0.5, ((0, 2), (1, 4), (2, 4))),
        "adapter_hidden_down": scatter_about(keys[14], (LOOP_COUNT, ADAPTER_RANK, FEED_HIDDEN), FEED_HIDDEN ** -0.5, 0.046875, ((0, 2), (1, 4), (2, 4))),
        "adapter_model_up": scatter_about(keys[15], (LOOP_COUNT, 2, ADAPTER_RANK, MODEL_WIDTH), ADAPTER_RANK ** -0.5, 0.375, ((0, 2), (2, 4))),
        "adapter_gate_up": scatter_about(keys[16], (LOOP_COUNT, 2, ADAPTER_RANK, FEED_HIDDEN), ADAPTER_RANK ** -0.5, 0.375, ((0, 2), (2, 4), (3, 4))),
    }


EPS = 1e-06
THETA = 10000.0
HIGH = lax.Precision.HIGHEST

@jax.custom_vjp
def rank_rows(v):
    return lax.optimization_barrier(v.astype(jnp.bfloat16)).astype(jnp.float32)

@jax.custom_vjp
def rank_rows_backward(v):
    return v

def low_keep(v):
    return (rank_rows(v), None)

def low_pass(kept, grad):
    return (grad,)

def back_keep(v):
    return (v, None)

def back_low(kept, grad):
    return (rank_rows(grad),)
rank_rows.defvjp(low_keep, low_pass)
rank_rows_backward.defvjp(back_keep, back_low)

def matrix_product(left_op, right_op):
    return jnp.dot(left_op, right_op, precision=HIGH)

def layout(seq_lens, row_count):
    seq_ends = jnp.cumsum(seq_lens).astype(jnp.int32)
    places = jnp.arange(row_count, dtype=jnp.int32)
    passed = (places[:, None] >= seq_ends[None, :]).astype(jnp.int32)
    segment = lax.optimization_barrier(jnp.sum(passed, axis=1)).astype(jnp.int32)
    starts = lax.optimization_barrier(jnp.sum(passed * seq_lens[None, :], axis=1)).astype(jnp.int32)
    valid_rows = (places < seq_ends[-1]).astype(jnp.float32)
    within = (places - starts).astype(jnp.float32)
    return (places, segment, within, valid_rows)

def rotary(within, head_width):
    half_width = head_width // 2
    frequency = THETA ** (-2.0 * jnp.arange(half_width, dtype=jnp.float32) / head_width)
    angles = within[:, None] * frequency[None, :]
    return (jnp.cos(angles), jnp.sin(angles))

def rotate(vector, cosine, sine_part):
    half_width = vector.shape[-1] // 2
    former = vector[..., :half_width]
    latter = vector[..., half_width:]
    return jnp.concatenate([former * cosine - latter * sine_part, latter * cosine + former * sine_part], axis=-1)

def rms_norm(values, gain_row):
    inverse = lax.rsqrt(lax.optimization_barrier(jnp.mean(values * values, axis=-1, keepdims=True)) + EPS)
    return values * inverse * gain_row

def select_loop(adapter_table, current_loop):
    return lax.dynamic_index_in_dim(adapter_table, current_loop, 0, keepdims=False)

def bucket_pass(weight_list, item):
    query_weight, key_value_weight, output_weight, gate_up_weight, down_weight, gains, adapter_input_down, adapter_query_up, adapter_key_value, adapter_output_down, adapter_hidden_down, adapter_model_up, adapter_gate_up = weight_list
    tok_rows, seq_lens, current_loop = item
    adapter_input = select_loop(adapter_input_down, current_loop)
    query_lifted = select_loop(adapter_query_up, current_loop)
    key_value_lifted = select_loop(adapter_key_value, current_loop)
    output_down_adapter = select_loop(adapter_output_down, current_loop)
    hidden_down_adapter = select_loop(adapter_hidden_down, current_loop)
    model_lifted = select_loop(adapter_model_up, current_loop)
    gate_up_lifted = select_loop(adapter_gate_up, current_loop)
    places, segment, within, valid_rows = layout(seq_lens, BUCKET)
    cosine, sine_part = rotary(within, HEAD_SIZE)
    normalized_rows = rank_rows(rms_norm(tok_rows, gains[0]))
    rank_query_key_value = rank_rows(rank_rows_backward(jnp.einsum('bd,kdr->kbr', normalized_rows, adapter_input[:3], precision=HIGH)))
    query_raw = rank_rows_backward(matrix_product(normalized_rows, query_weight) + matrix_product(rank_query_key_value[0], query_lifted))
    query_rows = rank_rows(rotate(query_raw.reshape(BUCKET, QUERY_HEADS, HEAD_SIZE), cosine[:, None, :], sine_part[:, None, :]))
    adapter_joint = jnp.concatenate([matrix_product(rank_query_key_value[1], key_value_lifted[:, :HEAD_SIZE]), matrix_product(rank_query_key_value[2], key_value_lifted[:, HEAD_SIZE:])], axis=1)
    joint_key_value = rank_rows(rank_rows_backward(matrix_product(normalized_rows, key_value_weight) + adapter_joint))
    key_rows = rank_rows(rotate(joint_key_value[:, :HEAD_SIZE], cosine, sine_part))
    value_rows = joint_key_value[:, HEAD_SIZE:]
    allowed = (segment[:, None] == segment[None, :]) & (places[None, :] <= places[:, None])
    scores = rank_rows_backward(jnp.einsum('qhd,kd->hqk', query_rows, key_rows, precision=HIGH) * HEAD_SIZE ** (-0.5))
    scores = jnp.where(allowed[None], scores, -1e+30)
    row_peak = lax.optimization_barrier(jnp.max(scores, axis=-1, keepdims=True))
    powers = jnp.exp(scores - row_peak)
    attn_probs = rank_rows(powers / lax.optimization_barrier(jnp.sum(powers, axis=-1, keepdims=True)))
    attended = jnp.einsum('hqk,kd->qhd', attn_probs, value_rows, precision=HIGH).reshape(BUCKET, QUERY_HEADS * HEAD_SIZE)
    attended = rank_rows(rank_rows_backward(attended))
    rank_out = rank_rows(rank_rows_backward(matrix_product(attended, output_down_adapter.T)))
    branch = rank_rows_backward(matrix_product(attended, output_weight) + matrix_product(rank_out, model_lifted[0]))
    hidden_state = tok_rows + branch
    normed_two = rank_rows(rms_norm(hidden_state, gains[1]))
    rank_gu = rank_rows(rank_rows_backward(jnp.einsum('bd,kdr->kbr', normed_two, adapter_input[3:], precision=HIGH)))
    gate_rows = rank_rows_backward(matrix_product(normed_two, gate_up_weight[0]) + matrix_product(rank_gu[0], gate_up_lifted[0]))
    up_rows = rank_rows_backward(matrix_product(normed_two, gate_up_weight[1]) + matrix_product(rank_gu[1], gate_up_lifted[1]))
    gated_rows = rank_rows(jax.nn.gelu(gate_rows, approximate=True) * up_rows)
    rank_down = rank_rows(rank_rows_backward(matrix_product(gated_rows, hidden_down_adapter.T)))
    branch_two = rank_rows_backward(matrix_product(gated_rows, down_weight) + matrix_product(rank_down, model_lifted[1]))
    return hidden_state + branch_two

def reference(tokens, cotangent, lengths, bucket_loop_index, query_weight, key_value_weight, output_weight, gate_up_weight, down_weight, gains, adapter_input_down, adapter_query_up, adapter_key_value, adapter_output_down, adapter_hidden_down, adapter_model_up, adapter_gate_up):
    buckets = GROUPS * LOOP_COUNT
    weight_list = tuple((adapter_table.astype(jnp.float32) for adapter_table in (query_weight, key_value_weight, output_weight, gate_up_weight, down_weight, gains, adapter_input_down, adapter_query_up, adapter_key_value, adapter_output_down, adapter_hidden_down, adapter_model_up, adapter_gate_up)))
    tok_rows = tokens.astype(jnp.float32).reshape(buckets, BUCKET, MODEL_WIDTH)
    seq_lens = lengths.reshape(buckets, NSEQ).astype(jnp.int32)
    loop_ids = bucket_loop_index.reshape(buckets).astype(jnp.int32)

    def forward(params, inputs):
        bucket_step = jax.checkpoint(partial(bucket_pass, params))
        return lax.map(bucket_step, (inputs, seq_lens, loop_ids))
    outputs, pullback = jax.vjp(forward, weight_list, tok_rows)
    valid_rows = jax.vmap(partial(layout, row_count=BUCKET))(seq_lens)[3]
    grad_out = cotangent.astype(jnp.float32).reshape(buckets, BUCKET, MODEL_WIDTH) * valid_rows[:, :, None]
    weight_grads, grad_rows = pullback(grad_out)
    return (outputs.reshape(TOKENS, MODEL_WIDTH).astype(jnp.bfloat16), grad_rows.reshape(TOKENS, MODEL_WIDTH).astype(jnp.bfloat16), weight_grads[0], weight_grads[1], weight_grads[2], weight_grads[3], weight_grads[4], weight_grads[5], weight_grads[6], weight_grads[7], weight_grads[8], weight_grads[9], weight_grads[10], weight_grads[11], weight_grads[12])
```

```python
import functools

import jax
import jax.numpy as jnp
from jax import lax
from jax.experimental import pallas as pl
from jax.experimental.pallas import tpu as pltpu
from jax.sharding import PartitionSpec as P

HEAD_SIZE = 256


EPS = 1e-06
THETA = 10000.0
NEGATIVE = -1e30


def product(left_op, right_op, left_dim, right_dim):
    return lax.dot_general(
        left_op,
        right_op,
        (((left_dim,), (right_dim,)), ((), ())),
        preferred_element_type=jnp.float32,
    )


def layout(seq_lens, row_count):
    seq_ends = jnp.cumsum(seq_lens)
    places = jnp.arange(row_count, dtype=jnp.int32)
    passed = (places[:, None] >= seq_ends[None, :]).astype(jnp.int32)
    segment = jnp.sum(passed, axis=1)
    starts = jnp.sum(passed * seq_lens[None, :], axis=1)
    valid_rows = (places < seq_ends[-1]).astype(jnp.float32)
    within = (places - starts).astype(jnp.float32)
    return (places, segment, within, valid_rows)


def rotary(within, head_width):
    half_width = head_width // 2
    frequency = THETA ** (-2.0 * jnp.arange(half_width, dtype=jnp.float32) / head_width)
    angles = within[:, None] * frequency[None, :]
    return (jnp.cos(angles), jnp.sin(angles))


def rotate(vector, cosine, sine_part):
    half_width = vector.shape[-1] // 2
    former = vector[..., :half_width]
    latter = vector[..., half_width:]
    return jnp.concatenate(
        [former * cosine - latter * sine_part, latter * cosine + former * sine_part], axis=-1
    )


def rotate_back(vector, cosine, sine_part):
    half_width = vector.shape[-1] // 2
    former = vector[..., :half_width]
    latter = vector[..., half_width:]
    return jnp.concatenate(
        [former * cosine + latter * sine_part, latter * cosine - former * sine_part], axis=-1
    )


def rms_forward(values, gain_row):
    inverse = lax.rsqrt(jnp.mean(values * values, axis=-1, keepdims=True) + EPS)
    return (values * inverse * gain_row, inverse)


def rms_backward(values, inverse, gain_row, grad_norm):
    weighted = grad_norm * gain_row
    grad_values = inverse * weighted - values * inverse**3 * jnp.mean(
        weighted * values, axis=-1, keepdims=True
    )
    grad_gain = jnp.sum(grad_norm * values * inverse, axis=0)
    return (grad_values, grad_gain)


def gelu_tanh(values):
    return jax.nn.gelu(values, approximate=True)


def block_mask(places, segment):
    return (segment[:, None] == segment[None, :]) & (places[None, :] <= places[:, None])


def attend(query_rows, key_rows, value_rows, places, segment, factor):
    row_count = query_rows.shape[0]
    block_rows = min(512, row_count)

    def one_block(block_id):
        allowed = block_mask(places, segment)
        scores = (
            jnp.einsum("qhd,kd->hqk", query_rows, key_rows, preferred_element_type=jnp.float32)
            * factor
        )
        scores = jnp.where(allowed[None], scores, NEGATIVE)
        row_peak = jnp.max(scores, axis=-1, keepdims=True)
        powers = jnp.exp(scores - row_peak)
        row_total = jnp.sum(powers, axis=-1, keepdims=True)
        attn_weights = (powers / row_total).astype(jnp.bfloat16)
        block_out = jnp.einsum(
            "hqk,kd->qhd", attn_weights, value_rows, preferred_element_type=jnp.float32
        )
        return (block_out, (row_peak + jnp.log(row_total))[..., 0])

    outputs, logsum = lax.map(one_block, jnp.arange(row_count // block_rows))
    return (outputs.reshape(query_rows.shape), logsum)


def attend_back(query_rows, key_rows, value_rows, places, segment, factor, logsum, grad_att):
    row_count = query_rows.shape[0]
    block_rows = min(512, row_count)

    def one_block(carry, block_id):
        grad_keys, grad_values = carry
        allowed = block_mask(places, segment)
        scores = (
            jnp.einsum("qhd,kd->hqk", query_rows, key_rows, preferred_element_type=jnp.float32)
            * factor
        )
        scores = jnp.where(allowed[None], scores, NEGATIVE)
        attn_probs = jnp.exp(scores - logsum[block_id][..., None])
        attn_weights = attn_probs.astype(jnp.bfloat16)
        grad_probs = jnp.einsum(
            "qhd,kd->hqk", grad_att, value_rows, preferred_element_type=jnp.float32
        )
        grad_values = grad_values + jnp.einsum(
            "hqk,qhd->kd", attn_weights, grad_att, preferred_element_type=jnp.float32
        )
        centre = jnp.sum(grad_probs * attn_probs, axis=-1, keepdims=True)
        grad_scores = (attn_probs * (grad_probs - centre)).astype(jnp.bfloat16)
        grad_query = (
            jnp.einsum("hqk,kd->qhd", grad_scores, key_rows, preferred_element_type=jnp.float32)
            * factor
        )
        grad_keys = (
            grad_keys
            + jnp.einsum("hqk,qhd->kd", grad_scores, query_rows, preferred_element_type=jnp.float32)
            * factor
        )
        return ((grad_keys, grad_values), grad_query)

    zero_rows = jnp.zeros(key_rows.shape, jnp.float32)
    (grad_keys, grad_values), grad_query = lax.scan(
        one_block, (zero_rows, zero_rows), jnp.arange(row_count // block_rows)
    )
    return (grad_query.reshape(query_rows.shape), grad_keys, grad_values)


CHUNKS = 4
GROUPS = 2
BF16 = jnp.bfloat16
F32 = jnp.float32


def trade(block, axis, mask):
    count = lax.axis_size(axis)
    return lax.ppermute(block, axis, [(i, i ^ mask) for i in range(count)])


def gather_dp(piece, *hold):
    count = lax.axis_size("dp")
    if count == 4:
        half = piece.shape[0] // 2
        from_one = trade(piece, "dp", 1)
        from_two = trade(piece, "dp", 2)
        far = jnp.concatenate(
            [
                trade(after(from_two[:half], *hold), "dp", 1),
                trade(after(from_one[half:], *hold), "dp", 2),
            ],
            axis=0,
        )
        return [piece, from_one, from_two, far]
    pieces, mask = [piece], 1
    while mask < count:
        pieces = pieces + [trade(held, "dp", mask) for held in pieces]
        mask *= 2
    return pieces


def gather_pair(one, two):
    count = lax.axis_size("dp")
    if count == 4:
        first_one, first_two = trade(one, "dp", 1), trade(one, "dp", 2)
        second_one, second_two = trade(two, "dp", 1), trade(two, "dp", 2)
        far = trade(first_two, "dp", 1), trade(second_one, "dp", 2)
        pieces = [(one, two), (first_one, second_one), (first_two, second_two), far]
        return pieces, far
    ones, twos = gather_dp(one), gather_dp(two)
    return list(zip(ones, twos)), (ones[-1], twos[-1])


def gather_near(bundle):
    count = lax.axis_size("dp")
    pieces, mask = [bundle], 1
    while mask < count:
        first = pieces if count != 4 else pieces[:1]
        pieces = pieces + [trade(held, "dp", mask) for held in first]
        mask *= 2
    return pieces


def gather_far(near, hold, height):
    chunks = [[((b, c), (b, CHUNKS + c)) for b in near] for c in range(CHUNKS)]
    if lax.axis_size("dp") == 4:
        size = CHUNKS // GROUPS
        for group in range(GROUPS):
            rows = (size * group * height, size * (group + 1) * height)
            one = lax.slice_in_dim(after(near[2], hold), *rows, axis=0)
            two = lax.slice_in_dim(
                after(near[1], hold), *[CHUNKS * height + r for r in rows], axis=0
            )
            one, two = trade(one, "dp", 1), trade(two, "dp", 2)
            for n in range(size):
                chunks[group * size + n].append(((one, n), (two, n)))
    return chunks


def scatter_dp(parts, *hold):
    count = lax.axis_size("dp")
    if hold:
        parts = [after(part, *hold) for part in parts]
    if count == 4:
        half = parts[3].shape[0] // 2
        near_one = trade(parts[3][:half], "dp", 1)
        near_two = trade(parts[3][half:], "dp", 2)
        for_two = jnp.concatenate([add_rounded(parts[2][:half], near_one), parts[2][half:]], axis=0)
        for_one = jnp.concatenate([parts[1][:half], add_rounded(parts[1][half:], near_two)], axis=0)
        got_one = trade(for_one, "dp", 1)
        got_two = trade(for_two, "dp", 2)
        return parts[0].astype(F32) + got_one.astype(F32) + got_two.astype(F32)
    mask = count // 2
    while mask:
        parts = [
            add_rounded(parts[p], trade(parts[p + mask], "dp", mask)) for p in range(mask)
        ]
        mask //= 2
    return parts[0].astype(F32)


def add_rounded(one, two):
    return (one.astype(F32) + two.astype(F32)).astype(BF16)


def relative(block, axis, index, count):
    width = block.shape[axis] // count
    mask = 1
    while mask < count:
        flipped = jnp.concatenate(
            [
                lax.slice_in_dim(block, (b ^ mask) * width, ((b ^ mask) + 1) * width, axis=axis)
                for b in range(count)
            ],
            axis=axis,
        )
        block = jnp.where((index & mask) > 0, flipped, block)
        mask *= 2
    return block


VMEM_LIMIT = 50 * 1024 * 1024
GELU_SCALE = 0.7978845608028654
BRIEF = pl.CostEstimate(flops=1, bytes_accessed=1, transcendentals=0)


def after(block, *earlier):
    return lax.optimization_barrier((block, *earlier))[0]


def whole_spec(shape):
    return pl.BlockSpec(shape, lambda *_: (0,) * len(shape), pipeline_mode=pl.Buffered(1))


def params():
    return pltpu.CompilerParams(vmem_limit_bytes=VMEM_LIMIT)


def nn(left_op, right_op):
    return product(left_op, right_op, 1, 0)


def nt(left_op, right_op):
    return product(left_op, right_op, 1, 1)


def late_split(height):
    return -(-height // 48) * 16


def pack_kernel(part, rank_part, rank, mp, *refs):
    query, key_value, output, gains, query_up, key_value_up, output_down = refs[:7]
    inputs, input_share, model_share, attn, one, late = refs[7:]
    heads = query.shape[1]
    one[...] = jnp.zeros_like(one)
    one[:part, :heads] = query[...]
    one[:part, heads:] = key_value[...]
    one[part : 2 * part, :heads] = output[...].T
    one[2 * part : 2 * part + 2, :part] = gains[...]
    first = 2 * part + 16
    one[first : first + rank_part, :heads] = query_up[0]
    one[first : first + rank_part, heads:] = key_value_up[0]
    one[first + rank_part :, :heads] = output_down[0]
    wide = inputs.shape[2]
    attn[wide:, :] = jnp.zeros_like(attn[wide:, :])
    for k in range(3):
        attn[:wide, k * rank : (k + 1) * rank] = inputs[0, k]
    row = 0
    for at in range(0, model_share.shape[3], rank):
        for k in range(2):
            late[row : row + rank_part, :] = model_share[0, k, :, at : at + rank]
            row += rank_part
    height = input_share.shape[2]
    for k in range(2):
        late[row : row + height, :] = input_share[0, 3 + k]
        row += height
    split = late_split(row)
    for k in range(3):
        rows = min(split, row - k * split)
        attn[wide : wide + rows, k * rank : (k + 1) * rank] = late[
            k * split : k * split + rows, :
        ]


def pack_pass(mp, arrays, mp_count, rank):
    query, key_value, output, gains, query_up, _, _, inputs, model_up = arrays
    part, rank_part = query.shape[0], query_up.shape[1]
    slice_width, columns = inputs.shape[2], model_up.shape[3] // mp_count
    rows = slice_width // mp_count
    late_rows = 2 * rank_part * (columns // rank) + 2 * rows
    shapes = [
        (slice_width + late_split(late_rows), 3 * rank),
        (2 * part + 16 + 2 * rank_part, query.shape[1] + key_value.shape[1]),
    ]

    def whole(shape):
        return pl.BlockSpec(shape, lambda s, mp: (0,) * len(shape))

    return pl.pallas_call(
        functools.partial(pack_kernel, part, rank_part, rank),
        grid_spec=pltpu.PrefetchScalarGridSpec(
            num_scalar_prefetch=1,
            grid=(1,),
            in_specs=[whole(a.shape) for a in arrays[:8]]
            + [
                pl.BlockSpec((1, 5, rows, rank), lambda s, mp: (0, 0, mp[0], 0)),
                pl.BlockSpec((1, 2, rank_part, columns), lambda s, mp: (0, 0, 0, mp[0])),
            ],
            out_specs=[whole(s) for s in shapes],
            scratch_shapes=[pltpu.VMEM((late_rows, rank), BF16)],
        ),
        out_shape=[jax.ShapeDtypeStruct(s, BF16) for s in shapes],
        compiler_params=params(),
        cost_estimate=BRIEF,
        name="pack_pass",
    )(mp, *arrays[:7], inputs, inputs, model_up)


def unpack_kernel(count, part, rank_part, *refs):
    pieces, (shared, inputs, late, lifted, out_down) = refs[: 2 * count], refs[2 * count :]
    rows = shared.shape[0] // count
    wide, rank = 2 * part, late.shape[2]
    heads = out_down.shape[1]
    height = late.shape[1]
    split = late_split(height)
    for p in range(count):
        attn, one = pieces[2 * p : 2 * p + 2]
        shared[p * rows : (p + 1) * rows, :] = one[:rows, :]
        here = slice(p * rank_part, (p + 1) * rank_part)
        lifted[here, :] = one[rows : rows + rank_part, :]
        out_down[here, :] = one[rows + rank_part :, :heads]
        inputs[p * wide : (p + 1) * wide, :] = attn[:wide, :]
        for k in range(3):
            number = min(split, height - k * split)
            late[p, k * split : k * split + number, :] = attn[
                wide : wide + number, k * rank : (k + 1) * rank
            ]


def unpack_pass(pieces, part, rank_part, rank, rows, columns, heads):
    count = len(pieces)
    joint = pieces[0][1].shape[1]
    late_rows = 2 * rank_part * (columns // rank) + 2 * rows
    flat = [b for pair in pieces for b in pair]
    shapes = [
        (count * (2 * part + 16), joint),
        (count * 2 * part, 3 * rank),
        (count, late_rows, rank),
        (count * rank_part, joint),
        (count * rank_part, heads),
    ]
    return pl.pallas_call(
        functools.partial(unpack_kernel, count, part, rank_part),
        grid=(1,),
        in_specs=[whole_spec(b.shape) for b in flat],
        out_specs=[whole_spec(s) for s in shapes],
        out_shape=[jax.ShapeDtypeStruct(s, BF16) for s in shapes],
        compiler_params=params(),
        cost_estimate=BRIEF,
        name="unpack_pass",
    )(*flat)


def shared_kernel(count, part, core, own, other, joint, output, gains):
    rows = own.shape[0] // count
    heads = output.shape[1]
    gains[...] = jnp.zeros_like(gains)
    for e in range(2):

        @pl.when(core[0] == e)
        def _(e=e):
            for side, source in ((e, own), (1 - e, other)):
                for p in range(count):
                    here = slice((2 * p + side) * part, (2 * p + side + 1) * part)
                    first = p * rows
                    joint[here, :] = source[first : first + part, :]
                    output[here, :] = source[first + part : first + 2 * part, :heads]
                    gains[:2, here] = source[first + 2 * part : first + 2 * part + 2, :part]


def shared_pass(core, own, other, count, part, heads):
    shapes = [(count * 2 * part, own.shape[1]), (count * 2 * part, heads), (16, count * 2 * part)]
    return pl.pallas_call(
        functools.partial(shared_kernel, count, part),
        grid=(1,),
        in_specs=[pl.BlockSpec(memory_space=pltpu.SMEM)] + [whole_spec(own.shape)] * 2,
        out_specs=[whole_spec(s) for s in shapes],
        out_shape=[jax.ShapeDtypeStruct(s, BF16) for s in shapes],
        compiler_params=params(),
        cost_estimate=BRIEF,
        name="shared_pass",
    )(core, own, other)


def late_kernel(rank_part, rows, count, late, model, inputs):
    rank = late.shape[3]
    for p in range(count):
        for n in range(model.shape[2] // rank):
            for k in range(2):
                first = (2 * n + k) * rank_part
                model[k, p * rank_part : (p + 1) * rank_part, n * rank : (n + 1) * rank] = late[
                    0, p, first : first + rank_part, :
                ]
        first = 2 * rank_part * (model.shape[2] // rank)
        for k in range(2):
            inputs[p, 0, :, k * rank : (k + 1) * rank] = late[
                0, p, first + k * rows : first + (k + 1) * rows, :
            ]


def late_pass(late, rows, columns, rank_part):
    mp_count, count, height, rank = late.shape
    model, inputs = pl.pallas_call(
        functools.partial(late_kernel, rank_part, rows, count),
        grid=(mp_count,),
        in_specs=[pl.BlockSpec((1, count, height, rank), lambda z: (z, 0, 0, 0))],
        out_specs=[
            pl.BlockSpec((2, rank, columns), lambda z: (0, 0, z)),
            pl.BlockSpec((count, 1, rows, 2 * rank), lambda z: (0, z, 0, 0)),
        ],
        out_shape=[
            jax.ShapeDtypeStruct((2, rank, mp_count * columns), BF16),
            jax.ShapeDtypeStruct((count, mp_count, rows, 2 * rank), BF16),
        ],
        compiler_params=params(),
        cost_estimate=BRIEF,
        name="late_pass",
    )(late)
    return model, inputs.reshape(count * mp_count * rows, 2 * rank)


def ffn_blocks(arrays, chunk, side):
    gate_up, down, lora_gate_up, lora_hidden = arrays

    def column(s, core):
        return side(core[0]) * CHUNKS + s

    return [
        pl.BlockSpec((2, gate_up.shape[1], chunk), lambda s, core: (0, 0, column(s, core))),
        pl.BlockSpec((chunk, down.shape[1]), lambda s, core: (column(s, core), 0)),
        pl.BlockSpec(
            (1, 2, lora_gate_up.shape[2], chunk), lambda s, core: (0, 0, 0, column(s, core))
        ),
        pl.BlockSpec((1, lora_hidden.shape[1], chunk), lambda s, core: (0, 0, column(s, core))),
    ]


def ffn_rows(gate_up, down, lora_gate_up, lora_hidden):
    return [
        gate_up[0],
        gate_up[1],
        down[...].T,
        jnp.concatenate([lora_gate_up[0, 0], lora_gate_up[0, 1], lora_hidden[0]], axis=0),
    ]


def give_kernel(core, gate_up, down, lora_gate_up, lora_hidden, given):
    first = 0
    for block in ffn_rows(gate_up, down, lora_gate_up, lora_hidden):
        given[first : first + block.shape[0], :] = block
        first += block.shape[0]


def give_pass(core, arrays, chunk):
    part, rank_part = arrays[0].shape[1], arrays[3].shape[1]
    height = 3 * (part + rank_part)
    return pl.pallas_call(
        give_kernel,
        grid_spec=pltpu.PrefetchScalarGridSpec(
            num_scalar_prefetch=1,
            grid=(CHUNKS,),
            in_specs=ffn_blocks(arrays, chunk, lambda me: 1 - me),
            out_specs=pl.BlockSpec((height, chunk), lambda s, core: (s, 0)),
        ),
        out_shape=jax.ShapeDtypeStruct((CHUNKS * height, chunk), BF16),
        compiler_params=params(),
        cost_estimate=BRIEF,
        name="give_pass",
    )(core, *arrays)


def bundle_kernel(part, core, gate_up, down, lora_gate_up, lora_hidden, taken, bundle):
    own_first = core[0] == 0
    one, two = bundle.at[0], bundle.at[1]
    gate, upper, lower, lifted = ffn_rows(gate_up, down, lora_gate_up, lora_hidden)

    def pair(own, start):
        other = taken[start : start + part, :]
        return jnp.where(own_first, own, other), jnp.where(own_first, other, own)

    one[:part, :], one[part : 2 * part, :] = pair(gate, 0)
    two[:part, :], two[part : 2 * part, :] = pair(upper, part)
    one[2 * part : 3 * part, :], two[2 * part : 3 * part, :] = pair(lower, 2 * part)
    one[3 * part :, :] = lifted
    two[3 * part :, :] = taken[3 * part :, :]


def bundle_pass(core, arrays, taken, chunk):
    part = arrays[0].shape[1]
    height = taken.shape[0] // CHUNKS
    out = pl.pallas_call(
        functools.partial(bundle_kernel, part),
        grid_spec=pltpu.PrefetchScalarGridSpec(
            num_scalar_prefetch=1,
            grid=(CHUNKS,),
            in_specs=ffn_blocks(arrays, chunk, lambda me: me)
            + [pl.BlockSpec((height, chunk), lambda s, core: (s, 0))],
            out_specs=pl.BlockSpec((2, height, chunk), lambda s, core: (0, s, 0)),
        ),
        out_shape=jax.ShapeDtypeStruct((2, CHUNKS * height, chunk), BF16),
        compiler_params=params(),
        cost_estimate=BRIEF,
        name="bundle_pass",
    )(core, *arrays, taken)
    return out.reshape(2 * CHUNKS * height, chunk)


def gate_kernel(count, width, rank_part, has_base, *refs):
    blocks, refs = refs[:4], refs[4:]
    pieces = [(refs[2 * p], refs[2 * p + 1]) for p in range(count)]
    refs = refs[2 * count :]
    bases, refs = (refs[:2], refs[2:]) if has_base else ((), refs)
    gated_ref, gate_ref, upper_ref, *outs = refs[:5]
    adapters = refs[5]
    rows = blocks[0].shape[0]
    part = width // 2
    rank = count * rank_part
    model_width = count * width
    for b in range(2):
        for k in range(3):
            first = 3 * part + k * rank_part
            for p in range(count):
                adapters[3 * b + k, p * rank_part : (p + 1) * rank_part, :] = pieces[p][b][
                    first : first + rank_part, :
                ]
    for b in range(2):
        normed, grad = blocks[b], blocks[2 + b]
        span = slice(b * rows, (b + 1) * rows)
        gate = nn(normed[:, model_width : model_width + rank], adapters[3 * b])
        upper = nn(normed[:, model_width + rank :], adapters[3 * b + 1])
        grad_gated = nn(grad[:, model_width:], adapters[3 * b + 2])
        for p in range(count):
            columns = slice(p * width, (p + 1) * width)
            gate += nn(normed[:, columns], pieces[p][0][:width, :])
            upper += nn(normed[:, columns], pieces[p][1][:width, :])
            for e in range(2):
                columns = slice(p * width + e * part, p * width + (e + 1) * part)
                grad_gated += nn(grad[:, columns], pieces[p][e][width : width + part, :])
        square = gate * gate
        bent = jnp.tanh(GELU_SCALE * gate * (1.0 + 0.044715 * square))
        half = 0.5 * (1.0 + bent)
        active = gate * half
        slope = half + 0.5 * gate * (1.0 - bent * bent) * GELU_SCALE * (
            1.0 + 3.0 * 0.044715 * square
        )
        gated_ref[span, :] = (active * upper).astype(BF16)
        gate_ref[span, :] = (grad_gated * upper * slope).astype(BF16)
        upper_ref[span, :] = (grad_gated * active).astype(BF16)

    def put(b, first, value):
        columns = slice(first, first + value.shape[1])
        if bases:
            value = value + bases[b][:, columns].astype(F32)
        outs[b][:, columns] = value.astype(outs[b].dtype)

    for p in range(count):
        value = nt(gate_ref[...], pieces[p][0][:width, :]) + nt(
            upper_ref[...], pieces[p][1][:width, :]
        )
        for b in range(2):
            put(b, p * width, value[b * rows : (b + 1) * rows])
    for b in range(2):
        span = slice(b * rows, (b + 1) * rows)
        put(b, model_width, nt(gate_ref[span, :], adapters[3 * b]))
        put(b, model_width + rank, nt(upper_ref[span, :], adapters[3 * b + 1]))


def gate_pass(normed_pair, grad_pair, pieces, width, rank_part, bases, last):
    blocks = (*normed_pair, *grad_pair)
    rows, columns = blocks[0].shape
    both_rows = 2 * rows
    pairs = [block for pair in pieces for block in pair]
    height = 3 * (width // 2 + rank_part)
    chunk = pairs[0][0].shape[1]
    return pl.pallas_call(
        functools.partial(gate_kernel, len(pieces), width, rank_part, bool(bases)),
        grid=(1,),
        in_specs=[whole_spec(a.shape) for a in blocks]
        + [
            pl.BlockSpec(
                (height, chunk),
                functools.partial(lambda at, t: (at, 0), at),
                pipeline_mode=pl.Buffered(1),
            )
            for _, at in pairs
        ]
        + [whole_spec(a.shape) for a in bases],
        out_specs=[whole_spec((both_rows, chunk))] * 3 + [whole_spec((rows, columns))] * 2,
        out_shape=[jax.ShapeDtypeStruct((both_rows, chunk), BF16)] * 3
        + [
            jax.ShapeDtypeStruct((rows, columns), F32 if last else BF16),
            jax.ShapeDtypeStruct((rows, columns), BF16),
        ],
        scratch_shapes=[pltpu.VMEM((6, len(pieces) * rank_part, chunk), BF16)],
        compiler_params=params(),
        cost_estimate=BRIEF,
        name="gate_pass",
    )(*blocks, *[block for block, _ in pairs], *bases)


def down_kernel(count, rows, width, rank_part, chunks, *refs):
    acts, refs = refs[:chunks], refs[chunks:]
    outs, adapters = refs[-3:-1], refs[-1]
    part = width // 2
    pieces = [
        [refs[2 * (q * count + p) : 2 * (q * count + p) + 2] for p in range(count)]
        for q in range(chunks)
    ]
    for b in range(2):
        span = slice(b * rows, (b + 1) * rows)
        for p in range(count):
            for e in range(2):
                value = nt(acts[0][span, :], pieces[0][p][e][width : width + part, :])
                for q in range(1, chunks):
                    value += nt(acts[q][span, :], pieces[q][p][e][width : width + part, :])
                first = p * width + e * part
                outs[b][:, first : first + part] = value.astype(outs[b].dtype)
        value = 0.0
        first = 3 * part + 2 * rank_part
        for q in range(chunks):
            for p in range(count):
                adapters[p * rank_part : (p + 1) * rank_part, :] = pieces[q][p][b][
                    first : first + rank_part, :
                ]
            value += nt(acts[q][span, :], adapters[...])
        outs[b][:, count * width :] = value.astype(outs[b].dtype)


def down_pass(acts, chunks, width, rank_part):
    count = len(chunks[0])
    both_rows, chunk = acts[0].shape
    rows = both_rows // 2
    columns = count * (width + rank_part)
    height = 3 * (width // 2 + rank_part)
    pairs = [block for pieces in chunks for pair in pieces for block in pair]
    shapes = [
        jax.ShapeDtypeStruct((rows, columns), F32),
        jax.ShapeDtypeStruct((rows, columns), BF16),
    ]
    return pl.pallas_call(
        functools.partial(down_kernel, count, rows, width, rank_part, len(chunks)),
        grid=(1,),
        in_specs=[whole_spec(a.shape) for a in acts]
        + [
            pl.BlockSpec(
                (height, chunk),
                functools.partial(lambda at, t: (at, 0), at),
                pipeline_mode=pl.Buffered(1),
            )
            for _, at in pairs
        ],
        out_specs=[whole_spec(s.shape) for s in shapes],
        out_shape=shapes,
        scratch_shapes=[pltpu.VMEM((count * rank_part, chunk), BF16)],
        compiler_params=params(),
        cost_estimate=BRIEF,
        name="down_pass",
    )(*acts, *[block for block, _ in pairs])


def sum_kernel(own, other, total):
    total[...] = (own[...].astype(F32) + other[...].astype(F32)).astype(BF16)


def sum_pass(own, other):
    rows, columns = own.shape
    tile = pl.BlockSpec((rows // 4, columns), lambda t: (t, 0))
    return pl.pallas_call(
        sum_kernel,
        grid=(4,),
        in_specs=[tile, tile],
        out_specs=tile,
        out_shape=jax.ShapeDtypeStruct((rows, columns), BF16),
        compiler_params=params(),
        cost_estimate=BRIEF,
        name="sum_pass",
    )(own, other)


def turn_kernel(own, other, turned):
    rows = own.shape[0]
    turned[:, :rows] = own[...].T
    turned[:, rows:] = other[...].T


def turn_pass(own, other):
    rows, columns = own.shape
    tile = 256
    source = pl.BlockSpec((rows, tile), lambda t: (0, t))
    return pl.pallas_call(
        turn_kernel,
        grid=(columns // tile,),
        in_specs=[source, source],
        out_specs=pl.BlockSpec((tile, 2 * rows), lambda t: (t, 0)),
        out_shape=jax.ShapeDtypeStruct((columns, 2 * rows), own.dtype),
        compiler_params=params(),
        cost_estimate=BRIEF,
        name="turn_pass",
    )(own, other)


def weight_kernel(part, rank_part, sides, adds, aliased, core, *refs):
    gate, upper, gated = refs[:3]
    refs = refs[3:]
    rows = gate.shape[0] // 2
    outs = refs[-len(sides) :]
    for side, number, out in zip(sides, adds, outs):
        normed, grad, *ranks = refs[:5]
        added = refs[5 : 5 + number]
        refs = refs[5 + number :]

        def store(start, value):
            here = slice(start, start + value.shape[0])
            for other in added:
                value = value + other[here, :].astype(F32)
            out[here, :] = value.astype(out.dtype)

        for n, (columns, act) in enumerate(((normed, gate), (normed, upper), (grad, gated))):
            store(n * part, nn(columns[...], act[...]))
        span = slice(side * rows, (side + 1) * rows)
        for n, act in enumerate((gate, upper, gated)):
            store(3 * part + n * rank_part, nn(ranks[n][:, span], act[span, :]))


def weight_pass(core, normed_t, grad_t, width, rank_part, acts, at, count, items, held=()):
    both_rows = normed_t.shape[1]
    chunk = acts[0].shape[1]
    part = width // 2
    height = 3 * (part + rank_part)
    tile = min(256, chunk)
    model_blocks = (2 * grad_t.shape[0] - normed_t.shape[0]) // rank_part
    rank_blocks = (normed_t.shape[0] - grad_t.shape[0]) // rank_part

    def rows_of(index, side):
        return pl.BlockSpec(
            (part, both_rows),
            lambda t, core: (2 * index + (core[0] ^ side), 0),
            pipeline_mode=pl.Buffered(1),
        )

    def ranks_of(block):
        return pl.BlockSpec(
            (rank_part, both_rows), lambda t, core: (block, 0), pipeline_mode=pl.Buffered(1)
        )

    tiled = pl.BlockSpec((height, tile), lambda t, core: (at, t))
    inputs = list(acts)
    specs = [pl.BlockSpec((both_rows, tile), lambda t, core: (0, t)) for _ in acts]
    for index, side, added, _ in items:
        inputs += [normed_t, grad_t, normed_t, normed_t, grad_t, *[block for block, _ in added]]
        specs += [rows_of(index, side)] * 2
        specs += [ranks_of(model_blocks + n * rank_blocks + index) for n in (0, 1, 0)]
        specs += [
            pl.BlockSpec((height, tile), functools.partial(lambda n, t, core: (n, t), n))
            for _, n in added
        ]
    aliases = {1 + len(inputs) + n: n for n in range(len(held))}
    return pl.pallas_call(
        functools.partial(
            weight_kernel,
            part,
            rank_part,
            tuple(item[1] for item in items),
            tuple(len(item[2]) for item in items),
            len(held),
        ),
        grid_spec=pltpu.PrefetchScalarGridSpec(
            num_scalar_prefetch=1,
            grid=(chunk // tile,),
            in_specs=specs + [pl.BlockSpec(memory_space=pl.ANY) for _ in held],
            out_specs=[tiled] * len(items),
        ),
        out_shape=[jax.ShapeDtypeStruct((count * height, chunk), item[3]) for item in items],
        input_output_aliases=aliases,
        compiler_params=params(),
        cost_estimate=BRIEF,
        name="weight_pass",
    )(core, *inputs, *held)


def finish_kernel(part, rank_part, groups, core, *refs):
    gate_up, down, lora_gate_up, lora_hidden = refs[-4:]
    for n, source in enumerate(refs[:-4]):
        here = pl.program_id(0) == n // groups
        if groups > 1:
            here &= pl.program_id(1) // (CHUNKS // groups) == n % groups

        @pl.when(here)
        def _(source=source):
            def rows(start, height):
                return source[start : start + height, :].astype(F32)

            gate_up[0] = rows(0, part)
            gate_up[1] = rows(part, part)
            down[...] = rows(2 * part, part).T
            lora_gate_up[0, 0] = rows(3 * part, rank_part)
            lora_gate_up[0, 1] = rows(3 * part + rank_part, rank_part)
            lora_hidden[0] = rows(3 * part + 2 * rank_part, rank_part)


def finish_pass(core, mine, other, part, rank_part, hidden):
    chunk = mine[0].shape[1]
    groups = len(mine)
    size = CHUNKS // groups
    height = mine[0].shape[0] // size

    def source(side, group):
        def index(s, q, core):
            inside = jnp.clip(q - group * size, 0, size - 1)
            return (jnp.where(s == side, inside, (size - 1) * (1 - side)), 0)

        return pl.BlockSpec((height, chunk), index)

    def column(s, q, core):
        return (core[0] ^ s) * CHUNKS + q

    shapes = [
        jax.ShapeDtypeStruct(s, F32)
        for s in (
            (2, part, hidden),
            (hidden, part),
            (1, 2, rank_part, hidden),
            (1, rank_part, hidden),
        )
    ]
    grid_spec = pltpu.PrefetchScalarGridSpec(
        num_scalar_prefetch=1,
        grid=(2, CHUNKS),
        in_specs=[source(side, group) for side in range(2) for group in range(groups)],
        out_specs=[
            pl.BlockSpec((2, part, chunk), lambda s, q, core: (0, 0, column(s, q, core))),
            pl.BlockSpec((chunk, part), lambda s, q, core: (column(s, q, core), 0)),
            pl.BlockSpec(
                (1, 2, rank_part, chunk), lambda s, q, core: (0, 0, 0, column(s, q, core))
            ),
            pl.BlockSpec((1, rank_part, chunk), lambda s, q, core: (0, 0, column(s, q, core))),
        ],
    )
    return pl.pallas_call(
        functools.partial(finish_kernel, part, rank_part, groups),
        grid_spec=grid_spec,
        out_shape=shapes,
        compiler_params=params(),
        cost_estimate=BRIEF,
        name="finish_pass",
    )(core, *mine, *other)


def dot(left_op, right_op):
    return jnp.dot(left_op, right_op, preferred_element_type=F32)


def pad_rows(block, rows, width):
    return jnp.pad(block, ((0, rows - block.shape[0]), (0, width - block.shape[1])))


def local(
    tokens,
    cotangent,
    lengths,
    bucket_loop_index,
    query_weight,
    key_value_weight,
    output_weight,
    gate_up_weight,
    down_weight,
    gains,
    adapter_input_down,
    adapter_query_up,
    adapter_key_value,
    adapter_output_down,
    adapter_hidden_down,
    adapter_model_up,
    adapter_gate_up,
):
    dp_count = lax.axis_size("dp")
    dp_id = lax.axis_index("dp")
    depth_id = lax.axis_index("depth")
    mp_index = lax.axis_index("mp")
    first_core = depth_id == 0
    row_count, model_width = tokens.shape
    slice_width = model_width // dp_count
    part_width = slice_width // 2
    heads_width = query_weight.shape[1]
    heads_here = heads_width // HEAD_SIZE
    kv_width = key_value_weight.shape[1]
    joint_width = heads_width + kv_width
    rank_part = adapter_query_up.shape[1]
    rank = rank_part * dp_count
    hidden = down_weight.shape[0]
    half_hidden = hidden // 2
    chunk = half_hidden // CHUNKS

    def partner(block):
        return trade(block, "depth", 1)

    def in_core_order(own, other):
        return jnp.where(first_core, own, other), jnp.where(first_core, other, own)

    keep_own = bucket_loop_index[0, depth_id] == depth_id
    tok_swap, grad_swap = partner(tokens), partner(cotangent)
    slot_id = jnp.where(keep_own, depth_id, 1 - depth_id)
    seq_lens = lengths[0, slot_id]
    places, segment, within, valid_rows = layout(seq_lens, row_count)
    cosine, sine_part = rotary(within, HEAD_SIZE)
    head_cos = cosine[:, None, :]
    head_sin = sine_part[:, None, :]
    factor = HEAD_SIZE ** (-0.5)
    tok_rows = relative(jnp.where(keep_own, tokens, tok_swap), 1, dp_id, dp_count)
    source = tok_rows.astype(F32)
    grad_rows = relative(jnp.where(keep_own, cotangent, grad_swap), 1, dp_id, dp_count)
    grad_out = grad_rows.astype(F32) * valid_rows[:, None]
    grad_ffn = grad_out.astype(BF16)

    mp_count = lax.axis_size("mp")
    share_rows = slice_width // mp_count
    share_columns = model_width // mp_count
    core = depth_id[None].astype(jnp.int32)
    ffn_arrays = (gate_up_weight, down_weight, adapter_gate_up, adapter_hidden_down)
    taken = partner(give_pass(core, ffn_arrays, chunk))
    bundles = pack_pass(
        mp_index[None].astype(jnp.int32),
        (query_weight, key_value_weight, output_weight, gains)
        + (adapter_query_up, adapter_key_value, adapter_output_down)
        + (adapter_input_down, adapter_model_up),
        mp_count,
        rank,
    )
    bundle = bundle_pass(core, ffn_arrays, taken, chunk)
    pieces, hold = gather_pair(*bundles)
    shared_own, input_attn, late, joint_lifted, out_down = unpack_pass(
        pieces, part_width, rank_part, rank, share_rows, share_columns, heads_width
    )
    joint_weight, out_weight, gains_all = shared_pass(
        core, shared_own, partner(shared_own), dp_count, part_width, heads_width
    )
    gains_all = gains_all[:2].astype(F32)
    gain_one, gain_two = gains_all[0], gains_all[1]
    model_all, input_ffn = late_pass(
        lax.all_gather(late, "mp", axis=0, tiled=False),
        share_rows,
        share_columns,
        rank_part,
    )
    model_all = relative(model_all, 2, dp_id, dp_count)
    model_lifted = [model_all[0], model_all[1]]

    near = gather_near(after(bundle, *hold))
    height = 3 * (part_width + rank_part)

    norm_one, inverse_one = rms_forward(source, gain_one)
    normalized_rows = norm_one.astype(BF16)
    ranks = jnp.arange(rank, dtype=jnp.int32)
    rank_swap = ((ranks[:, None] ^ (dp_id * rank_part)) == ranks[None, :]).astype(BF16)

    def swap_ranks(block):
        return dot(block, rank_swap).astype(BF16)

    rank_rows = dot(normalized_rows, input_attn).astype(BF16)
    rank_query, rank_key, rank_value = [
        swap_ranks(rank_rows[:, k * rank : (k + 1) * rank]) for k in range(3)
    ]
    is_key = mp_index * kv_width < HEAD_SIZE
    rank_pick = jnp.where(is_key, rank_key, rank_value)
    joint_raw = dot(normalized_rows, joint_weight)
    query_lifted = joint_lifted[:, :heads_width]
    key_value_lifted = joint_lifted[:, heads_width:]
    joint_part = (joint_raw[:, heads_width:] + dot(rank_pick, key_value_lifted)).astype(BF16)
    joint_key_value = lax.all_gather(joint_part, "mp", axis=1, tiled=True)
    query_raw = joint_raw[:, :heads_width] + dot(rank_query, query_lifted)
    query_rows = rotate(
        query_raw.reshape(row_count, heads_here, HEAD_SIZE), head_cos, head_sin
    ).astype(BF16)
    key_rows = rotate(joint_key_value[:, :HEAD_SIZE].astype(F32), cosine, sine_part).astype(BF16)
    value_rows = joint_key_value[:, HEAD_SIZE:]
    attended, logsum = attend(query_rows, key_rows, value_rows, places, segment, factor)
    flat_heads = attended.reshape(row_count, heads_width).astype(BF16)
    chunks = gather_far(near, flat_heads, height)
    branch_part = product(flat_heads, out_weight, 1, 1)
    rank_out_part = product(flat_heads, out_down, 1, 1)
    branch_sum, rank_out = lax.psum(
        (branch_part.astype(BF16), rank_out_part.astype(BF16)), "mp"
    )
    hidden_state = source + branch_sum.astype(F32) + dot(rank_out, model_lifted[0])

    norm_two, inverse_two = rms_forward(hidden_state, gain_two)
    normed_two = norm_two.astype(BF16)
    rank_gu_abs = dot(normed_two, input_ffn).astype(BF16)
    rank_gate = swap_ranks(rank_gu_abs[:, :rank])
    rank_up = swap_ranks(rank_gu_abs[:, rank:])
    grad_rank_down = product(grad_ffn, model_lifted[1], 1, 1).astype(BF16)

    normed_own = jnp.concatenate([normed_two, rank_gate, rank_up], axis=1)
    grad_own = jnp.concatenate([grad_ffn, grad_rank_down], axis=1)
    grad_pair = (grad_own, partner(grad_own))
    grad_t = turn_pass(*grad_pair)
    normed_pair = (after(normed_own, grad_t), partner(normed_own))

    acts, sums = [], ()
    for c in range(CHUNKS):
        *act, own_sum, other_sum = gate_pass(
            normed_pair, grad_pair, chunks[c], slice_width, rank_part, sums, c == CHUNKS - 1
        )
        acts.append(act)
        sums = (own_sum, other_sum)
    normed_t = turn_pass(after(normed_own, sums[1]), normed_pair[1])
    grad_norm_ready = sum_pass(sums[0], partner(sums[1]))
    grad_norm_sum = lax.psum(grad_norm_ready, "mp")

    groups = [range(0, CHUNKS // 2), range(CHUNKS // 2, CHUNKS)]

    def weight_share(items, group, hold):
        held = ()
        for n, c in enumerate(group):
            gated, grad_gate, grad_upper = acts[c]
            if hold is not None:
                grad_gate = after(grad_gate, hold)
            held = weight_pass(
                core,
                normed_t,
                grad_t,
                slice_width,
                rank_part,
                (grad_gate, grad_upper, gated),
                n,
                len(group),
                items(n) if callable(items) else items,
                held,
            )
        return held

    far, last_sent = (), []
    if dp_count == 4:
        far = weight_share([(3, 0, (), BF16), (3, 1, (), BF16)], range(CHUNKS), grad_norm_ready)
        near_one, near_two = trade(far[0], "dp", 1), trade(far[1], "dp", 2)
        blocks = weight_share([(1, 0, (), BF16), (2, 1, (), BF16)], range(CHUNKS), grad_norm_ready)
        first_sent = (trade(blocks[0], "dp", 1), trade(blocks[1], "dp", 2))
        for group in groups:
            blocks = weight_share(
                lambda n, at=group.start: [
                    (1, 1, ((near_two, at + n),), BF16),
                    (2, 0, ((near_one, at + n),), BF16),
                ],
                group,
                grad_norm_ready,
            )
            last_sent.append((trade(blocks[0], "dp", 1), trade(blocks[1], "dp", 2)))

    grad_norm_two = grad_norm_sum[:, :model_width]
    grad_gate_rank = grad_norm_sum[:, model_width : model_width + rank]
    grad_up_rank = grad_norm_sum[:, model_width + rank :]

    acts_down = [after(a[0], *far) for a in acts]
    ffn_own, ffn_given = down_pass(acts_down, chunks, slice_width, rank_part)
    ffn_all = after(sum_pass(ffn_own, partner(ffn_given)), grad_norm_sum)
    half_rows = row_count // 2
    ffn_first, rank_down = lax.psum(
        (ffn_all[:half_rows, :model_width], ffn_all[:, model_width:]), "mp"
    )

    grad_rank_gu = jnp.concatenate([swap_ranks(grad_gate_rank), swap_ranks(grad_up_rank)], axis=1)
    grad_input_ffn = product(normed_two, grad_rank_gu, 0, 0).astype(BF16)
    grad_norm_two = grad_norm_two.astype(F32) + product(grad_rank_gu, input_ffn, 1, 1)
    grad_hidden, grad_gain_two = rms_backward(hidden_state, inverse_two, gain_two, grad_norm_two)
    grad_hidden = grad_hidden + grad_out
    grad_branch = grad_hidden.astype(BF16)

    grad_rank_out = product(grad_branch, model_lifted[0], 1, 1).astype(BF16)
    grad_flat = dot(grad_branch, out_weight) + dot(grad_rank_out, out_down)
    grad_out_down = product(grad_rank_out, flat_heads, 0, 0).astype(BF16)
    grad_w_out = product(grad_branch, flat_heads, 0, 0).astype(BF16)
    grad_att = grad_flat.astype(BF16).reshape(row_count, heads_here, HEAD_SIZE)
    grad_query, grad_keys, grad_values = attend_back(
        query_rows, key_rows, value_rows, places, segment, factor, logsum, grad_att
    )
    grad_query = (
        rotate_back(grad_query, head_cos, head_sin).reshape(row_count, heads_width).astype(BF16)
    )
    grad_joint_all = jnp.concatenate(
        [rotate_back(grad_keys, cosine, sine_part), grad_values], axis=1
    )
    grad_joint_all = grad_joint_all.astype(BF16)
    grad_kv = lax.psum_scatter(
        grad_joint_all, "mp", scatter_dimension=1, tiled=True
    )
    grad_joint = jnp.concatenate([grad_query, grad_kv], axis=1)
    grad_pick = product(grad_kv, key_value_lifted, 1, 1)
    zero_rank = jnp.zeros_like(grad_pick)
    grad_rank_part = [
        product(grad_query, query_lifted, 1, 1),
        jnp.where(is_key, grad_pick, zero_rank),
        jnp.where(is_key, zero_rank, grad_pick),
    ]
    grad_norm_part = product(grad_joint, joint_weight, 1, 1)
    grad_norm_part = jnp.concatenate([grad_norm_part, *grad_rank_part], axis=1).astype(BF16)
    grad_norm_part = after(grad_norm_part, ffn_first)
    if dp_count == 4:
        grad_norm_part = after(grad_norm_part, *first_sent)
    grad_norm_one = lax.psum(grad_norm_part, "mp")
    grad_rank_qkv = [
        grad_norm_one[:, model_width + k * rank : model_width + (k + 1) * rank] for k in range(3)
    ]
    grad_norm_one = grad_norm_one[:, :model_width]
    ffn_last = lax.psum(after(ffn_all[half_rows:, :model_width], grad_norm_one), "mp")
    ffn_sum = jnp.concatenate([ffn_first, ffn_last], axis=0)
    output = hidden_state + ffn_sum.astype(F32) + dot(rank_down, model_lifted[1])
    result_rows = relative(output.astype(BF16), 1, dp_id, dp_count)
    grad_rank_qkv = jnp.concatenate([swap_ranks(g) for g in grad_rank_qkv], axis=1)
    grad_input_attn = product(normalized_rows, grad_rank_qkv, 0, 0).astype(BF16)
    grad_norm_one = grad_norm_one.astype(F32) + product(grad_rank_qkv, input_attn, 1, 1)
    grad_source, grad_gain_one = rms_backward(source, inverse_one, gain_one, grad_norm_one)
    grad_input = relative((grad_source + grad_hidden).astype(BF16), 1, dp_id, dp_count)

    def by_dp(block):
        return block.reshape(dp_count, block.shape[0] // dp_count, block.shape[1])

    def over_cores(block):
        halves = block.reshape(dp_count, 2, part_width, block.shape[1])
        mine = lax.dynamic_index_in_dim(halves, depth_id, 1, keepdims=False)
        theirs = lax.dynamic_index_in_dim(halves, 1 - depth_id, 1, keepdims=False)
        return add_rounded(mine, partner(theirs))

    grad_w_joint = over_cores(product(normalized_rows, grad_joint, 0, 0).astype(BF16))
    grad_lifted = by_dp(
        jnp.concatenate(
            [product(rank_query, grad_query, 0, 0), product(rank_pick, grad_kv, 0, 0)], axis=1
        ).astype(BF16)
    )
    joint_own = scatter_dp(
        [jnp.concatenate([grad_w_joint[p], grad_lifted[p]], axis=0) for p in range(dp_count)],
        grad_norm_part,
    )
    grad_w_out = over_cores(grad_w_out)
    grad_out_down = by_dp(grad_out_down)
    out_own = scatter_dp(
        [jnp.concatenate([grad_w_out[p], grad_out_down[p]], axis=0) for p in range(dp_count)],
        grad_norm_part,
    )
    grad_model = [
        by_dp(relative(product(rank_out, grad_branch, 0, 0).astype(BF16), 1, dp_id, dp_count)),
        by_dp(relative(product(rank_down, grad_ffn, 0, 0).astype(BF16), 1, dp_id, dp_count)),
    ]
    model_own = scatter_dp(
        [jnp.concatenate([g[p] for g in grad_model], axis=0) for p in range(dp_count)],
        grad_norm_part,
    )
    grad_input_ffn = by_dp(grad_input_ffn)
    ffn_in_own = scatter_dp([grad_input_ffn[p] for p in range(dp_count)], grad_norm_part)
    gain_grads = jnp.stack([grad_gain_one, grad_gain_two])
    gain_grads = gain_grads + partner(gain_grads)
    gain_grads = gain_grads.reshape(2, dp_count, 2, part_width)
    gain_grads = lax.dynamic_index_in_dim(gain_grads, depth_id, 2, keepdims=False).astype(BF16)
    grad_input_attn = by_dp(grad_input_attn)
    attn_in_own = scatter_dp(
        [
            jnp.concatenate(
                [grad_input_attn[p], pad_rows(gain_grads[:, p], 16, 3 * rank)], axis=0
            )
            for p in range(dp_count)
        ]
    )
    grad_w_gains = attn_in_own[slice_width : slice_width + 2, :part_width]
    input_own = jnp.concatenate([attn_in_own[:slice_width], ffn_in_own], axis=1)
    grad_lora_in = jnp.stack([input_own[:, k * rank : (k + 1) * rank] for k in range(5)])[None]

    if dp_count == 4:
        mine, theirs = [], []
        for group, (last_one, last_two) in zip(groups, last_sent):
            own_blocks = weight_share(
                lambda n, at=group.start, got=(last_one, last_two): [
                    (0, 0, ((first_sent[0], at + n), (got[1], n)), F32),
                    (0, 1, ((first_sent[1], at + n), (got[0], n)), BF16),
                ],
                group,
                grad_norm_part,
            )
            mine.append(own_blocks[0])
            theirs.append(partner(own_blocks[1]))
    else:
        blocks = [
            weight_share([(p, 0, (), BF16), (p, 1, (), BF16)], range(CHUNKS), None)
            for p in range(dp_count)
        ]
        mine = [scatter_dp([b[0] for b in blocks])]
        theirs = [partner(scatter_dp([b[1] for b in blocks]).astype(BF16))]
    grad_w_gateup, grad_w_down, grad_lora_gateup, grad_lora_hidden = finish_pass(
        core, mine, theirs, part_width, rank_part, hidden
    )

    mixed_rows = jnp.where(keep_own, result_rows, partner(result_rows))
    grad_tokens = jnp.where(keep_own, grad_input, partner(grad_input))
    return (
        mixed_rows,
        grad_tokens,
        joint_own[:part_width, :heads_width],
        joint_own[:part_width, heads_width:],
        out_own[:part_width].T,
        grad_w_gateup,
        grad_w_down,
        grad_w_gains,
        grad_lora_in,
        joint_own[part_width:, :heads_width][None],
        joint_own[part_width:, heads_width:][None],
        out_own[part_width:][None],
        grad_lora_hidden,
        model_own.reshape(1, 2, rank_part, model_width),
        grad_lora_gateup,
    )


def solution(mesh):
    return jax.shard_map(
        local,
        mesh=mesh,
        in_specs=(
            P(("dp", "depth"), None),
            P(("dp", "depth"), None),
            P("dp", None, None),
            P("dp", None),
            P(("dp", "depth"), "mp"),
            P(("dp", "depth"), "mp"),
            P("mp", ("dp", "depth")),
            P(None, ("dp", "depth"), "mp"),
            P("mp", ("dp", "depth")),
            P(None, ("dp", "depth")),
            P("depth", None, "dp", None),
            P("depth", "dp", "mp"),
            P("depth", "dp", "mp"),
            P("depth", "dp", "mp"),
            P("depth", "dp", "mp"),
            P("depth", None, "dp", None),
            P("depth", None, "dp", "mp"),
        ),
        out_specs=(
            P(("dp", "depth"), None),
            P(("dp", "depth"), None),
            P(("dp", "depth"), "mp"),
            P(("dp", "depth"), "mp"),
            P("mp", ("dp", "depth")),
            P(None, ("dp", "depth"), "mp"),
            P("mp", ("dp", "depth")),
            P(None, ("dp", "depth")),
            P("depth", None, "dp", None),
            P("depth", "dp", "mp"),
            P("depth", "dp", "mp"),
            P("depth", "dp", "mp"),
            P("depth", "dp", "mp"),
            P("depth", None, "dp", None),
            P("depth", None, "dp", "mp"),
        ),
        check_vma=False,
    )
```

```python
import functools

import jax
import jax.numpy as jnp
from jax import lax
from jax.experimental import pallas as pl
from jax.experimental.pallas import tpu as pltpu
from jax.sharding import PartitionSpec as P

HEAD_SIZE = 256


EPS = 1e-06
THETA = 10000.0
NEGATIVE = -1e30


def product(left_op, right_op, left_dim, right_dim):
    return lax.dot_general(
        left_op,
        right_op,
        (((left_dim,), (right_dim,)), ((), ())),
        preferred_element_type=jnp.float32,
    )


def layout(seq_lens, row_count):
    seq_ends = jnp.cumsum(seq_lens)
    places = jnp.arange(row_count, dtype=jnp.int32)
    passed = (places[:, None] >= seq_ends[None, :]).astype(jnp.int32)
    segment = jnp.sum(passed, axis=1)
    starts = jnp.sum(passed * seq_lens[None, :], axis=1)
    valid_rows = (places < seq_ends[-1]).astype(jnp.float32)
    within = (places - starts).astype(jnp.float32)
    return (places, segment, within, valid_rows)


def rotary(within, head_width):
    half_width = head_width // 2
    frequency = THETA ** (-2.0 * jnp.arange(half_width, dtype=jnp.float32) / head_width)
    angles = within[:, None] * frequency[None, :]
    return (jnp.cos(angles), jnp.sin(angles))


def rotate(vector, cosine, sine_part):
    half_width = vector.shape[-1] // 2
    former = vector[..., :half_width]
    latter = vector[..., half_width:]
    return jnp.concatenate(
        [former * cosine - latter * sine_part, latter * cosine + former * sine_part], axis=-1
    )


def rotate_back(vector, cosine, sine_part):
    half_width = vector.shape[-1] // 2
    former = vector[..., :half_width]
    latter = vector[..., half_width:]
    return jnp.concatenate(
        [former * cosine + latter * sine_part, latter * cosine - former * sine_part], axis=-1
    )


def rms_forward(values, gain_row):
    inverse = lax.rsqrt(jnp.mean(values * values, axis=-1, keepdims=True) + EPS)
    return (values * inverse * gain_row, inverse)


def rms_backward(values, inverse, gain_row, grad_norm):
    weighted = grad_norm * gain_row
    grad_values = inverse * weighted - values * inverse**3 * jnp.mean(
        weighted * values, axis=-1, keepdims=True
    )
    grad_gain = jnp.sum(grad_norm * values * inverse, axis=0)
    return (grad_values, grad_gain)


def gelu_tanh(values):
    return jax.nn.gelu(values, approximate=True)


def block_mask(places, segment):
    return (segment[:, None] == segment[None, :]) & (places[None, :] <= places[:, None])


CHUNKS = 4
GROUPS = 2
BF16 = jnp.bfloat16
F32 = jnp.float32


def trade(block, axis, mask):
    count = lax.axis_size(axis)
    return lax.ppermute(block, axis, [(i, i ^ mask) for i in range(count)])


def gather_dp(piece, *hold):
    count = lax.axis_size("dp")
    if count == 4:
        half = piece.shape[0] // 2
        from_one = trade(piece, "dp", 1)
        from_two = trade(piece, "dp", 2)
        far = jnp.concatenate(
            [
                trade(after(from_two[:half], *hold), "dp", 1),
                trade(after(from_one[half:], *hold), "dp", 2),
            ],
            axis=0,
        )
        return [piece, from_one, from_two, far]
    pieces, mask = [piece], 1
    while mask < count:
        pieces = pieces + [trade(held, "dp", mask) for held in pieces]
        mask *= 2
    return pieces


def gather_pair(one, two, early):
    count = lax.axis_size("dp")
    if count == 4:
        first_one, first_two = trade(one, "dp", 1), trade(one, "dp", 2)
        second_one, second_two = trade(two, "dp", 1), trade(two, "dp", 2)
        far = trade(after(first_two, early), "dp", 1), trade(second_one, "dp", 2)
        pieces = [(one, two), (first_one, second_one), (first_two, second_two), far]
        return pieces, far
    ones, twos = gather_dp(one), gather_dp(two)
    return list(zip(ones, twos)), (ones[-1], twos[-1])


def gather_near(bundle):
    count = lax.axis_size("dp")
    pieces, mask = [bundle], 1
    while mask < count:
        first = pieces if count != 4 else pieces[:1]
        pieces = pieces + [trade(held, "dp", mask) for held in first]
        mask *= 2
    return pieces


def gather_far(near, hold, height):
    chunks = [[((b, c), (b, CHUNKS + c)) for b in near] for c in range(CHUNKS)]
    if lax.axis_size("dp") == 4:
        size = CHUNKS // GROUPS
        for group in range(GROUPS):
            rows = (size * group * height, size * (group + 1) * height)
            one = lax.slice_in_dim(after(near[2], hold), *rows, axis=0)
            two = lax.slice_in_dim(
                after(near[1], hold), *[CHUNKS * height + r for r in rows], axis=0
            )
            one, two = trade(one, "dp", 1), trade(two, "dp", 2)
            for n in range(size):
                chunks[group * size + n].append(((one, n), (two, n)))
    return chunks


def scatter_dp(parts, *hold):
    count = lax.axis_size("dp")
    if hold:
        parts = [after(part, *hold) for part in parts]
    if count == 4:
        half = parts[3].shape[0] // 2
        near_one = trade(parts[3][:half], "dp", 1)
        near_two = trade(parts[3][half:], "dp", 2)
        for_two = jnp.concatenate([add_rounded(parts[2][:half], near_one), parts[2][half:]], axis=0)
        for_one = jnp.concatenate([parts[1][:half], add_rounded(parts[1][half:], near_two)], axis=0)
        got_one = trade(for_one, "dp", 1)
        got_two = trade(for_two, "dp", 2)
        return parts[0].astype(F32) + got_one.astype(F32) + got_two.astype(F32)
    mask = count // 2
    while mask:
        parts = [
            add_rounded(parts[p], trade(parts[p + mask], "dp", mask)) for p in range(mask)
        ]
        mask //= 2
    return parts[0].astype(F32)


def add_rounded(one, two):
    return (one.astype(F32) + two.astype(F32)).astype(BF16)


def relative(block, axis, index, count):
    width = block.shape[axis] // count
    mask = 1
    while mask < count:
        flipped = jnp.concatenate(
            [
                lax.slice_in_dim(block, (b ^ mask) * width, ((b ^ mask) + 1) * width, axis=axis)
                for b in range(count)
            ],
            axis=axis,
        )
        block = jnp.where((index & mask) > 0, flipped, block)
        mask *= 2
    return block


VMEM_LIMIT = 50 * 1024 * 1024
GELU_SCALE = 0.7978845608028654
LONG = pl.CostEstimate(flops=10**14, bytes_accessed=1, transcendentals=0)
BRIEF = pl.CostEstimate(flops=1, bytes_accessed=1, transcendentals=0)


def after(block, *earlier):
    return lax.optimization_barrier((block, *earlier))[0]


def whole_spec(shape):
    return pl.BlockSpec(shape, lambda *_: (0,) * len(shape), pipeline_mode=pl.Buffered(1))


def params():
    return pltpu.CompilerParams(vmem_limit_bytes=VMEM_LIMIT)


def nn(left_op, right_op):
    return product(left_op, right_op, 1, 0)


def nt(left_op, right_op):
    return product(left_op, right_op, 1, 1)


def late_split(height):
    return -(-height // 48) * 16


def pack_kernel(part, rank_part, rank, mp, *refs):
    query, key_value, output, gains, query_up, key_value_up, output_down = refs[:7]
    inputs, input_share, model_share, attn, one, late = refs[7:]
    heads = query.shape[1]
    one[...] = jnp.zeros_like(one)
    one[:part, :heads] = query[...]
    one[:part, heads:] = key_value[...]
    one[part : 2 * part, :heads] = output[...].T
    one[2 * part : 2 * part + 2, :part] = gains[...]
    first = 2 * part + 16
    one[first : first + rank_part, :heads] = query_up[0]
    one[first : first + rank_part, heads:] = key_value_up[0]
    one[first + rank_part :, :heads] = output_down[0]
    wide = inputs.shape[2]
    attn[wide:, :] = jnp.zeros_like(attn[wide:, :])
    for k in range(3):
        attn[:wide, k * rank : (k + 1) * rank] = inputs[0, k]
    row = 0
    for at in range(0, model_share.shape[3], rank):
        for k in range(2):
            late[row : row + rank_part, :] = model_share[0, k, :, at : at + rank]
            row += rank_part
    height = input_share.shape[2]
    for k in range(2):
        late[row : row + height, :] = input_share[0, 3 + k]
        row += height
    split = late_split(row)
    for k in range(3):
        rows = min(split, row - k * split)
        attn[wide : wide + rows, k * rank : (k + 1) * rank] = late[
            k * split : k * split + rows, :
        ]


def pack_pass(mp, arrays, mp_count, rank):
    query, key_value, output, gains, query_up, _, _, inputs, model_up = arrays
    part, rank_part = query.shape[0], query_up.shape[1]
    slice_width, columns = inputs.shape[2], model_up.shape[3] // mp_count
    rows = slice_width // mp_count
    late_rows = 2 * rank_part * (columns // rank) + 2 * rows
    shapes = [
        (slice_width + late_split(late_rows), 3 * rank),
        (2 * part + 16 + 2 * rank_part, query.shape[1] + key_value.shape[1]),
    ]

    def whole(shape):
        return pl.BlockSpec(shape, lambda s, mp: (0,) * len(shape))

    return pl.pallas_call(
        functools.partial(pack_kernel, part, rank_part, rank),
        grid_spec=pltpu.PrefetchScalarGridSpec(
            num_scalar_prefetch=1,
            grid=(1,),
            in_specs=[whole(a.shape) for a in arrays[:8]]
            + [
                pl.BlockSpec((1, 5, rows, rank), lambda s, mp: (0, 0, mp[0], 0)),
                pl.BlockSpec((1, 2, rank_part, columns), lambda s, mp: (0, 0, 0, mp[0])),
            ],
            out_specs=[whole(s) for s in shapes],
            scratch_shapes=[pltpu.VMEM((late_rows, rank), BF16)],
        ),
        out_shape=[jax.ShapeDtypeStruct(s, BF16) for s in shapes],
        compiler_params=params(),
        cost_estimate=BRIEF,
        name="pack_pass",
    )(mp, *arrays[:7], inputs, inputs, model_up)


def unpack_kernel(count, part, rank_part, *refs):
    pieces, (shared, inputs, late, lifted, out_down) = refs[: 2 * count], refs[2 * count :]
    rows = shared.shape[0] // count
    wide, rank = 2 * part, late.shape[2]
    heads = out_down.shape[1]
    height = late.shape[1]
    split = late_split(height)
    for p in range(count):
        attn, one = pieces[2 * p : 2 * p + 2]
        shared[p * rows : (p + 1) * rows, :] = one[:rows, :]
        here = slice(p * rank_part, (p + 1) * rank_part)
        lifted[here, :] = one[rows : rows + rank_part, :]
        out_down[here, :] = one[rows + rank_part :, :heads]
        inputs[p * wide : (p + 1) * wide, :] = attn[:wide, :]
        for k in range(3):
            number = min(split, height - k * split)
            late[p, k * split : k * split + number, :] = attn[
                wide : wide + number, k * rank : (k + 1) * rank
            ]


def unpack_pass(pieces, part, rank_part, rank, rows, columns, heads):
    count = len(pieces)
    joint = pieces[0][1].shape[1]
    late_rows = 2 * rank_part * (columns // rank) + 2 * rows
    flat = [b for pair in pieces for b in pair]
    shapes = [
        (count * (2 * part + 16), joint),
        (count * 2 * part, 3 * rank),
        (count, late_rows, rank),
        (count * rank_part, joint),
        (count * rank_part, heads),
    ]
    return pl.pallas_call(
        functools.partial(unpack_kernel, count, part, rank_part),
        grid=(1,),
        in_specs=[whole_spec(b.shape) for b in flat],
        out_specs=[whole_spec(s) for s in shapes],
        out_shape=[jax.ShapeDtypeStruct(s, BF16) for s in shapes],
        compiler_params=params(),
        cost_estimate=BRIEF,
        name="unpack_pass",
    )(*flat)


def shared_kernel(count, part, core, own, other, joint, output, gains):
    rows = own.shape[0] // count
    heads = output.shape[1]
    gains[...] = jnp.zeros_like(gains)
    for e in range(2):

        @pl.when(core[0] == e)
        def _(e=e):
            for side, source in ((e, own), (1 - e, other)):
                for p in range(count):
                    here = slice((2 * p + side) * part, (2 * p + side + 1) * part)
                    first = p * rows
                    joint[here, :] = source[first : first + part, :]
                    output[here, :] = source[first + part : first + 2 * part, :heads]
                    gains[:2, here] = source[first + 2 * part : first + 2 * part + 2, :part]


def shared_pass(core, own, other, count, part, heads):
    shapes = [(count * 2 * part, own.shape[1]), (count * 2 * part, heads), (16, count * 2 * part)]
    return pl.pallas_call(
        functools.partial(shared_kernel, count, part),
        grid=(1,),
        in_specs=[pl.BlockSpec(memory_space=pltpu.SMEM)] + [whole_spec(own.shape)] * 2,
        out_specs=[whole_spec(s) for s in shapes],
        out_shape=[jax.ShapeDtypeStruct(s, BF16) for s in shapes],
        compiler_params=params(),
        cost_estimate=BRIEF,
        name="shared_pass",
    )(core, own, other)


def late_kernel(rank_part, rows, count, late, model, inputs):
    rank = late.shape[3]
    for p in range(count):
        for n in range(model.shape[2] // rank):
            for k in range(2):
                first = (2 * n + k) * rank_part
                model[k, p * rank_part : (p + 1) * rank_part, n * rank : (n + 1) * rank] = late[
                    0, p, first : first + rank_part, :
                ]
        first = 2 * rank_part * (model.shape[2] // rank)
        for k in range(2):
            inputs[p, 0, :, k * rank : (k + 1) * rank] = late[
                0, p, first + k * rows : first + (k + 1) * rows, :
            ]


def late_pass(late, rows, columns, rank_part):
    mp_count, count, height, rank = late.shape
    model, inputs = pl.pallas_call(
        functools.partial(late_kernel, rank_part, rows, count),
        grid=(mp_count,),
        in_specs=[pl.BlockSpec((1, count, height, rank), lambda z: (z, 0, 0, 0))],
        out_specs=[
            pl.BlockSpec((2, rank, columns), lambda z: (0, 0, z)),
            pl.BlockSpec((count, 1, rows, 2 * rank), lambda z: (0, z, 0, 0)),
        ],
        out_shape=[
            jax.ShapeDtypeStruct((2, rank, mp_count * columns), BF16),
            jax.ShapeDtypeStruct((count, mp_count, rows, 2 * rank), BF16),
        ],
        compiler_params=params(),
        cost_estimate=BRIEF,
        name="late_pass",
    )(late)
    return model, inputs.reshape(count * mp_count * rows, 2 * rank)


def ffn_blocks(arrays, chunk, side):
    gate_up, down, lora_gate_up, lora_hidden = arrays

    def column(s, core):
        return side(core[0]) * CHUNKS + s

    return [
        pl.BlockSpec((2, gate_up.shape[1], chunk), lambda s, core: (0, 0, column(s, core))),
        pl.BlockSpec((chunk, down.shape[1]), lambda s, core: (column(s, core), 0)),
        pl.BlockSpec(
            (1, 2, lora_gate_up.shape[2], chunk), lambda s, core: (0, 0, 0, column(s, core))
        ),
        pl.BlockSpec((1, lora_hidden.shape[1], chunk), lambda s, core: (0, 0, column(s, core))),
    ]


def ffn_rows(gate_up, down, lora_gate_up, lora_hidden):
    return [
        gate_up[0],
        gate_up[1],
        down[...].T,
        jnp.concatenate([lora_gate_up[0, 0], lora_gate_up[0, 1], lora_hidden[0]], axis=0),
    ]


def give_kernel(core, gate_up, down, lora_gate_up, lora_hidden, given):
    first = 0
    for block in ffn_rows(gate_up, down, lora_gate_up, lora_hidden):
        given[first : first + block.shape[0], :] = block
        first += block.shape[0]


def give_pass(core, arrays, chunk):
    part, rank_part = arrays[0].shape[1], arrays[3].shape[1]
    height = 3 * (part + rank_part)
    return pl.pallas_call(
        give_kernel,
        grid_spec=pltpu.PrefetchScalarGridSpec(
            num_scalar_prefetch=1,
            grid=(CHUNKS,),
            in_specs=ffn_blocks(arrays, chunk, lambda me: 1 - me),
            out_specs=pl.BlockSpec((height, chunk), lambda s, core: (s, 0)),
        ),
        out_shape=jax.ShapeDtypeStruct((CHUNKS * height, chunk), BF16),
        compiler_params=params(),
        cost_estimate=BRIEF,
        name="give_pass",
    )(core, *arrays)


def bundle_kernel(part, core, gate_up, down, lora_gate_up, lora_hidden, taken, bundle):
    own_first = core[0] == 0
    one, two = bundle.at[0], bundle.at[1]
    gate, upper, lower, lifted = ffn_rows(gate_up, down, lora_gate_up, lora_hidden)

    def pair(own, start):
        other = taken[start : start + part, :]
        return jnp.where(own_first, own, other), jnp.where(own_first, other, own)

    one[:part, :], one[part : 2 * part, :] = pair(gate, 0)
    two[:part, :], two[part : 2 * part, :] = pair(upper, part)
    one[2 * part : 3 * part, :], two[2 * part : 3 * part, :] = pair(lower, 2 * part)
    one[3 * part :, :] = lifted
    two[3 * part :, :] = taken[3 * part :, :]


def bundle_pass(core, arrays, taken, chunk):
    part = arrays[0].shape[1]
    height = taken.shape[0] // CHUNKS
    out = pl.pallas_call(
        functools.partial(bundle_kernel, part),
        grid_spec=pltpu.PrefetchScalarGridSpec(
            num_scalar_prefetch=1,
            grid=(CHUNKS,),
            in_specs=ffn_blocks(arrays, chunk, lambda me: me)
            + [pl.BlockSpec((height, chunk), lambda s, core: (s, 0))],
            out_specs=pl.BlockSpec((2, height, chunk), lambda s, core: (0, s, 0)),
        ),
        out_shape=jax.ShapeDtypeStruct((2, CHUNKS * height, chunk), BF16),
        compiler_params=params(),
        cost_estimate=BRIEF,
        name="bundle_pass",
    )(core, *arrays, taken)
    return out.reshape(2 * CHUNKS * height, chunk)


def simple_pass(kernel, name, inputs, shapes, scalars=None, cost=BRIEF):
    specs = [whole_spec(a.shape) for a in inputs]
    if scalars is not None:
        inputs = (scalars, *inputs)
        specs = [pl.BlockSpec(memory_space=pltpu.SMEM)] + specs
    return pl.pallas_call(
        kernel,
        grid=(1,),
        in_specs=specs,
        out_specs=[whole_spec(shape) for shape, _ in shapes],
        out_shape=[jax.ShapeDtypeStruct(shape, dtype) for shape, dtype in shapes],
        compiler_params=params(),
        cost_estimate=cost,
        name=name,
    )(*inputs)


def tn(left_op, right_op):
    return product(left_op, right_op, 0, 0)


def rank_order(block, rank, shift):
    row = lax.broadcasted_iota(jnp.int32, (rank, rank), 0)
    column = lax.broadcasted_iota(jnp.int32, (rank, rank), 1)
    swap = (jnp.bitwise_xor(row, shift) == column).astype(F32).astype(BF16)
    parts = [
        nn(block[:, at : at + rank], swap).astype(BF16)
        for at in range(0, block.shape[1], rank)
    ]
    return jnp.concatenate(parts, axis=1)


def inverse_rms(values):
    return lax.rsqrt(jnp.mean(values * values, axis=-1, keepdims=True) + EPS)


def project_kernel(place, rows, gains, inputs, joint, lifted, cosine, sine, *outs):
    normed, ranks, query, joint_part = outs
    heads = query.shape[1]
    rank = inputs.shape[1] // 3
    values = rows[...].astype(F32)
    gain = gains[0:1, :].astype(F32)
    normed[...] = (values * inverse_rms(values) * gain).astype(BF16)
    ranks[...] = rank_order(nn(normed[...], inputs[...]).astype(BF16), rank, place[0])
    raw = nn(normed[...], joint[...])
    query_raw = raw[:, :heads] + nn(ranks[:, :rank], lifted[:, :heads])
    for at in range(0, heads, HEAD_SIZE):
        here = slice(at, at + HEAD_SIZE)
        query[:, here] = rotate(query_raw[:, here], cosine[...], sine[...]).astype(BF16)
    pick = jnp.where(place[1] == 1, ranks[:, rank : 2 * rank], ranks[:, 2 * rank :])
    joint_part[...] = (raw[:, heads:] + nn(pick, lifted[:, heads:])).astype(BF16)


def beside(blocks):
    return jnp.concatenate([blocks[n] for n in range(blocks.shape[0])], axis=1)


def head_probs(query, keys, rows_segment, columns_segment):
    count = query.shape[0]
    scores = nt(query, keys) * HEAD_SIZE ** (-0.5)
    row = lax.broadcasted_iota(jnp.int32, (count, count), 0)
    column = lax.broadcasted_iota(jnp.int32, (count, count), 1)
    allowed = (rows_segment == columns_segment) & (column <= row)
    scores = jnp.where(allowed, scores, NEGATIVE)
    powers = jnp.exp(scores - jnp.max(scores, axis=-1, keepdims=True))
    return powers / jnp.sum(powers, axis=-1, keepdims=True)


def attend_kernel(query, joint, cosine, sine, row_seg, column_seg, output, down, *outs):
    keys, flat, branch = outs
    width = output.shape[0]
    both = beside(joint)
    keys[...] = rotate(both[:, :HEAD_SIZE].astype(F32), cosine[...], sine[...]).astype(BF16)
    for at in range(0, flat.shape[1], HEAD_SIZE):
        here = slice(at, at + HEAD_SIZE)
        probs = head_probs(query[:, here], keys[...], row_seg[...], column_seg[...])
        flat[:, here] = nn(probs.astype(BF16), both[:, HEAD_SIZE:]).astype(BF16)
    branch[:, :width] = nt(flat[...], output[...]).astype(BF16)
    branch[:, width:] = nt(flat[...], down[...]).astype(BF16)


def second_kernel(place, rows, branch, model, gains, inputs, hidden, normed):
    width = rows.shape[1]
    rank = model.shape[1]
    hidden[...] = (
        rows[...].astype(F32)
        + branch[:, :width].astype(F32)
        + nn(branch[:, width:], model[0])
    )
    values = hidden[...]
    gain = gains[1:2, :].astype(F32)
    normed[:, :width] = (values * inverse_rms(values) * gain).astype(BF16)
    normed[:, width:] = rank_order(
        nn(normed[:, :width], inputs[...]).astype(BF16), rank, place[0]
    )


def early_kernel(block, early, late):
    rows, columns = early.shape[0], block.shape[1]
    early[:, :columns] = block[:rows, :]
    early[:, columns:] = block[rows:, columns - (early.shape[1] - columns) :]
    late[...] = block[rows:, : late.shape[1]]


def grad_kernel(rows, model, grad):
    width = rows.shape[1]
    grad[:, :width] = rows[...]
    grad[:, width:] = nt(rows[...], model[1]).astype(BF16)


def norm_back(values, gain, grad_norm):
    inverse = inverse_rms(values)
    weighted = grad_norm * gain
    grad_values = inverse * weighted - values * inverse**3 * jnp.mean(
        weighted * values, axis=-1, keepdims=True
    )
    return grad_values, jnp.sum(grad_norm * values * inverse, axis=0, keepdims=True)


def attend_back_kernel(place, summed, hidden, gains, inputs, grad_ffn, model, *refs):
    output, down, query, keys, joint, cosine, sine, row_seg, column_seg = refs[:9]
    grad_hidden, branch, rank_gu, rank_out, grad_query, grad_joint, grad_gain = refs[9:]
    width = hidden.shape[1]
    rank = down.shape[0]
    factor = HEAD_SIZE ** (-0.5)
    rank_gu[...] = rank_order(summed[:, width:], rank, place[0])
    grad_norm = summed[:, :width].astype(F32) + nt(rank_gu[...], inputs[...])
    values, gain_row = norm_back(hidden[...], gains[1:2, :].astype(F32), grad_norm)
    grad_gain[...] = jnp.broadcast_to(gain_row, grad_gain.shape)
    grad_hidden[...] = values + grad_ffn[...].astype(F32)
    branch[...] = grad_hidden[...].astype(BF16)
    rank_out[...] = nt(branch[...], model[0]).astype(BF16)
    grad_flat = (nn(branch[...], output[...]) + nn(rank_out[...], down[...])).astype(BF16)
    values_here = beside(joint)[:, HEAD_SIZE:]
    grad_keys = grad_values = 0.0
    for at in range(0, query.shape[1], HEAD_SIZE):
        here = slice(at, at + HEAD_SIZE)
        probs = head_probs(query[:, here], keys[...], row_seg[...], column_seg[...])
        grad_probs = nt(grad_flat[:, here], values_here)
        grad_values += tn(probs.astype(BF16), grad_flat[:, here])
        centre = jnp.sum(grad_probs * probs, axis=-1, keepdims=True)
        grad_scores = (probs * (grad_probs - centre)).astype(BF16)
        turned = rotate_back(nn(grad_scores, keys[...]) * factor, cosine[...], sine[...])
        grad_query[:, here] = turned.astype(BF16)
        grad_keys += tn(grad_scores, query[:, here]) * factor
    both = jnp.concatenate([rotate_back(grad_keys, cosine[...], sine[...]), grad_values], axis=1)
    kv = grad_joint.shape[2]
    for n in range(grad_joint.shape[0]):
        grad_joint[n] = both[:, n * kv : (n + 1) * kv].astype(BF16)


def project_back_kernel(place, grad_query, grad_kv, joint, lifted, out):
    heads = grad_query.shape[1]
    width, rank = joint.shape[0], lifted.shape[0]
    out[:, :width] = (
        nt(grad_query[...], joint[:, :heads]) + nt(grad_kv[...], joint[:, heads:])
    ).astype(BF16)
    pick = nt(grad_kv[...], lifted[:, heads:]).astype(BF16)
    none = jnp.zeros_like(pick)
    out[:, width : width + rank] = nt(grad_query[...], lifted[:, :heads]).astype(BF16)
    out[:, width + rank : width + 2 * rank] = jnp.where(place[1] == 1, pick, none)
    out[:, width + 2 * rank :] = jnp.where(place[1] == 1, none, pick)


def first_back_kernel(place, summed, rows, gains, inputs, grad_hidden, *outs):
    grad_rows, ranks, grad_gain = outs
    width = rows.shape[1]
    ranks[...] = rank_order(summed[:, width:], inputs.shape[1] // 3, place[0])
    grad_norm = summed[:, :width].astype(F32) + nt(ranks[...], inputs[...])
    values, gain_row = norm_back(rows[...].astype(F32), gains[0:1, :].astype(F32), grad_norm)
    grad_gain[...] = jnp.broadcast_to(gain_row, grad_gain.shape)
    grad_rows[...] = (values + grad_hidden[...]).astype(BF16)


def folded(block, width):
    blocks = [block[:, at : at + width] for at in range(0, block.shape[1], width)]
    return blocks[0] if len(blocks) == 1 else jnp.concatenate(blocks, axis=0)


def share_of(block, first, rows):
    total = jnp.zeros((rows, block.shape[1]), block.dtype)
    for at in range(0, block.shape[0], rows):
        total = jnp.where(first == at, block[at : at + rows], total)
    return total


def shares_kernel(count, share_rows, share_columns, place, normed, grad_query, grad_kv, ranks, branch, flat, *refs):
    rank_out, out_sum, second, rank_gu, down_sum, grad_ffn = refs[:6]
    mine, theirs, *rest = refs[6:]
    heads, kv = grad_query.shape[1], grad_kv.shape[1]
    width = normed.shape[1]
    rank = rank_out.shape[1]
    part, rank_part = width // (2 * count), rank // count
    own_first = place[2] == 0
    pick = jnp.where(place[1] == 1, ranks[:, rank : 2 * rank], ranks[:, 2 * rank : 3 * rank])

    def put(target, p, start, block):
        target[p, start : start + block.shape[0], :] = block.astype(BF16)
        return start + block.shape[0]

    def put_rest(p, start, block):
        rest[p][start : start + block.shape[0], :] = block.astype(BF16)
        return start + block.shape[0]

    lift_query = tn(ranks[:, :rank], grad_query[...])
    lift_kv = tn(pick, grad_kv[...])
    out_down = tn(rank_out[...], flat[...])
    for p in range(count):
        columns = slice(2 * p * part, 2 * (p + 1) * part)
        here = slice(p * rank_part, (p + 1) * rank_part)
        query = tn(normed[:, columns], grad_query[...])
        joint = tn(normed[:, columns], grad_kv[...])
        output = tn(branch[:, columns], flat[...])
        quarter = part * kv // heads
        for side, target in ((0, mine), (1, theirs)):
            first = [jnp.where(own_first, b[:part], b[part:]) for b in (query, joint, output)]
            other = [jnp.where(own_first, b[part:], b[:part]) for b in (query, joint, output)]
            blocks = first if side == 0 else other
            put(target, p, 0, blocks[0])
            for n in range(part // quarter):
                target[p, part : part + quarter, n * kv : (n + 1) * kv] = blocks[1][
                    n * quarter : (n + 1) * quarter
                ].astype(BF16)
            put(target, p, part + quarter, blocks[2])
        at = put_rest(p, 0, lift_query[here])
        small = rank_part * kv // heads
        for n in range(rank_part // small):
            rest[p][at : at + small, n * kv : (n + 1) * kv] = lift_kv[
                p * rank_part + n * small : p * rank_part + (n + 1) * small
            ].astype(BF16)
        at = put_rest(p, at + small, out_down[here])
        here_columns = pl.multiple_of(place[4], 128)
        for ranks_of, rows_of in ((out_sum, branch), (down_sum, grad_ffn)):
            value = tn(ranks_of[:, here], rows_of[:, pl.ds(here_columns, share_columns)])
            for block in range(0, share_columns, heads):
                at = put_rest(p, at, value[:, block : block + heads])
        if share_rows % 128 == 0:
            first = pl.multiple_of(2 * p * part + place[5], 128)
            value = tn(second[:, pl.ds(first, share_rows)], rank_gu[...])
        else:
            value = share_of(tn(second[:, columns], rank_gu[...]), place[5], share_rows)
        for block in range(0, value.shape[1], heads):
            at = put_rest(p, at, value[:, block : block + heads])


def add_kernel(*refs):
    total = 0.0
    for ref in refs[:-1]:
        total += ref[...].astype(F32).reshape(refs[-1].shape)
    refs[-1][...] = total.astype(refs[-1].dtype)


def add_pass(dtype, *blocks):
    inputs, specs = [], []
    for block in blocks:
        if isinstance(block, tuple):
            block, at = block
            specs.append(
                pl.BlockSpec(
                    (1, *block.shape[1:]), functools.partial(lambda at, t: (at, 0, 0), at)
                )
            )
            shape = block.shape[1:]
        else:
            specs.append(whole_spec(block.shape))
            shape = block.shape
        inputs.append(block)
    return pl.pallas_call(
        add_kernel,
        grid=(1,),
        in_specs=specs,
        out_specs=whole_spec(shape),
        out_shape=jax.ShapeDtypeStruct(shape, dtype),
        compiler_params=params(),
        cost_estimate=BRIEF,
        name="add_pass",
    )(*inputs)


def gate_kernel(count, width, rank_part, has_base, *refs):
    blocks, refs = refs[:4], refs[4:]
    pieces = [(refs[2 * p], refs[2 * p + 1]) for p in range(count)]
    refs = refs[2 * count :]
    bases, refs = (refs[:2], refs[2:]) if has_base else ((), refs)
    gated_ref, gate_ref, upper_ref, *outs = refs[:5]
    adapters = refs[5]
    start = pl.program_id(0) == 0
    rows = blocks[0].shape[0]
    part = width // 2
    rank = count * rank_part
    model_width = count * width
    for b in range(2):
        for k in range(3):
            first = 3 * part + k * rank_part
            for p in range(count):
                adapters[3 * b + k, p * rank_part : (p + 1) * rank_part, :] = pieces[p][b][
                    first : first + rank_part, :
                ]
    for b in range(2):
        normed, grad = blocks[b], blocks[2 + b]
        span = slice(b * rows, (b + 1) * rows)
        gate = nn(normed[:, model_width : model_width + rank], adapters[3 * b])
        upper = nn(normed[:, model_width + rank :], adapters[3 * b + 1])
        grad_gated = nn(grad[:, model_width:], adapters[3 * b + 2])
        for p in range(count):
            columns = slice(p * width, (p + 1) * width)
            gate += nn(normed[:, columns], pieces[p][0][:width, :])
            upper += nn(normed[:, columns], pieces[p][1][:width, :])
            for e in range(2):
                columns = slice(p * width + e * part, p * width + (e + 1) * part)
                grad_gated += nn(grad[:, columns], pieces[p][e][width : width + part, :])
        square = gate * gate
        bent = jnp.tanh(GELU_SCALE * gate * (1.0 + 0.044715 * square))
        half = 0.5 * (1.0 + bent)
        active = gate * half
        slope = half + 0.5 * gate * (1.0 - bent * bent) * GELU_SCALE * (
            1.0 + 3.0 * 0.044715 * square
        )
        gated_ref[span, :] = (active * upper).astype(BF16)
        gate_ref[span, :] = (grad_gated * upper * slope).astype(BF16)
        upper_ref[span, :] = (grad_gated * active).astype(BF16)

    def put(b, first, value):
        columns = slice(first, first + value.shape[1])
        before = outs[b][:, columns].astype(F32)
        base = bases[b][:, columns].astype(F32) if bases else jnp.zeros_like(before)
        value = value + jnp.where(start, base, before)
        outs[b][:, columns] = value.astype(outs[b].dtype)

    for p in range(count):
        value = nt(gate_ref[...], pieces[p][0][:width, :]) + nt(
            upper_ref[...], pieces[p][1][:width, :]
        )
        for b in range(2):
            put(b, p * width, value[b * rows : (b + 1) * rows])
    for b in range(2):
        span = slice(b * rows, (b + 1) * rows)
        put(b, model_width, nt(gate_ref[span, :], adapters[3 * b]))
        put(b, model_width + rank, nt(upper_ref[span, :], adapters[3 * b + 1]))


def gate_pass(normed_pair, grad_pair, chunks, width, rank_part, bases, last):
    blocks = (*normed_pair, *grad_pair)
    rows, columns = blocks[0].shape
    both_rows, size = 2 * rows, len(chunks)
    pairs = [block for pair in chunks[0] for block in pair]
    height = 3 * (width // 2 + rank_part)
    chunk = pairs[0][0].shape[1]
    tiled = pl.BlockSpec((both_rows, chunk), lambda t: (0, t))
    return pl.pallas_call(
        functools.partial(gate_kernel, len(chunks[0]), width, rank_part, bool(bases)),
        grid=(size,),
        in_specs=[whole_spec(a.shape) for a in blocks]
        + [
            pl.BlockSpec((height, chunk), functools.partial(lambda at, t: (at + t, 0), at))
            for _, at in pairs
        ]
        + [whole_spec(a.shape) for a in bases],
        out_specs=[tiled] * 3 + [whole_spec((rows, columns))] * 2,
        out_shape=[jax.ShapeDtypeStruct((both_rows, size * chunk), BF16)] * 3
        + [
            jax.ShapeDtypeStruct((rows, columns), F32 if last else BF16),
            jax.ShapeDtypeStruct((rows, columns), BF16),
        ],
        scratch_shapes=[pltpu.VMEM((6, len(chunks[0]) * rank_part, chunk), BF16)],
        compiler_params=pltpu.CompilerParams(vmem_limit_bytes=60 * 1024 * 1024),
        cost_estimate=BRIEF,
        name="gate_pass",
    )(*blocks, *[block for block, _ in pairs], *bases)


def down_kernel(count, rows, width, rank_part, chunks, *refs):
    acts, refs = refs[:chunks], refs[chunks:]
    outs, adapters = refs[-3:-1], refs[-1]
    part = width // 2
    pieces = [
        [refs[2 * (q * count + p) : 2 * (q * count + p) + 2] for p in range(count)]
        for q in range(chunks)
    ]
    for b in range(2):
        span = slice(b * rows, (b + 1) * rows)
        for p in range(count):
            for e in range(2):
                value = nt(acts[0][span, :], pieces[0][p][e][width : width + part, :])
                for q in range(1, chunks):
                    value += nt(acts[q][span, :], pieces[q][p][e][width : width + part, :])
                first = p * width + e * part
                outs[b][:, first : first + part] = value.astype(outs[b].dtype)
        value = 0.0
        first = 3 * part + 2 * rank_part
        for q in range(chunks):
            for p in range(count):
                adapters[p * rank_part : (p + 1) * rank_part, :] = pieces[q][p][b][
                    first : first + rank_part, :
                ]
            value += nt(acts[q][span, :], adapters[...])
        outs[b][:, count * width :] = value.astype(outs[b].dtype)


def down_pass(acts, chunks, width, rank_part):
    count = len(chunks[0])
    both_rows = acts[0][0].shape[0]
    chunk = chunks[0][0][0][0].shape[1]
    rows = both_rows // 2
    columns = count * (width + rank_part)
    height = 3 * (width // 2 + rank_part)
    pairs = [block for pieces in chunks for pair in pieces for block in pair]
    shapes = [
        jax.ShapeDtypeStruct((rows, columns), F32),
        jax.ShapeDtypeStruct((rows, columns), BF16),
    ]
    return pl.pallas_call(
        functools.partial(down_kernel, count, rows, width, rank_part, len(chunks)),
        grid=(1,),
        in_specs=[
            pl.BlockSpec(
                (both_rows, chunk),
                functools.partial(lambda n, t: (0, n), n),
                pipeline_mode=pl.Buffered(1),
            )
            for _, n in acts
        ]
        + [
            pl.BlockSpec(
                (height, chunk),
                functools.partial(lambda at, t: (at, 0), at),
                pipeline_mode=pl.Buffered(1),
            )
            for _, at in pairs
        ],
        out_specs=[whole_spec(s.shape) for s in shapes],
        out_shape=shapes,
        scratch_shapes=[pltpu.VMEM((count * rank_part, chunk), BF16)],
        compiler_params=params(),
        cost_estimate=BRIEF,
        name="down_pass",
    )(*[a for a, _ in acts], *[block for block, _ in pairs])


def sum_kernel(*refs):
    total = refs[0][...].astype(F32)
    for other in refs[1:-1]:
        total = total + other[...].astype(F32)
    refs[-1][...] = total.astype(BF16)


def sum_pass(*blocks):
    blocks = [b if isinstance(b, tuple) else (b, 0) for b in blocks]
    rows, columns = min((b.shape for b, _ in blocks), key=lambda shape: shape[0])
    steps = 4
    return pl.pallas_call(
        sum_kernel,
        grid=(steps,),
        in_specs=[
            pl.BlockSpec(
                (rows // steps, columns), functools.partial(lambda at, t: (at * steps + t, 0), at)
            )
            for _, at in blocks
        ],
        out_specs=pl.BlockSpec((rows // steps, columns), lambda t: (t, 0)),
        out_shape=jax.ShapeDtypeStruct((rows, columns), BF16),
        compiler_params=params(),
        cost_estimate=BRIEF,
        name="sum_pass",
    )(*[b for b, _ in blocks])


def turn_kernel(own, other, turned):
    rows = own.shape[0]
    turned[:, :rows] = own[...].T
    turned[:, rows:] = other[...].T


def turn_pass(own, other):
    rows, columns = own.shape
    tile = 256
    source = pl.BlockSpec((rows, tile), lambda t: (0, t))
    return pl.pallas_call(
        turn_kernel,
        grid=(columns // tile,),
        in_specs=[source, source],
        out_specs=pl.BlockSpec((tile, 2 * rows), lambda t: (t, 0)),
        out_shape=jax.ShapeDtypeStruct((columns, 2 * rows), own.dtype),
        compiler_params=params(),
        cost_estimate=BRIEF,
        name="turn_pass",
    )(own, other)


def weight_kernel(part, rank_part, sides, adds, aliased, core, *refs):
    gate, upper, gated = refs[:3]
    refs = refs[3:]
    rows = gate.shape[0] // 2
    outs = refs[-len(sides) :]
    for side, number, out in zip(sides, adds, outs):
        normed, grad, *ranks = refs[:5]
        added = refs[5 : 5 + number]
        refs = refs[5 + number :]

        def store(start, value):
            here = slice(start, start + value.shape[0])
            for other in added:
                value = value + other[here, :].astype(F32)
            out[here, :] = value.astype(out.dtype)

        for n, (columns, act) in enumerate(((normed, gate), (normed, upper), (grad, gated))):
            store(n * part, nn(columns[...], act[...]))
        span = slice(side * rows, (side + 1) * rows)
        for n, act in enumerate((gate, upper, gated)):
            store(3 * part + n * rank_part, nn(ranks[n][:, span], act[span, :]))


def weight_pass(core, normed_t, grad_t, width, rank_part, acts, chunk, at, count, items, held=()):
    both_rows = normed_t.shape[1]
    part = width // 2
    height = 3 * (part + rank_part)
    tile = min(256, chunk)
    model_blocks = (2 * grad_t.shape[0] - normed_t.shape[0]) // rank_part
    rank_blocks = (normed_t.shape[0] - grad_t.shape[0]) // rank_part

    def rows_of(index, side):
        return pl.BlockSpec(
            (part, both_rows),
            lambda t, core: (2 * index + (core[0] ^ side), 0),
            pipeline_mode=pl.Buffered(1),
        )

    def ranks_of(block):
        return pl.BlockSpec(
            (rank_part, both_rows), lambda t, core: (block, 0), pipeline_mode=pl.Buffered(1)
        )

    tiled = pl.BlockSpec((height, tile), lambda t, core: (at, t))
    inputs = [a for a, _ in acts]
    specs = [
        pl.BlockSpec(
            (both_rows, tile),
            functools.partial(lambda n, t, core: (0, n * (chunk // tile) + t), n),
        )
        for _, n in acts
    ]
    for index, side, added, _ in items:
        inputs += [normed_t, grad_t, normed_t, normed_t, grad_t, *[block for block, _ in added]]
        specs += [rows_of(index, side)] * 2
        specs += [ranks_of(model_blocks + n * rank_blocks + index) for n in (0, 1, 0)]
        specs += [
            pl.BlockSpec((height, tile), functools.partial(lambda n, t, core: (n, t), n))
            for _, n in added
        ]
    aliases = {1 + len(inputs) + n: n for n in range(len(held))}
    return pl.pallas_call(
        functools.partial(
            weight_kernel,
            part,
            rank_part,
            tuple(item[1] for item in items),
            tuple(len(item[2]) for item in items),
            len(held),
        ),
        grid_spec=pltpu.PrefetchScalarGridSpec(
            num_scalar_prefetch=1,
            grid=(chunk // tile,),
            in_specs=specs + [pl.BlockSpec(memory_space=pl.ANY) for _ in held],
            out_specs=[tiled] * len(items),
        ),
        out_shape=[jax.ShapeDtypeStruct((count * height, chunk), item[3]) for item in items],
        input_output_aliases=aliases,
        compiler_params=params(),
        cost_estimate=BRIEF,
        name="weight_pass",
    )(core, *inputs, *held)


def finish_kernel(part, rank_part, core, *refs):
    *mine, other = refs[:-4]
    gate_up, down, lora_gate_up, lora_hidden = refs[-4:]
    for side, sources in enumerate((mine, [other])):

        @pl.when(pl.program_id(0) == side)
        def _(sources=sources):
            def rows(start, height):
                total = sources[0][start : start + height, :].astype(F32)
                for source in sources[1:]:
                    total = total + source[start : start + height, :].astype(F32)
                return total

            gate_up[0] = rows(0, part)
            gate_up[1] = rows(part, part)
            down[...] = rows(2 * part, part).T
            lora_gate_up[0, 0] = rows(3 * part, rank_part)
            lora_gate_up[0, 1] = rows(3 * part + rank_part, rank_part)
            lora_hidden[0] = rows(3 * part + 2 * rank_part, rank_part)


def finish_pass(core, mine, other, part, rank_part, hidden):
    chunk = other.shape[1]
    height = other.shape[0] // CHUNKS

    def source(side, first=0):
        return pl.BlockSpec(
            (height, chunk),
            lambda s, q, core: (first + jnp.where(s == side, q, (CHUNKS - 1) * (1 - side)), 0),
        )

    def column(s, q, core):
        return (core[0] ^ s) * CHUNKS + q

    shapes = [
        jax.ShapeDtypeStruct(s, F32)
        for s in (
            (2, part, hidden),
            (hidden, part),
            (1, 2, rank_part, hidden),
            (1, rank_part, hidden),
        )
    ]
    grid_spec = pltpu.PrefetchScalarGridSpec(
        num_scalar_prefetch=1,
        grid=(2, CHUNKS),
        in_specs=[source(0, first) for _, first in mine] + [source(1)],
        out_specs=[
            pl.BlockSpec((2, part, chunk), lambda s, q, core: (0, 0, column(s, q, core))),
            pl.BlockSpec((chunk, part), lambda s, q, core: (column(s, q, core), 0)),
            pl.BlockSpec(
                (1, 2, rank_part, chunk), lambda s, q, core: (0, 0, 0, column(s, q, core))
            ),
            pl.BlockSpec((1, rank_part, chunk), lambda s, q, core: (0, 0, column(s, q, core))),
        ],
    )
    return pl.pallas_call(
        functools.partial(finish_kernel, part, rank_part),
        grid_spec=grid_spec,
        out_shape=shapes,
        compiler_params=params(),
        cost_estimate=BRIEF,
        name="finish_pass",
    )(core, *[block for block, _ in mine], other)


def dot(left_op, right_op):
    return jnp.dot(left_op, right_op, preferred_element_type=F32)


def pad_rows(block, rows, width):
    return jnp.pad(block, ((0, rows - block.shape[0]), (0, width - block.shape[1])))


def local(
    tokens,
    cotangent,
    lengths,
    bucket_loop_index,
    query_weight,
    key_value_weight,
    output_weight,
    gate_up_weight,
    down_weight,
    gains,
    adapter_input_down,
    adapter_query_up,
    adapter_key_value,
    adapter_output_down,
    adapter_hidden_down,
    adapter_model_up,
    adapter_gate_up,
):
    dp_count = lax.axis_size("dp")
    dp_id = lax.axis_index("dp")
    depth_id = lax.axis_index("depth")
    mp_index = lax.axis_index("mp")
    first_core = depth_id == 0
    row_count, model_width = tokens.shape
    slice_width = model_width // dp_count
    part_width = slice_width // 2
    heads_width = query_weight.shape[1]
    heads_here = heads_width // HEAD_SIZE
    kv_width = key_value_weight.shape[1]
    joint_width = heads_width + kv_width
    rank_part = adapter_query_up.shape[1]
    rank = rank_part * dp_count
    hidden = down_weight.shape[0]
    half_hidden = hidden // 2
    chunk = half_hidden // CHUNKS

    def partner(block):
        return trade(block, "depth", 1)

    def in_core_order(own, other):
        return jnp.where(first_core, own, other), jnp.where(first_core, other, own)

    keep_own = bucket_loop_index[0, depth_id] == depth_id
    tok_swap, grad_swap = partner(tokens), partner(cotangent)
    slot_id = jnp.where(keep_own, depth_id, 1 - depth_id)
    seq_lens = lengths[0, slot_id]
    places, segment, within, valid_rows = layout(seq_lens, row_count)
    cosine, sine_part = rotary(within, HEAD_SIZE)
    tok_rows = relative(jnp.where(keep_own, tokens, tok_swap), 1, dp_id, dp_count)
    grad_rows = relative(jnp.where(keep_own, cotangent, grad_swap), 1, dp_id, dp_count)
    grad_ffn = (grad_rows.astype(F32) * valid_rows[:, None]).astype(BF16)

    mp_count = lax.axis_size("mp")
    share_rows = slice_width // mp_count
    share_columns = model_width // mp_count
    core = depth_id[None].astype(jnp.int32)
    ffn_arrays = (gate_up_weight, down_weight, adapter_gate_up, adapter_hidden_down)
    taken = partner(give_pass(core, ffn_arrays, chunk))
    bundles = pack_pass(
        mp_index[None].astype(jnp.int32),
        (query_weight, key_value_weight, output_weight, gains)
        + (adapter_query_up, adapter_key_value, adapter_output_down)
        + (adapter_input_down, adapter_model_up),
        mp_count,
        rank,
    )
    bundle = bundle_pass(core, ffn_arrays, taken, chunk)
    pieces, hold = gather_pair(*bundles, bundle)
    shared_own, input_attn, late, joint_lifted, out_down = unpack_pass(
        pieces, part_width, rank_part, rank, share_rows, share_columns, heads_width
    )
    joint_weight, out_weight, gains_all = shared_pass(
        core, shared_own, partner(shared_own), dp_count, part_width, heads_width
    )
    model_all, input_ffn = late_pass(
        lax.all_gather(late, "mp", axis=0, tiled=False),
        share_rows,
        share_columns,
        rank_part,
    )
    model_all = relative(model_all, 2, dp_id, dp_count)

    near = gather_near(after(bundle, *hold))
    height = 3 * (part_width + rank_part)

    is_key = mp_index * kv_width < HEAD_SIZE
    place = jnp.stack([dp_id * rank_part, is_key.astype(jnp.int32), depth_id, dp_id]
        + [((mp_index * share_columns // slice_width) ^ dp_id) * slice_width + mp_index * share_columns % slice_width, mp_index * share_rows]).astype(jnp.int32)
    row_segment, column_segment = segment[:, None], segment[None, :]
    normalized_rows, rank_rows, query_rows, joint_part = simple_pass(
        project_kernel,
        "project_pass",
        (tok_rows, gains_all, input_attn, joint_weight, joint_lifted, cosine, sine_part),
        [
            ((row_count, model_width), BF16),
            ((row_count, 3 * rank), BF16),
            ((row_count, heads_width), BF16),
            ((row_count, kv_width), BF16),
        ],
        place,
    )
    joint_key_value = lax.all_gather(joint_part, "mp", axis=0, tiled=False)
    key_rows, flat_heads, branch_part = simple_pass(
        attend_kernel,
        "attend_pass",
        (query_rows, joint_key_value, cosine, sine_part, row_segment, column_segment)
        + (out_weight, out_down),
        [
            ((row_count, HEAD_SIZE), BF16),
            ((row_count, heads_width), BF16),
            ((row_count, model_width + rank), BF16),
        ],
    )
    chunks = gather_far(near, flat_heads, height)
    branch_sum = lax.psum(branch_part, "mp")
    rank_out = branch_sum[:, model_width:]

    hidden_state, normed_own = simple_pass(
        second_kernel,
        "second_pass",
        (tok_rows, branch_sum, model_all, gains_all, input_ffn),
        [((row_count, model_width), F32), ((row_count, model_width + 2 * rank), BF16)],
        place,
    )
    (grad_own,) = simple_pass(
        grad_kernel,
        "grad_pass",
        (grad_ffn, model_all),
        [((row_count, model_width + rank), BF16)],
    )
    grad_pair = (grad_own, partner(grad_own))
    grad_t = turn_pass(*grad_pair)
    normed_pair = (after(normed_own, grad_t), partner(normed_own))

    acts, sums = [], ()
    size = CHUNKS // GROUPS
    for group in range(GROUPS):
        *act, own_sum, other_sum = gate_pass(
            normed_pair,
            grad_pair,
            chunks[group * size : (group + 1) * size],
            slice_width,
            rank_part,
            sums,
            group == GROUPS - 1,
        )
        acts += [[(a, n) for a in act] for n in range(size)]
        sums = (own_sum, other_sum)
    normed_t = turn_pass(after(normed_own, sums[1]), normed_pair[1])
    grad_norm_ready = sum_pass(sums[0], partner(sums[1]))
    first_space = partner(grad_norm_ready[:16])
    grad_norm_sum = lax.psum(grad_norm_ready, "mp")

    def weight_share(items, hold, held=(), start=0, count=CHUNKS):
        for c in range(CHUNKS):
            gated, grad_gate, grad_upper = acts[c]
            if hold is not None:
                grad_gate = (after(grad_gate[0], hold), grad_gate[1])
            held = weight_pass(
                core,
                normed_t,
                grad_t,
                slice_width,
                rank_part,
                (grad_gate, grad_upper, gated),
                chunk,
                start + c,
                count,
                items,
                held,
            )
        return held

    sends, held, last_sent = (), (), ()
    if dp_count == 4:
        sends = weight_share(
            [(3, 0, (), BF16), (3, 1, (), BF16)], first_space, count=2 * CHUNKS
        )
        sends = weight_share(
            [(1, 0, (), BF16), (2, 1, (), BF16)], first_space, sends, CHUNKS, 2 * CHUNKS
        )
        near_one, near_two = trade(sends[0], "dp", 1), trade(sends[1], "dp", 2)
        held = weight_share([(1, 1, (), BF16), (2, 0, (), BF16)], sends[0])

    acts_down = [(after(a[0][0], first_space, *sends), a[0][1]) for a in acts]
    ffn_own, ffn_given = down_pass(acts_down, chunks, slice_width, rank_part)
    ffn_ready = sum_pass(ffn_own, partner(ffn_given))
    grad_norm_sum = after(grad_norm_sum, ffn_ready)
    if dp_count == 4:
        grad_norm_sum = after(grad_norm_sum, *held)
    half_rows = row_count // 2
    ffn_first, ffn_last = simple_pass(
        early_kernel,
        "early_pass",
        (ffn_ready,),
        [((half_rows, model_width + 2 * rank), BF16), ((half_rows, model_width), BF16)],
    )
    ffn_first = after(ffn_first, grad_norm_sum)
    grad_norm_sum = after(grad_norm_sum, partner(ffn_first))
    ffn_first = lax.psum(ffn_first, "mp")
    rank_down = jnp.concatenate(
        [ffn_first[:, model_width : model_width + rank], ffn_first[:, model_width + rank :]],
        axis=0,
    )

    grad_hidden, grad_branch, grad_rank_gu, grad_rank_out, grad_query, grad_joint, gain_two = (
        simple_pass(
            attend_back_kernel,
            "attend_back_pass",
            (grad_norm_sum, hidden_state, gains_all, input_ffn, grad_ffn, model_all)
            + (out_weight, out_down, query_rows, key_rows, joint_key_value)
            + (cosine, sine_part, row_segment, column_segment),
            [
                ((row_count, model_width), F32),
                ((row_count, model_width), BF16),
                ((row_count, 2 * rank), BF16),
                ((row_count, rank), BF16),
                ((row_count, heads_width), BF16),
                ((mp_count, row_count, kv_width), BF16),
                ((8, model_width), F32),
            ],
            place,
            LONG,
        )
    )
    grad_kv = lax.psum_scatter(after(grad_joint, ffn_first), "mp", scatter_dimension=0, tiled=False)
    if dp_count == 4:
        near_one, near_two = after(near_one, grad_query), after(near_two, grad_query)
        last_one = sum_pass(held[0], (near_two, 0))
        last_two = sum_pass(held[1], (near_one, 0))
        last_sent = (trade(last_one, "dp", 1), trade(last_two, "dp", 2))
    (grad_norm_part,) = simple_pass(
        project_back_kernel,
        "project_back_pass",
        (grad_query, grad_kv, joint_weight, joint_lifted),
        [((row_count, model_width + 3 * rank), BF16)],
        place,
    )
    ffn_last = after(ffn_last, ffn_first)
    grad_norm_one, ffn_last = lax.psum((grad_norm_part, ffn_last), "mp")
    grad_rows, grad_rank_qkv, gain_one = simple_pass(
        first_back_kernel,
        "first_back_pass",
        (grad_norm_one, tok_rows, gains_all, input_attn, grad_hidden),
        [
            ((row_count, model_width), BF16),
            ((row_count, 3 * rank), BF16),
            ((8, model_width), F32),
        ],
        place,
        LONG,
    )
    grad_input = relative(grad_rows, 1, dp_id, dp_count)

    quarter = part_width * kv_width // heads_width
    small = rank_part * kv_width // heads_width
    blocks = share_columns // heads_width
    mp_rows = 2 * blocks * rank_part + 2 * rank // heads_width * share_rows
    rest_rows = 2 * rank_part + small + mp_rows
    base_rows = 2 * part_width + quarter
    shares, shares_given, *rest = simple_pass(
        functools.partial(shares_kernel, dp_count, share_rows, share_columns),
        "shares_pass",
        (after(normalized_rows, grad_norm_part), grad_query, grad_kv, rank_rows, grad_branch, flat_heads)
        + (grad_rank_out, rank_out, normed_own, grad_rank_gu, rank_down, grad_ffn),
        [
            ((dp_count, base_rows, heads_width), BF16),
            ((dp_count, base_rows, heads_width), BF16),
            *[((rest_rows, heads_width), BF16)] * dp_count,
        ],
        place,
    )
    own = ()
    if dp_count == 4:
        own = weight_share([(0, 0, (), BF16), (0, 1, (), BF16)], grad_norm_part)
    shares_given = after(shares_given, *own)
    if dp_count == 4:
        mine = [(own[0], 0), (near_one, CHUNKS), (last_sent[1], 0)]
        theirs = sum_pass(own[1], (near_two, 1), after(last_sent[0], last_sent[1]))
        grad_rank_qkv = after(grad_rank_qkv, theirs)
        theirs = partner(theirs)
    else:
        by_index = [
            weight_share([(p, 0, (), BF16), (p, 1, (), BF16)], None)
            for p in range(dp_count)
        ]
        mine = [(scatter_dp([b[0] for b in by_index]), 0)]
        theirs = partner(scatter_dp([b[1] for b in by_index]).astype(BF16))
    grad_w_gateup, grad_w_down, grad_lora_gateup, grad_lora_hidden = finish_pass(
        core, mine, theirs, part_width, rank_part, hidden
    )

    ffn_sum = jnp.concatenate([ffn_first[:, :model_width], ffn_last], axis=0)
    output = hidden_state + ffn_sum.astype(F32) + dot(rank_down, model_all[1])
    result_rows = relative(output.astype(BF16), 1, dp_id, dp_count)
    shares_got = after(partner(shares_given), grad_rank_qkv)

    def shared(p, dtype, *more):
        return add_pass(dtype, (shares, p), (shares_got, p), *more)

    if dp_count == 4:
        near_share = trade(shared(3, BF16), "dp", 1)
        near_rest = after(trade(after(rest[3], *own), "dp", 2), grad_rank_qkv)
        share_one, rest_two = trade(shared(1, BF16), "dp", 1), trade(after(rest[2], near_rest), "dp", 2)
        share_two = trade(shared(2, BF16, near_share), "dp", 2)
        rest_one = trade(add_pass(BF16, rest[1], near_rest), "dp", 1)
        share_own = shared(0, F32, after(share_one, grad_w_down), share_two)
        rest_own = add_pass(F32, rest[0], after(rest_one, grad_rank_qkv), rest_two)
    else:
        share_own = scatter_dp([shared(p, BF16) for p in range(dp_count)])
        rest_own = scatter_dp([rest[p] for p in range(dp_count)])

    share_own, rest_own = after(share_own, grad_rank_qkv), after(rest_own, grad_rank_qkv)

    def unfolded(block, width, heights):
        rows = heights
        columns = [block[at : at + rows, :width] for at in range(0, block.shape[0], rows)]
        return jnp.concatenate(columns, axis=1)

    def side_by_side(block, width):
        return jnp.concatenate(
            [block[:, at : at + width] for at in range(0, heads_width, width)], axis=0
        )

    grad_w_query = share_own[:part_width]
    grad_w_keyval = side_by_side(share_own[part_width : part_width + quarter], kv_width)
    grad_w_output = share_own[part_width + quarter :].T
    at = rank_part
    grad_lora_query = rest_own[:at][None]
    grad_lora_keyval = side_by_side(rest_own[at : at + small], kv_width)[None]
    at += small
    grad_lora_out = rest_own[at : at + rank_part][None]
    at += rank_part
    gathered = lax.all_gather(rest_own[at:].astype(BF16), "mp", axis=0, tiled=False).astype(F32)
    model_own, at = [], 0
    for _ in range(2):
        block = gathered[:, at : at + blocks * rank_part].reshape(-1, heads_width)
        model_own.append(unfolded(block, heads_width, rank_part))
        at += blocks * rank_part
    grad_lora_model = jnp.stack(model_own)[None]
    ffn_in_own = jnp.concatenate(
        [unfolded(gathered[z, at:], heads_width, share_rows) for z in range(mp_count)], axis=0
    )

    def by_dp(block):
        return block.reshape(dp_count, block.shape[0] // dp_count, block.shape[1])

    gain_grads = jnp.stack([gain_one[0], gain_two[0]]).astype(BF16)
    gain_grads = gain_grads.reshape(2, dp_count, slice_width)
    grad_input_attn = by_dp(product(normalized_rows, grad_rank_qkv, 0, 0).astype(BF16))
    attn_in_own = scatter_dp(
        [
            jnp.concatenate(
                [grad_input_attn[p], pad_rows(gain_grads[:, p], 16, 3 * rank)], axis=0
            )
            for p in range(dp_count)
        ]
    )
    gain_grads = attn_in_own[slice_width : slice_width + 2, :slice_width]
    gain_first, gain_second = gain_grads[:, :part_width], gain_grads[:, part_width:]
    grad_w_gains = jnp.where(first_core, gain_first, gain_second) + partner(
        jnp.where(first_core, gain_second, gain_first)
    )
    input_own = jnp.concatenate([attn_in_own[:slice_width], ffn_in_own], axis=1)
    grad_lora_in = jnp.stack([input_own[:, k * rank : (k + 1) * rank] for k in range(5)])[None]

    mixed_rows = jnp.where(keep_own, result_rows, partner(result_rows))
    grad_tokens = jnp.where(keep_own, grad_input, partner(grad_input))
    return (
        mixed_rows,
        grad_tokens,
        grad_w_query,
        grad_w_keyval,
        grad_w_output,
        grad_w_gateup,
        grad_w_down,
        grad_w_gains,
        grad_lora_in,
        grad_lora_query,
        grad_lora_keyval,
        grad_lora_out,
        grad_lora_hidden,
        grad_lora_model,
        grad_lora_gateup,
    )


def solution(mesh):
    return jax.shard_map(
        local,
        mesh=mesh,
        in_specs=(
            P(("dp", "depth"), None),
            P(("dp", "depth"), None),
            P("dp", None, None),
            P("dp", None),
            P(("dp", "depth"), "mp"),
            P(("dp", "depth"), "mp"),
            P("mp", ("dp", "depth")),
            P(None, ("dp", "depth"), "mp"),
            P("mp", ("dp", "depth")),
            P(None, ("dp", "depth")),
            P("depth", None, "dp", None),
            P("depth", "dp", "mp"),
            P("depth", "dp", "mp"),
            P("depth", "dp", "mp"),
            P("depth", "dp", "mp"),
            P("depth", None, "dp", None),
            P("depth", None, "dp", "mp"),
        ),
        out_specs=(
            P(("dp", "depth"), None),
            P(("dp", "depth"), None),
            P(("dp", "depth"), "mp"),
            P(("dp", "depth"), "mp"),
            P("mp", ("dp", "depth")),
            P(None, ("dp", "depth"), "mp"),
            P("mp", ("dp", "depth")),
            P(None, ("dp", "depth")),
            P("depth", None, "dp", None),
            P("depth", "dp", "mp"),
            P("depth", "dp", "mp"),
            P("depth", "dp", "mp"),
            P("depth", "dp", "mp"),
            P("depth", None, "dp", None),
            P("depth", None, "dp", "mp"),
        ),
        check_vma=False,
    )
```

```python
import functools

import jax
import jax.numpy as jnp
from jax import lax
from jax.experimental import pallas as pl
from jax.experimental.pallas import tpu as pltpu
from jax.sharding import PartitionSpec as P

HEAD_SIZE = 256


EPS = 1e-06
THETA = 10000.0
NEGATIVE = -1e30


def product(left_op, right_op, left_dim, right_dim):
    return lax.dot_general(
        left_op,
        right_op,
        (((left_dim,), (right_dim,)), ((), ())),
        preferred_element_type=jnp.float32,
    )


def layout(seq_lens, row_count):
    seq_ends = jnp.cumsum(seq_lens)
    places = jnp.arange(row_count, dtype=jnp.int32)
    passed = (places[:, None] >= seq_ends[None, :]).astype(jnp.int32)
    segment = jnp.sum(passed, axis=1)
    starts = jnp.sum(passed * seq_lens[None, :], axis=1)
    valid_rows = (places < seq_ends[-1]).astype(jnp.float32)
    within = (places - starts).astype(jnp.float32)
    return (places, segment, within, valid_rows)


def rotary(within, head_width):
    half_width = head_width // 2
    frequency = THETA ** (-2.0 * jnp.arange(half_width, dtype=jnp.float32) / head_width)
    angles = within[:, None] * frequency[None, :]
    return (jnp.cos(angles), jnp.sin(angles))


def rotate(vector, cosine, sine_part):
    half_width = vector.shape[-1] // 2
    former = vector[..., :half_width]
    latter = vector[..., half_width:]
    return jnp.concatenate(
        [former * cosine - latter * sine_part, latter * cosine + former * sine_part], axis=-1
    )


def rotate_back(vector, cosine, sine_part):
    half_width = vector.shape[-1] // 2
    former = vector[..., :half_width]
    latter = vector[..., half_width:]
    return jnp.concatenate(
        [former * cosine + latter * sine_part, latter * cosine - former * sine_part], axis=-1
    )


def rms_forward(values, gain_row):
    inverse = lax.rsqrt(jnp.mean(values * values, axis=-1, keepdims=True) + EPS)
    return (values * inverse * gain_row, inverse)


def rms_backward(values, inverse, gain_row, grad_norm):
    weighted = grad_norm * gain_row
    grad_values = inverse * weighted - values * inverse**3 * jnp.mean(
        weighted * values, axis=-1, keepdims=True
    )
    grad_gain = jnp.sum(grad_norm * values * inverse, axis=0)
    return (grad_values, grad_gain)


def gelu_tanh(values):
    return jax.nn.gelu(values, approximate=True)


def block_mask(places, segment):
    return (segment[:, None] == segment[None, :]) & (places[None, :] <= places[:, None])


CHUNKS = 4
GROUPS = 2
BF16 = jnp.bfloat16
F32 = jnp.float32


def trade(block, axis, mask):
    count = lax.axis_size(axis)
    return lax.ppermute(block, axis, [(i, i ^ mask) for i in range(count)])


def gather_dp(piece, *hold):
    count = lax.axis_size("dp")
    if count == 4:
        half = piece.shape[0] // 2
        from_one = trade(piece, "dp", 1)
        from_two = trade(piece, "dp", 2)
        far = jnp.concatenate(
            [
                trade(after(from_two[:half], *hold), "dp", 1),
                trade(after(from_one[half:], *hold), "dp", 2),
            ],
            axis=0,
        )
        return [piece, from_one, from_two, far]
    pieces, mask = [piece], 1
    while mask < count:
        pieces = pieces + [trade(held, "dp", mask) for held in pieces]
        mask *= 2
    return pieces


def gather_pair(one, two, *early):
    count = lax.axis_size("dp")
    if count == 4:
        first_one, first_two = trade(one, "dp", 1), trade(one, "dp", 2)
        second_one, second_two = trade(two, "dp", 1), trade(two, "dp", 2)
        far = trade(after(first_two, *early), "dp", 1), trade(second_one, "dp", 2)
        pieces = [(one, two), (first_one, second_one), (first_two, second_two), far]
        return pieces, (first_two, second_one)
    ones, twos = gather_dp(one), gather_dp(two)
    return list(zip(ones, twos)), (ones[-1], twos[-1])


def gather_near(bundle):
    count = lax.axis_size("dp")
    pieces, mask = [bundle], 1
    while mask < count:
        first = pieces if count != 4 else pieces[:1]
        pieces = pieces + [trade(held, "dp", mask) for held in first]
        mask *= 2
    return pieces


def gather_far(near, hold, height):
    chunks = [[((b, c), (b, CHUNKS + c)) for b in near] for c in range(CHUNKS)]
    if lax.axis_size("dp") == 4:
        size = CHUNKS // GROUPS
        for group in range(GROUPS):
            rows = (size * group * height, size * (group + 1) * height)
            one = lax.slice_in_dim(after(near[2], hold), *rows, axis=0)
            two = lax.slice_in_dim(
                after(near[1], hold), *[CHUNKS * height + r for r in rows], axis=0
            )
            one, two = trade(one, "dp", 1), trade(two, "dp", 2)
            for n in range(size):
                chunks[group * size + n].append(((one, n), (two, n)))
    return chunks


def scatter_dp(parts, *last):
    count = lax.axis_size("dp")
    if count == 4:
        half = parts[3].shape[0] // 2
        near_one = trade(parts[3][:half], "dp", 1)
        near_two = trade(parts[3][half:], "dp", 2)
        for_two = jnp.concatenate([add_rounded(parts[2][:half], near_one), parts[2][half:]], axis=0)
        for_one = jnp.concatenate([parts[1][:half], add_rounded(parts[1][half:], near_two)], axis=0)
        got_one = trade(for_one, "dp", 1)
        got_two = after(trade(for_two, "dp", 2), *last)
        return parts[0].astype(F32) + got_one.astype(F32) + got_two.astype(F32)
    mask = count // 2
    while mask:
        parts = [
            add_rounded(parts[p], trade(parts[p + mask], "dp", mask)) for p in range(mask)
        ]
        mask //= 2
    return parts[0].astype(F32)


def add_rounded(one, two):
    return (one.astype(F32) + two.astype(F32)).astype(BF16)


def relative(block, axis, index, count):
    width = block.shape[axis] // count
    mask = 1
    while mask < count:
        flipped = jnp.concatenate(
            [
                lax.slice_in_dim(block, (b ^ mask) * width, ((b ^ mask) + 1) * width, axis=axis)
                for b in range(count)
            ],
            axis=axis,
        )
        block = jnp.where((index & mask) > 0, flipped, block)
        mask *= 2
    return block


VMEM_LIMIT = 50 * 1024 * 1024
GELU_SCALE = 0.7978845608028654
LONG = pl.CostEstimate(flops=10**14, bytes_accessed=1, transcendentals=0)
BRIEF = pl.CostEstimate(flops=1, bytes_accessed=1, transcendentals=0)


def after(block, *earlier):
    return lax.optimization_barrier((block, *earlier))[0]


def whole_spec(shape):
    return pl.BlockSpec(shape, lambda *_: (0,) * len(shape), pipeline_mode=pl.Buffered(1))


def params():
    return pltpu.CompilerParams(vmem_limit_bytes=VMEM_LIMIT)


def nn(left_op, right_op):
    return product(left_op, right_op, 1, 0)


def nt(left_op, right_op):
    return product(left_op, right_op, 1, 1)


def late_split(height):
    return -(-height // 48) * 16


def pack_kernel(part, rank_part, rank, mp, *refs):
    query, key_value, output, gains, query_up, key_value_up, output_down = refs[:7]
    inputs, input_share, model_share, attn, one, late = refs[7:]
    heads = query.shape[1]
    one[...] = jnp.zeros_like(one)
    one[:part, :heads] = query[...]
    one[:part, heads:] = key_value[...]
    one[part : 2 * part, :heads] = output[...].T
    one[2 * part : 2 * part + 2, :part] = gains[...]
    first = 2 * part + 16
    one[first : first + rank_part, :heads] = query_up[0]
    one[first : first + rank_part, heads:] = key_value_up[0]
    one[first + rank_part :, :heads] = output_down[0]
    wide = inputs.shape[2]
    attn[wide:, :] = jnp.zeros_like(attn[wide:, :])
    for k in range(3):
        attn[:wide, k * rank : (k + 1) * rank] = inputs[0, k]
    row = 0
    for at in range(0, model_share.shape[3], rank):
        for k in range(2):
            late[row : row + rank_part, :] = model_share[0, k, :, at : at + rank]
            row += rank_part
    height = input_share.shape[2]
    for k in range(2):
        late[row : row + height, :] = input_share[0, 3 + k]
        row += height
    split = late_split(row)
    for k in range(3):
        rows = min(split, row - k * split)
        attn[wide : wide + rows, k * rank : (k + 1) * rank] = late[
            k * split : k * split + rows, :
        ]


def pack_pass(mp, arrays, mp_count, rank):
    query, key_value, output, gains, query_up, _, _, inputs, model_up = arrays
    part, rank_part = query.shape[0], query_up.shape[1]
    slice_width, columns = inputs.shape[2], model_up.shape[3] // mp_count
    rows = slice_width // mp_count
    late_rows = 2 * rank_part * (columns // rank) + 2 * rows
    shapes = [
        (slice_width + late_split(late_rows), 3 * rank),
        (2 * part + 16 + 2 * rank_part, query.shape[1] + key_value.shape[1]),
    ]

    def whole(shape):
        return pl.BlockSpec(shape, lambda s, mp: (0,) * len(shape))

    return pl.pallas_call(
        functools.partial(pack_kernel, part, rank_part, rank),
        grid_spec=pltpu.PrefetchScalarGridSpec(
            num_scalar_prefetch=1,
            grid=(1,),
            in_specs=[whole(a.shape) for a in arrays[:8]]
            + [
                pl.BlockSpec((1, 5, rows, rank), lambda s, mp: (0, 0, mp[0], 0)),
                pl.BlockSpec((1, 2, rank_part, columns), lambda s, mp: (0, 0, 0, mp[0])),
            ],
            out_specs=[whole(s) for s in shapes],
            scratch_shapes=[pltpu.VMEM((late_rows, rank), BF16)],
        ),
        out_shape=[jax.ShapeDtypeStruct(s, BF16) for s in shapes],
        compiler_params=params(),
        cost_estimate=BRIEF,
        name="pack_pass",
    )(mp, *arrays[:7], inputs, inputs, model_up)


def unpack_kernel(count, part, rank_part, *refs):
    pieces, (shared, inputs, late, lifted, out_down) = refs[: 2 * count], refs[2 * count :]
    rows = shared.shape[0] // count
    wide, rank = 2 * part, late.shape[2]
    heads = out_down.shape[1]
    height = late.shape[1]
    split = late_split(height)
    for p in range(count):
        attn, one = pieces[2 * p : 2 * p + 2]
        shared[p * rows : (p + 1) * rows, :] = one[:rows, :]
        here = slice(p * rank_part, (p + 1) * rank_part)
        lifted[here, :] = one[rows : rows + rank_part, :]
        out_down[here, :] = one[rows + rank_part :, :heads]
        inputs[p * wide : (p + 1) * wide, :] = attn[:wide, :]
        for k in range(3):
            number = min(split, height - k * split)
            late[p, k * split : k * split + number, :] = attn[
                wide : wide + number, k * rank : (k + 1) * rank
            ]


def unpack_pass(pieces, part, rank_part, rank, rows, columns, heads):
    count = len(pieces)
    joint = pieces[0][1].shape[1]
    late_rows = 2 * rank_part * (columns // rank) + 2 * rows
    flat = [b for pair in pieces for b in pair]
    shapes = [
        (count * (2 * part + 16), joint),
        (count * 2 * part, 3 * rank),
        (count, late_rows, rank),
        (count * rank_part, joint),
        (count * rank_part, heads),
    ]
    return pl.pallas_call(
        functools.partial(unpack_kernel, count, part, rank_part),
        grid=(1,),
        in_specs=[whole_spec(b.shape) for b in flat],
        out_specs=[whole_spec(s) for s in shapes],
        out_shape=[jax.ShapeDtypeStruct(s, BF16) for s in shapes],
        compiler_params=params(),
        cost_estimate=BRIEF,
        name="unpack_pass",
    )(*flat)


def shared_kernel(count, part, core, own, other, joint, output, gains):
    rows = own.shape[0] // count
    heads = output.shape[1]
    gains[...] = jnp.zeros_like(gains)
    for e in range(2):

        @pl.when(core[0] == e)
        def _(e=e):
            for side, source in ((e, own), (1 - e, other)):
                for p in range(count):
                    here = slice((2 * p + side) * part, (2 * p + side + 1) * part)
                    first = p * rows
                    joint[here, :] = source[first : first + part, :]
                    output[here, :] = source[first + part : first + 2 * part, :heads]
                    gains[:2, here] = source[first + 2 * part : first + 2 * part + 2, :part]


def shared_pass(core, own, other, count, part, heads):
    shapes = [(count * 2 * part, own.shape[1]), (count * 2 * part, heads), (16, count * 2 * part)]
    return pl.pallas_call(
        functools.partial(shared_kernel, count, part),
        grid=(1,),
        in_specs=[pl.BlockSpec(memory_space=pltpu.SMEM)] + [whole_spec(own.shape)] * 2,
        out_specs=[whole_spec(s) for s in shapes],
        out_shape=[jax.ShapeDtypeStruct(s, BF16) for s in shapes],
        compiler_params=params(),
        cost_estimate=BRIEF,
        name="shared_pass",
    )(core, own, other)


def late_kernel(rank_part, rows, count, late, model, inputs):
    rank = late.shape[3]
    for p in range(count):
        for n in range(model.shape[2] // rank):
            for k in range(2):
                first = (2 * n + k) * rank_part
                model[k, p * rank_part : (p + 1) * rank_part, n * rank : (n + 1) * rank] = late[
                    0, p, first : first + rank_part, :
                ]
        first = 2 * rank_part * (model.shape[2] // rank)
        for k in range(2):
            inputs[p, 0, :, k * rank : (k + 1) * rank] = late[
                0, p, first + k * rows : first + (k + 1) * rows, :
            ]


def late_pass(late, rows, columns, rank_part):
    mp_count, count, height, rank = late.shape
    model, inputs = pl.pallas_call(
        functools.partial(late_kernel, rank_part, rows, count),
        grid=(mp_count,),
        in_specs=[pl.BlockSpec((1, count, height, rank), lambda z: (z, 0, 0, 0))],
        out_specs=[
            pl.BlockSpec((2, rank, columns), lambda z: (0, 0, z)),
            pl.BlockSpec((count, 1, rows, 2 * rank), lambda z: (0, z, 0, 0)),
        ],
        out_shape=[
            jax.ShapeDtypeStruct((2, rank, mp_count * columns), BF16),
            jax.ShapeDtypeStruct((count, mp_count, rows, 2 * rank), BF16),
        ],
        compiler_params=params(),
        cost_estimate=BRIEF,
        name="late_pass",
    )(late)
    return model, inputs.reshape(count * mp_count * rows, 2 * rank)


def ffn_blocks(arrays, chunk, side):
    gate_up, down, lora_gate_up, lora_hidden = arrays

    def column(s, core):
        return side(core[0]) * CHUNKS + s

    return [
        pl.BlockSpec((2, gate_up.shape[1], chunk), lambda s, core: (0, 0, column(s, core))),
        pl.BlockSpec((chunk, down.shape[1]), lambda s, core: (column(s, core), 0)),
        pl.BlockSpec(
            (1, 2, lora_gate_up.shape[2], chunk), lambda s, core: (0, 0, 0, column(s, core))
        ),
        pl.BlockSpec((1, lora_hidden.shape[1], chunk), lambda s, core: (0, 0, column(s, core))),
    ]


def ffn_rows(gate_up, down, lora_gate_up, lora_hidden):
    return [
        gate_up[0],
        gate_up[1],
        down[...].T,
        jnp.concatenate([lora_gate_up[0, 0], lora_gate_up[0, 1], lora_hidden[0]], axis=0),
    ]


def give_kernel(core, gate_up, down, lora_gate_up, lora_hidden, given):
    first = 0
    for block in ffn_rows(gate_up, down, lora_gate_up, lora_hidden):
        given[first : first + block.shape[0], :] = block
        first += block.shape[0]


def give_pass(core, arrays, chunk):
    part, rank_part = arrays[0].shape[1], arrays[3].shape[1]
    height = 3 * (part + rank_part)
    return pl.pallas_call(
        give_kernel,
        grid_spec=pltpu.PrefetchScalarGridSpec(
            num_scalar_prefetch=1,
            grid=(CHUNKS,),
            in_specs=ffn_blocks(arrays, chunk, lambda me: 1 - me),
            out_specs=pl.BlockSpec((height, chunk), lambda s, core: (s, 0)),
        ),
        out_shape=jax.ShapeDtypeStruct((CHUNKS * height, chunk), BF16),
        compiler_params=params(),
        cost_estimate=BRIEF,
        name="give_pass",
    )(core, *arrays)


def bundle_kernel(part, core, gate_up, down, lora_gate_up, lora_hidden, taken, bundle):
    own_first = core[0] == 0
    one, two = bundle.at[0], bundle.at[1]
    gate, upper, lower, lifted = ffn_rows(gate_up, down, lora_gate_up, lora_hidden)

    def pair(own, start):
        other = taken[start : start + part, :]
        return jnp.where(own_first, own, other), jnp.where(own_first, other, own)

    one[:part, :], one[part : 2 * part, :] = pair(gate, 0)
    two[:part, :], two[part : 2 * part, :] = pair(upper, part)
    one[2 * part : 3 * part, :], two[2 * part : 3 * part, :] = pair(lower, 2 * part)
    one[3 * part :, :] = lifted
    two[3 * part :, :] = taken[3 * part :, :]


def bundle_pass(core, arrays, taken, chunk):
    part = arrays[0].shape[1]
    height = taken.shape[0] // CHUNKS
    out = pl.pallas_call(
        functools.partial(bundle_kernel, part),
        grid_spec=pltpu.PrefetchScalarGridSpec(
            num_scalar_prefetch=1,
            grid=(CHUNKS,),
            in_specs=ffn_blocks(arrays, chunk, lambda me: me)
            + [pl.BlockSpec((height, chunk), lambda s, core: (s, 0))],
            out_specs=pl.BlockSpec((2, height, chunk), lambda s, core: (0, s, 0)),
        ),
        out_shape=jax.ShapeDtypeStruct((2, CHUNKS * height, chunk), BF16),
        compiler_params=params(),
        cost_estimate=BRIEF,
        name="bundle_pass",
    )(core, *arrays, taken)
    return out.reshape(2 * CHUNKS * height, chunk)


def simple_pass(kernel, name, inputs, shapes, scalars=None, cost=BRIEF):
    specs = [whole_spec(a.shape) for a in inputs]
    if scalars is not None:
        inputs = (scalars, *inputs)
        specs = [pl.BlockSpec(memory_space=pltpu.SMEM)] + specs
    return pl.pallas_call(
        kernel,
        grid=(1,),
        in_specs=specs,
        out_specs=[whole_spec(shape) for shape, _ in shapes],
        out_shape=[jax.ShapeDtypeStruct(shape, dtype) for shape, dtype in shapes],
        compiler_params=params(),
        cost_estimate=cost,
        name=name,
    )(*inputs)


def tn(left_op, right_op):
    return product(left_op, right_op, 0, 0)


def rank_order(block, rank, shift):
    row = lax.broadcasted_iota(jnp.int32, (rank, rank), 0)
    column = lax.broadcasted_iota(jnp.int32, (rank, rank), 1)
    swap = (jnp.bitwise_xor(row, shift) == column).astype(F32).astype(BF16)
    parts = [
        nn(block[:, at : at + rank], swap).astype(BF16)
        for at in range(0, block.shape[1], rank)
    ]
    return jnp.concatenate(parts, axis=1)


def inverse_rms(values):
    return lax.rsqrt(jnp.mean(values * values, axis=-1, keepdims=True) + EPS)


def project_kernel(place, rows, gains, inputs, joint, lifted, cosine, sine, *outs):
    normed, ranks, query, joint_part = outs
    heads = query.shape[1]
    rank = inputs.shape[1] // 3
    values = rows[...].astype(F32)
    gain = gains[0:1, :].astype(F32)
    normed[...] = (values * inverse_rms(values) * gain).astype(BF16)
    ranks[...] = rank_order(nn(normed[...], inputs[...]).astype(BF16), rank, place[0])
    raw = nn(normed[...], joint[...])
    query_raw = raw[:, :heads] + nn(ranks[:, :rank], lifted[:, :heads])
    for at in range(0, heads, HEAD_SIZE):
        here = slice(at, at + HEAD_SIZE)
        query[:, here] = rotate(query_raw[:, here], cosine[...], sine[...]).astype(BF16)
    pick = jnp.where(place[1] == 1, ranks[:, rank : 2 * rank], ranks[:, 2 * rank :])
    joint_part[...] = (raw[:, heads:] + nn(pick, lifted[:, heads:])).astype(BF16)


def beside(blocks):
    return jnp.concatenate([blocks[n] for n in range(blocks.shape[0])], axis=1)


def head_probs(query, keys, rows_segment, columns_segment):
    count = query.shape[0]
    scores = nt(query, keys) * HEAD_SIZE ** (-0.5)
    row = lax.broadcasted_iota(jnp.int32, (count, count), 0)
    column = lax.broadcasted_iota(jnp.int32, (count, count), 1)
    allowed = (rows_segment == columns_segment) & (column <= row)
    scores = jnp.where(allowed, scores, NEGATIVE)
    powers = jnp.exp(scores - jnp.max(scores, axis=-1, keepdims=True))
    return powers / jnp.sum(powers, axis=-1, keepdims=True)


def attend_kernel(query, joint, cosine, sine, row_seg, column_seg, output, down, *outs):
    keys, flat, branch = outs
    width = output.shape[0]
    both = beside(joint)
    keys[...] = rotate(both[:, :HEAD_SIZE].astype(F32), cosine[...], sine[...]).astype(BF16)
    for at in range(0, flat.shape[1], HEAD_SIZE):
        here = slice(at, at + HEAD_SIZE)
        probs = head_probs(query[:, here], keys[...], row_seg[...], column_seg[...])
        flat[:, here] = nn(probs.astype(BF16), both[:, HEAD_SIZE:]).astype(BF16)
    branch[:, :width] = nt(flat[...], output[...]).astype(BF16)
    branch[:, width:] = nt(flat[...], down[...]).astype(BF16)


def second_kernel(place, rows, branch, model, gains, inputs, hidden, normed):
    width = rows.shape[1]
    rank = model.shape[1]
    hidden[...] = (
        rows[...].astype(F32)
        + branch[:, :width].astype(F32)
        + nn(branch[:, width:], model[0])
    )
    values = hidden[...]
    gain = gains[1:2, :].astype(F32)
    normed[:, :width] = (values * inverse_rms(values) * gain).astype(BF16)
    normed[:, width:] = rank_order(
        nn(normed[:, :width], inputs[...]).astype(BF16), rank, place[0]
    )


def early_kernel(block, early, late):
    rows, columns = early.shape[0], block.shape[1]
    early[:, :columns] = block[:rows, :]
    early[:, columns:] = block[rows:, columns - (early.shape[1] - columns) :]
    late[...] = block[rows:, : late.shape[1]]


def grad_kernel(rows, model, grad):
    width = rows.shape[1]
    grad[:, :width] = rows[...]
    grad[:, width:] = nt(rows[...], model[1]).astype(BF16)


def norm_back(values, gain, grad_norm):
    inverse = inverse_rms(values)
    weighted = grad_norm * gain
    grad_values = inverse * weighted - values * inverse**3 * jnp.mean(
        weighted * values, axis=-1, keepdims=True
    )
    return grad_values, jnp.sum(grad_norm * values * inverse, axis=0, keepdims=True)


def attend_back_kernel(place, summed, hidden, gains, inputs, grad_ffn, model, *refs):
    output, down, query, keys, joint, cosine, sine, row_seg, column_seg = refs[:9]
    grad_hidden, branch, rank_gu, rank_out, grad_query, grad_joint, grad_gain = refs[9:]
    width = hidden.shape[1]
    rank = down.shape[0]
    factor = HEAD_SIZE ** (-0.5)
    rank_gu[...] = rank_order(summed[:, width:], rank, place[0])
    grad_norm = summed[:, :width].astype(F32) + nt(rank_gu[...], inputs[...])
    values, gain_row = norm_back(hidden[...], gains[1:2, :].astype(F32), grad_norm)
    grad_gain[...] = jnp.broadcast_to(gain_row, grad_gain.shape)
    grad_hidden[...] = values + grad_ffn[...].astype(F32)
    branch[...] = grad_hidden[...].astype(BF16)
    rank_out[...] = nt(branch[...], model[0]).astype(BF16)
    grad_flat = (nn(branch[...], output[...]) + nn(rank_out[...], down[...])).astype(BF16)
    values_here = beside(joint)[:, HEAD_SIZE:]
    grad_keys = grad_values = 0.0
    for at in range(0, query.shape[1], HEAD_SIZE):
        here = slice(at, at + HEAD_SIZE)
        probs = head_probs(query[:, here], keys[...], row_seg[...], column_seg[...])
        grad_probs = nt(grad_flat[:, here], values_here)
        grad_values += tn(probs.astype(BF16), grad_flat[:, here])
        centre = jnp.sum(grad_probs * probs, axis=-1, keepdims=True)
        grad_scores = (probs * (grad_probs - centre)).astype(BF16)
        turned = rotate_back(nn(grad_scores, keys[...]) * factor, cosine[...], sine[...])
        grad_query[:, here] = turned.astype(BF16)
        grad_keys += tn(grad_scores, query[:, here]) * factor
    both = jnp.concatenate([rotate_back(grad_keys, cosine[...], sine[...]), grad_values], axis=1)
    kv = grad_joint.shape[2]
    for n in range(grad_joint.shape[0]):
        grad_joint[n] = both[:, n * kv : (n + 1) * kv].astype(BF16)


def project_back_kernel(place, grad_query, grad_kv, joint, lifted, out):
    heads = grad_query.shape[1]
    width, rank = joint.shape[0], lifted.shape[0]
    out[:, :width] = (
        nt(grad_query[...], joint[:, :heads]) + nt(grad_kv[...], joint[:, heads:])
    ).astype(BF16)
    pick = nt(grad_kv[...], lifted[:, heads:]).astype(BF16)
    none = jnp.zeros_like(pick)
    out[:, width : width + rank] = nt(grad_query[...], lifted[:, :heads]).astype(BF16)
    out[:, width + rank : width + 2 * rank] = jnp.where(place[1] == 1, pick, none)
    out[:, width + 2 * rank :] = jnp.where(place[1] == 1, none, pick)


def first_back_kernel(place, summed, rows, gains, inputs, grad_hidden, *outs):
    grad_rows, ranks, grad_gain = outs
    width = rows.shape[1]
    ranks[...] = rank_order(summed[:, width:], inputs.shape[1] // 3, place[0])
    grad_norm = summed[:, :width].astype(F32) + nt(ranks[...], inputs[...])
    values, gain_row = norm_back(rows[...].astype(F32), gains[0:1, :].astype(F32), grad_norm)
    grad_gain[...] = jnp.broadcast_to(gain_row, grad_gain.shape)
    grad_rows[...] = (values + grad_hidden[...]).astype(BF16)


def folded(block, width):
    blocks = [block[:, at : at + width] for at in range(0, block.shape[1], width)]
    return blocks[0] if len(blocks) == 1 else jnp.concatenate(blocks, axis=0)


def share_of(block, first, rows):
    total = jnp.zeros((rows, block.shape[1]), block.dtype)
    for at in range(0, block.shape[0], rows):
        total = jnp.where(first == at, block[at : at + rows], total)
    return total


def shares_kernel(count, share_rows, share_columns, place, normed, grad_query, grad_kv, ranks, branch, flat, *refs):
    rank_out, out_sum, second, rank_gu, down_sum, grad_ffn = refs[:6]
    mine, theirs, *rest = refs[6:]
    heads, kv = grad_query.shape[1], grad_kv.shape[1]
    width = normed.shape[1]
    rank = rank_out.shape[1]
    part, rank_part = width // (2 * count), rank // count
    own_first = place[2] == 0
    pick = jnp.where(place[1] == 1, ranks[:, rank : 2 * rank], ranks[:, 2 * rank : 3 * rank])

    def put(target, p, start, block):
        target[p, start : start + block.shape[0], :] = block.astype(BF16)
        return start + block.shape[0]

    def put_rest(p, start, block):
        rest[p][start : start + block.shape[0], :] = block.astype(BF16)
        return start + block.shape[0]

    lift_query = tn(ranks[:, :rank], grad_query[...])
    lift_kv = tn(pick, grad_kv[...])
    out_down = tn(rank_out[...], flat[...])
    for p in range(count):
        columns = slice(2 * p * part, 2 * (p + 1) * part)
        here = slice(p * rank_part, (p + 1) * rank_part)
        query = tn(normed[:, columns], grad_query[...])
        joint = tn(normed[:, columns], grad_kv[...])
        output = tn(branch[:, columns], flat[...])
        quarter = part * kv // heads
        for side, target in ((0, mine), (1, theirs)):
            first = [jnp.where(own_first, b[:part], b[part:]) for b in (query, joint, output)]
            other = [jnp.where(own_first, b[part:], b[:part]) for b in (query, joint, output)]
            blocks = first if side == 0 else other
            put(target, p, 0, blocks[0])
            for n in range(part // quarter):
                target[p, part : part + quarter, n * kv : (n + 1) * kv] = blocks[1][
                    n * quarter : (n + 1) * quarter
                ].astype(BF16)
            put(target, p, part + quarter, blocks[2])
        at = put_rest(p, 0, lift_query[here])
        small = rank_part * kv // heads
        for n in range(rank_part // small):
            rest[p][at : at + small, n * kv : (n + 1) * kv] = lift_kv[
                p * rank_part + n * small : p * rank_part + (n + 1) * small
            ].astype(BF16)
        at = put_rest(p, at + small, out_down[here])
        here_columns = pl.multiple_of(place[4], 128)
        for ranks_of, rows_of in ((out_sum, branch), (down_sum, grad_ffn)):
            value = tn(ranks_of[:, here], rows_of[:, pl.ds(here_columns, share_columns)])
            for block in range(0, share_columns, heads):
                at = put_rest(p, at, value[:, block : block + heads])
        if share_rows % 128 == 0:
            first = pl.multiple_of(2 * p * part + place[5], 128)
            value = tn(second[:, pl.ds(first, share_rows)], rank_gu[...])
        else:
            value = share_of(tn(second[:, columns], rank_gu[...]), place[5], share_rows)
        for block in range(0, value.shape[1], heads):
            at = put_rest(p, at, value[:, block : block + heads])


def add_kernel(*refs):
    total = 0.0
    for ref in refs[:-1]:
        total += ref[...].astype(F32).reshape(refs[-1].shape)
    refs[-1][...] = total.astype(refs[-1].dtype)


def add_pass(dtype, *blocks):
    inputs, specs = [], []
    for block in blocks:
        if isinstance(block, tuple):
            block, at = block
            specs.append(
                pl.BlockSpec(
                    (1, *block.shape[1:]), functools.partial(lambda at, t: (at, 0, 0), at)
                )
            )
            shape = block.shape[1:]
        else:
            specs.append(whole_spec(block.shape))
            shape = block.shape
        inputs.append(block)
    return pl.pallas_call(
        add_kernel,
        grid=(1,),
        in_specs=specs,
        out_specs=whole_spec(shape),
        out_shape=jax.ShapeDtypeStruct(shape, dtype),
        compiler_params=params(),
        cost_estimate=BRIEF,
        name="add_pass",
    )(*inputs)


def gate_kernel(count, width, rank_part, has_base, *refs):
    blocks, refs = refs[:4], refs[4:]
    pieces = [(refs[2 * p], refs[2 * p + 1]) for p in range(count)]
    refs = refs[2 * count :]
    bases, refs = (refs[:2], refs[2:]) if has_base else ((), refs)
    gated_ref, gate_ref, upper_ref, *outs = refs[:5]
    adapters = refs[5]
    start = pl.program_id(0) == 0
    rows = blocks[0].shape[0]
    part = width // 2
    rank = count * rank_part
    model_width = count * width
    for b in range(2):
        for k in range(3):
            first = 3 * part + k * rank_part
            for p in range(count):
                adapters[3 * b + k, p * rank_part : (p + 1) * rank_part, :] = pieces[p][b][
                    first : first + rank_part, :
                ]
    for b in range(2):
        normed, grad = blocks[b], blocks[2 + b]
        span = slice(b * rows, (b + 1) * rows)
        gate = nn(normed[:, model_width : model_width + rank], adapters[3 * b])
        upper = nn(normed[:, model_width + rank :], adapters[3 * b + 1])
        grad_gated = nn(grad[:, model_width:], adapters[3 * b + 2])
        for p in range(count):
            columns = slice(p * width, (p + 1) * width)
            gate += nn(normed[:, columns], pieces[p][0][:width, :])
            upper += nn(normed[:, columns], pieces[p][1][:width, :])
            for e in range(2):
                columns = slice(p * width + e * part, p * width + (e + 1) * part)
                grad_gated += nn(grad[:, columns], pieces[p][e][width : width + part, :])
        square = gate * gate
        bent = jnp.tanh(GELU_SCALE * gate * (1.0 + 0.044715 * square))
        half = 0.5 * (1.0 + bent)
        active = gate * half
        slope = half + 0.5 * gate * (1.0 - bent * bent) * GELU_SCALE * (
            1.0 + 3.0 * 0.044715 * square
        )
        gated_ref[span, :] = (active * upper).astype(BF16)
        gate_ref[span, :] = (grad_gated * upper * slope).astype(BF16)
        upper_ref[span, :] = (grad_gated * active).astype(BF16)

    def put(b, first, value):
        columns = slice(first, first + value.shape[1])
        before = outs[b][:, columns].astype(F32)
        base = bases[b][:, columns].astype(F32) if bases else jnp.zeros_like(before)
        value = value + jnp.where(start, base, before)
        outs[b][:, columns] = value.astype(outs[b].dtype)

    for p in range(count):
        value = nt(gate_ref[...], pieces[p][0][:width, :]) + nt(
            upper_ref[...], pieces[p][1][:width, :]
        )
        for b in range(2):
            put(b, p * width, value[b * rows : (b + 1) * rows])
    for b in range(2):
        span = slice(b * rows, (b + 1) * rows)
        put(b, model_width, nt(gate_ref[span, :], adapters[3 * b]))
        put(b, model_width + rank, nt(upper_ref[span, :], adapters[3 * b + 1]))


def gate_pass(normed_pair, grad_pair, chunks, width, rank_part, bases, last):
    blocks = (*normed_pair, *grad_pair)
    rows, columns = blocks[0].shape
    both_rows, size = 2 * rows, len(chunks)
    pairs = [block for pair in chunks[0] for block in pair]
    height = 3 * (width // 2 + rank_part)
    chunk = pairs[0][0].shape[1]
    tiled = pl.BlockSpec((both_rows, chunk), lambda t: (0, t))
    return pl.pallas_call(
        functools.partial(gate_kernel, len(chunks[0]), width, rank_part, bool(bases)),
        grid=(size,),
        in_specs=[whole_spec(a.shape) for a in blocks]
        + [
            pl.BlockSpec((height, chunk), functools.partial(lambda at, t: (at + t, 0), at))
            for _, at in pairs
        ]
        + [whole_spec(a.shape) for a in bases],
        out_specs=[tiled] * 3 + [whole_spec((rows, columns))] * 2,
        out_shape=[jax.ShapeDtypeStruct((both_rows, size * chunk), BF16)] * 3
        + [
            jax.ShapeDtypeStruct((rows, columns), F32 if last else BF16),
            jax.ShapeDtypeStruct((rows, columns), BF16),
        ],
        scratch_shapes=[pltpu.VMEM((6, len(chunks[0]) * rank_part, chunk), BF16)],
        compiler_params=pltpu.CompilerParams(vmem_limit_bytes=60 * 1024 * 1024),
        cost_estimate=BRIEF,
        name="gate_pass",
    )(*blocks, *[block for block, _ in pairs], *bases)


def down_kernel(count, rows, width, rank_part, chunks, *refs):
    acts, refs = refs[:chunks], refs[chunks:]
    outs, adapters = refs[-3:-1], refs[-1]
    part = width // 2
    pieces = [
        [refs[2 * (q * count + p) : 2 * (q * count + p) + 2] for p in range(count)]
        for q in range(chunks)
    ]
    for b in range(2):
        span = slice(b * rows, (b + 1) * rows)
        for p in range(count):
            for e in range(2):
                value = nt(acts[0][span, :], pieces[0][p][e][width : width + part, :])
                for q in range(1, chunks):
                    value += nt(acts[q][span, :], pieces[q][p][e][width : width + part, :])
                first = p * width + e * part
                outs[b][:, first : first + part] = value.astype(outs[b].dtype)
        value = 0.0
        first = 3 * part + 2 * rank_part
        for q in range(chunks):
            for p in range(count):
                adapters[p * rank_part : (p + 1) * rank_part, :] = pieces[q][p][b][
                    first : first + rank_part, :
                ]
            value += nt(acts[q][span, :], adapters[...])
        outs[b][:, count * width :] = value.astype(outs[b].dtype)


def down_pass(acts, chunks, width, rank_part):
    count = len(chunks[0])
    both_rows = acts[0][0].shape[0]
    chunk = chunks[0][0][0][0].shape[1]
    rows = both_rows // 2
    columns = count * (width + rank_part)
    height = 3 * (width // 2 + rank_part)
    pairs = [block for pieces in chunks for pair in pieces for block in pair]
    shapes = [
        jax.ShapeDtypeStruct((rows, columns), F32),
        jax.ShapeDtypeStruct((rows, columns), BF16),
    ]
    return pl.pallas_call(
        functools.partial(down_kernel, count, rows, width, rank_part, len(chunks)),
        grid=(1,),
        in_specs=[
            pl.BlockSpec(
                (both_rows, chunk),
                functools.partial(lambda n, t: (0, n), n),
                pipeline_mode=pl.Buffered(1),
            )
            for _, n in acts
        ]
        + [
            pl.BlockSpec(
                (height, chunk),
                functools.partial(lambda at, t: (at, 0), at),
                pipeline_mode=pl.Buffered(1),
            )
            for _, at in pairs
        ],
        out_specs=[whole_spec(s.shape) for s in shapes],
        out_shape=shapes,
        scratch_shapes=[pltpu.VMEM((count * rank_part, chunk), BF16)],
        compiler_params=params(),
        cost_estimate=BRIEF,
        name="down_pass",
    )(*[a for a, _ in acts], *[block for block, _ in pairs])


def sum_kernel(*refs):
    total = refs[0][...].astype(F32)
    for other in refs[1:-1]:
        total = total + other[...].astype(F32)
    refs[-1][...] = total.astype(BF16)


def sum_pass(*blocks):
    blocks = [b if isinstance(b, tuple) else (b, 0) for b in blocks]
    rows, columns = min((b.shape for b, _ in blocks), key=lambda shape: shape[0])
    steps = 4
    return pl.pallas_call(
        sum_kernel,
        grid=(steps,),
        in_specs=[
            pl.BlockSpec(
                (rows // steps, columns), functools.partial(lambda at, t: (at * steps + t, 0), at)
            )
            for _, at in blocks
        ],
        out_specs=pl.BlockSpec((rows // steps, columns), lambda t: (t, 0)),
        out_shape=jax.ShapeDtypeStruct((rows, columns), BF16),
        compiler_params=params(),
        cost_estimate=BRIEF,
        name="sum_pass",
    )(*[b for b, _ in blocks])


def turn_kernel(own, other, turned):
    rows = own.shape[0]
    turned[:, :rows] = own[...].T
    turned[:, rows:] = other[...].T


def turn_pass(own, other):
    rows, columns = own.shape
    tile = 256
    source = pl.BlockSpec((rows, tile), lambda t: (0, t))
    return pl.pallas_call(
        turn_kernel,
        grid=(columns // tile,),
        in_specs=[source, source],
        out_specs=pl.BlockSpec((tile, 2 * rows), lambda t: (t, 0)),
        out_shape=jax.ShapeDtypeStruct((columns, 2 * rows), own.dtype),
        compiler_params=params(),
        cost_estimate=BRIEF,
        name="turn_pass",
    )(own, other)


def weight_kernel(part, rank_part, sides, adds, aliased, core, *refs):
    gate, upper, gated = refs[:3]
    refs = refs[3:]
    rows = gate.shape[0] // 2
    outs = refs[-len(sides) :]
    for side, number, out in zip(sides, adds, outs):
        normed, grad, *ranks = refs[:5]
        added = refs[5 : 5 + number]
        refs = refs[5 + number :]

        def store(start, value):
            here = slice(start, start + value.shape[0])
            for other in added:
                value = value + other[here, :].astype(F32)
            out[here, :] = value.astype(out.dtype)

        for n, (columns, act) in enumerate(((normed, gate), (normed, upper), (grad, gated))):
            store(n * part, nn(columns[...], act[...]))
        span = slice(side * rows, (side + 1) * rows)
        for n, act in enumerate((gate, upper, gated)):
            store(3 * part + n * rank_part, nn(ranks[n][:, span], act[span, :]))


def weight_pass(core, normed_t, grad_t, width, rank_part, acts, chunk, at, count, items, held=()):
    both_rows = normed_t.shape[1]
    part = width // 2
    height = 3 * (part + rank_part)
    tile = min(256, chunk)
    model_blocks = (2 * grad_t.shape[0] - normed_t.shape[0]) // rank_part
    rank_blocks = (normed_t.shape[0] - grad_t.shape[0]) // rank_part

    def rows_of(index, side):
        return pl.BlockSpec(
            (part, both_rows),
            lambda t, core: (2 * index + (core[0] ^ side), 0),
            pipeline_mode=pl.Buffered(1),
        )

    def ranks_of(block):
        return pl.BlockSpec(
            (rank_part, both_rows), lambda t, core: (block, 0), pipeline_mode=pl.Buffered(1)
        )

    tiled = pl.BlockSpec((height, tile), lambda t, core: (at, t))
    inputs = [a for a, _ in acts]
    specs = [
        pl.BlockSpec(
            (both_rows, tile),
            functools.partial(lambda n, t, core: (0, n * (chunk // tile) + t), n),
        )
        for _, n in acts
    ]
    for index, side, added, _ in items:
        inputs += [normed_t, grad_t, normed_t, normed_t, grad_t, *[block for block, _ in added]]
        specs += [rows_of(index, side)] * 2
        specs += [ranks_of(model_blocks + n * rank_blocks + index) for n in (0, 1, 0)]
        specs += [
            pl.BlockSpec((height, tile), functools.partial(lambda n, t, core: (n, t), n))
            for _, n in added
        ]
    aliases = {1 + len(inputs) + n: n for n in range(len(held))}
    return pl.pallas_call(
        functools.partial(
            weight_kernel,
            part,
            rank_part,
            tuple(item[1] for item in items),
            tuple(len(item[2]) for item in items),
            len(held),
        ),
        grid_spec=pltpu.PrefetchScalarGridSpec(
            num_scalar_prefetch=1,
            grid=(chunk // tile,),
            in_specs=specs + [pl.BlockSpec(memory_space=pl.ANY) for _ in held],
            out_specs=[tiled] * len(items),
        ),
        out_shape=[jax.ShapeDtypeStruct((count * height, chunk), item[3]) for item in items],
        input_output_aliases=aliases,
        compiler_params=params(),
        cost_estimate=BRIEF,
        name="weight_pass",
    )(core, *inputs, *held)


def finish_kernel(part, rank_part, core, *refs):
    *mine, other = refs[:-4]
    gate_up, down, lora_gate_up, lora_hidden = refs[-4:]
    for side, sources in enumerate((mine, [other])):

        @pl.when(pl.program_id(0) == side)
        def _(sources=sources):
            def rows(start, height):
                total = sources[0][start : start + height, :].astype(F32)
                for source in sources[1:]:
                    total = total + source[start : start + height, :].astype(F32)
                return total

            gate_up[0] = rows(0, part)
            gate_up[1] = rows(part, part)
            down[...] = rows(2 * part, part).T
            lora_gate_up[0, 0] = rows(3 * part, rank_part)
            lora_gate_up[0, 1] = rows(3 * part + rank_part, rank_part)
            lora_hidden[0] = rows(3 * part + 2 * rank_part, rank_part)


def finish_pass(core, mine, other, part, rank_part, hidden):
    chunk = other.shape[1]
    height = other.shape[0] // CHUNKS

    def source(side, first=0):
        return pl.BlockSpec(
            (height, chunk),
            lambda s, q, core: (first + jnp.where(s == side, q, (CHUNKS - 1) * (1 - side)), 0),
        )

    def column(s, q, core):
        return (core[0] ^ s) * CHUNKS + q

    shapes = [
        jax.ShapeDtypeStruct(s, F32)
        for s in (
            (2, part, hidden),
            (hidden, part),
            (1, 2, rank_part, hidden),
            (1, rank_part, hidden),
        )
    ]
    grid_spec = pltpu.PrefetchScalarGridSpec(
        num_scalar_prefetch=1,
        grid=(2, CHUNKS),
        in_specs=[source(0, first) for _, first in mine] + [source(1)],
        out_specs=[
            pl.BlockSpec((2, part, chunk), lambda s, q, core: (0, 0, column(s, q, core))),
            pl.BlockSpec((chunk, part), lambda s, q, core: (column(s, q, core), 0)),
            pl.BlockSpec(
                (1, 2, rank_part, chunk), lambda s, q, core: (0, 0, 0, column(s, q, core))
            ),
            pl.BlockSpec((1, rank_part, chunk), lambda s, q, core: (0, 0, column(s, q, core))),
        ],
    )
    return pl.pallas_call(
        functools.partial(finish_kernel, part, rank_part),
        grid_spec=grid_spec,
        out_shape=shapes,
        compiler_params=params(),
        cost_estimate=BRIEF,
        name="finish_pass",
    )(core, *[block for block, _ in mine], other)


def dot(left_op, right_op):
    return jnp.dot(left_op, right_op, preferred_element_type=F32)


def pad_rows(block, rows, width):
    return jnp.pad(block, ((0, rows - block.shape[0]), (0, width - block.shape[1])))


def local(
    tokens,
    cotangent,
    lengths,
    bucket_loop_index,
    query_weight,
    key_value_weight,
    output_weight,
    gate_up_weight,
    down_weight,
    gains,
    adapter_input_down,
    adapter_query_up,
    adapter_key_value,
    adapter_output_down,
    adapter_hidden_down,
    adapter_model_up,
    adapter_gate_up,
):
    dp_count = lax.axis_size("dp")
    dp_id = lax.axis_index("dp")
    depth_id = lax.axis_index("depth")
    mp_index = lax.axis_index("mp")
    first_core = depth_id == 0
    row_count, model_width = tokens.shape
    slice_width = model_width // dp_count
    part_width = slice_width // 2
    heads_width = query_weight.shape[1]
    heads_here = heads_width // HEAD_SIZE
    kv_width = key_value_weight.shape[1]
    joint_width = heads_width + kv_width
    rank_part = adapter_query_up.shape[1]
    rank = rank_part * dp_count
    hidden = down_weight.shape[0]
    half_hidden = hidden // 2
    chunk = half_hidden // CHUNKS

    def partner(block):
        return trade(block, "depth", 1)

    def in_core_order(own, other):
        return jnp.where(first_core, own, other), jnp.where(first_core, other, own)

    keep_own = bucket_loop_index[0, depth_id] == depth_id
    tok_swap, grad_swap = partner(tokens), partner(cotangent)
    slot_id = jnp.where(keep_own, depth_id, 1 - depth_id)
    seq_lens = lengths[0, slot_id]
    places, segment, within, valid_rows = layout(seq_lens, row_count)
    cosine, sine_part = rotary(within, HEAD_SIZE)
    tok_rows = relative(jnp.where(keep_own, tokens, tok_swap), 1, dp_id, dp_count)
    grad_rows = relative(jnp.where(keep_own, cotangent, grad_swap), 1, dp_id, dp_count)
    grad_ffn = (grad_rows.astype(F32) * valid_rows[:, None]).astype(BF16)

    mp_count = lax.axis_size("mp")
    share_rows = slice_width // mp_count
    share_columns = model_width // mp_count
    core = depth_id[None].astype(jnp.int32)
    ffn_arrays = (gate_up_weight, down_weight, adapter_gate_up, adapter_hidden_down)
    taken = partner(give_pass(core, ffn_arrays, chunk))
    bundles = pack_pass(
        mp_index[None].astype(jnp.int32),
        (query_weight, key_value_weight, output_weight, gains)
        + (adapter_query_up, adapter_key_value, adapter_output_down)
        + (adapter_input_down, adapter_model_up),
        mp_count,
        rank,
    )
    bundle = bundle_pass(core, ffn_arrays, taken, chunk)
    pieces, hold = gather_pair(*bundles, bundle, tok_rows, grad_ffn)
    shared_own, input_attn, late, joint_lifted, out_down = unpack_pass(
        pieces, part_width, rank_part, rank, share_rows, share_columns, heads_width
    )
    joint_weight, out_weight, gains_all = shared_pass(
        core, shared_own, partner(shared_own), dp_count, part_width, heads_width
    )
    model_all, input_ffn = late_pass(
        lax.all_gather(late, "mp", axis=0, tiled=False),
        share_rows,
        share_columns,
        rank_part,
    )
    model_all = relative(model_all, 2, dp_id, dp_count)

    near = gather_near(after(bundle, *hold))
    height = 3 * (part_width + rank_part)

    is_key = mp_index * kv_width < HEAD_SIZE
    place = jnp.stack([dp_id * rank_part, is_key.astype(jnp.int32), depth_id, dp_id]
        + [((mp_index * share_columns // slice_width) ^ dp_id) * slice_width + mp_index * share_columns % slice_width, mp_index * share_rows]).astype(jnp.int32)
    row_segment, column_segment = segment[:, None], segment[None, :]
    normalized_rows, rank_rows, query_rows, joint_part = simple_pass(
        project_kernel,
        "project_pass",
        (tok_rows, gains_all, input_attn, joint_weight, joint_lifted, cosine, sine_part),
        [
            ((row_count, model_width), BF16),
            ((row_count, 3 * rank), BF16),
            ((row_count, heads_width), BF16),
            ((row_count, kv_width), BF16),
        ],
        place,
    )
    joint_key_value = lax.all_gather(joint_part, "mp", axis=0, tiled=False)
    key_rows, flat_heads, branch_part = simple_pass(
        attend_kernel,
        "attend_pass",
        (query_rows, joint_key_value, cosine, sine_part, row_segment, column_segment)
        + (out_weight, out_down),
        [
            ((row_count, HEAD_SIZE), BF16),
            ((row_count, heads_width), BF16),
            ((row_count, model_width + rank), BF16),
        ],
    )
    chunks = gather_far(near, flat_heads, height)
    branch_sum = lax.psum(branch_part, "mp")
    rank_out = branch_sum[:, model_width:]

    hidden_state, normed_own = simple_pass(
        second_kernel,
        "second_pass",
        (tok_rows, branch_sum, model_all, gains_all, input_ffn),
        [((row_count, model_width), F32), ((row_count, model_width + 2 * rank), BF16)],
        place,
    )
    (grad_own,) = simple_pass(
        grad_kernel,
        "grad_pass",
        (grad_ffn, model_all),
        [((row_count, model_width + rank), BF16)],
    )
    grad_pair = (grad_own, partner(grad_own))
    grad_t = turn_pass(*grad_pair)
    normed_pair = (after(normed_own, grad_t), partner(normed_own))

    acts, sums = [], ()
    size = CHUNKS // GROUPS
    for group in range(GROUPS):
        *act, own_sum, other_sum = gate_pass(
            normed_pair,
            grad_pair,
            chunks[group * size : (group + 1) * size],
            slice_width,
            rank_part,
            sums,
            group == GROUPS - 1,
        )
        acts += [[(a, n) for a in act] for n in range(size)]
        sums = (own_sum, other_sum)
    normed_t = turn_pass(after(normed_own, sums[1]), normed_pair[1])
    grad_norm_ready = sum_pass(sums[0], partner(sums[1]))
    first_space = partner(grad_norm_ready[:16])
    grad_norm_sum = lax.psum(grad_norm_ready, "mp")

    def weight_share(items, hold, held=(), start=0, count=CHUNKS):
        for c in range(CHUNKS):
            gated, grad_gate, grad_upper = acts[c]
            if hold is not None:
                grad_gate = (after(grad_gate[0], hold), grad_gate[1])
            held = weight_pass(
                core,
                normed_t,
                grad_t,
                slice_width,
                rank_part,
                (grad_gate, grad_upper, gated),
                chunk,
                start + c,
                count,
                items,
                held,
            )
        return held

    sends, held, last_sent = (), (), ()
    if dp_count == 4:
        sends = weight_share(
            [(3, 0, (), BF16), (3, 1, (), BF16)], first_space, count=2 * CHUNKS
        )
        sends = weight_share(
            [(1, 0, (), BF16), (2, 1, (), BF16)], first_space, sends, CHUNKS, 2 * CHUNKS
        )
        near_one, near_two = trade(sends[0], "dp", 1), trade(sends[1], "dp", 2)
        held = weight_share([(1, 1, (), BF16), (2, 0, (), BF16)], sends[0])

    acts_down = [(after(a[0][0], first_space, *sends), a[0][1]) for a in acts]
    ffn_own, ffn_given = down_pass(acts_down, chunks, slice_width, rank_part)
    ffn_ready = sum_pass(ffn_own, partner(ffn_given))
    grad_norm_sum = after(grad_norm_sum, ffn_ready)
    if dp_count == 4:
        grad_norm_sum = after(grad_norm_sum, *held)
    half_rows = row_count // 2
    ffn_first, ffn_last = simple_pass(
        early_kernel,
        "early_pass",
        (ffn_ready,),
        [((half_rows, model_width + 2 * rank), BF16), ((half_rows, model_width), BF16)],
    )
    ffn_first = after(ffn_first, grad_norm_sum)
    grad_norm_sum = after(grad_norm_sum, partner(ffn_first))
    ffn_first = lax.psum(ffn_first, "mp")
    rank_down = jnp.concatenate(
        [ffn_first[:, model_width : model_width + rank], ffn_first[:, model_width + rank :]],
        axis=0,
    )

    grad_hidden, grad_branch, grad_rank_gu, grad_rank_out, grad_query, grad_joint, gain_two = (
        simple_pass(
            attend_back_kernel,
            "attend_back_pass",
            (grad_norm_sum, hidden_state, gains_all, input_ffn, grad_ffn, model_all)
            + (out_weight, out_down, query_rows, key_rows, joint_key_value)
            + (cosine, sine_part, row_segment, column_segment),
            [
                ((row_count, model_width), F32),
                ((row_count, model_width), BF16),
                ((row_count, 2 * rank), BF16),
                ((row_count, rank), BF16),
                ((row_count, heads_width), BF16),
                ((mp_count, row_count, kv_width), BF16),
                ((8, model_width), F32),
            ],
            place,
            LONG,
        )
    )
    grad_kv = lax.psum_scatter(after(grad_joint, ffn_first), "mp", scatter_dimension=0, tiled=False)
    if dp_count == 4:
        near_one, near_two = after(near_one, grad_query), after(near_two, grad_query)
        last_one = sum_pass(held[0], (near_two, 0))
        last_two = sum_pass(held[1], (near_one, 0))
        last_sent = (trade(last_one, "dp", 1), trade(last_two, "dp", 2))
    (grad_norm_part,) = simple_pass(
        project_back_kernel,
        "project_back_pass",
        (grad_query, grad_kv, joint_weight, joint_lifted),
        [((row_count, model_width + 3 * rank), BF16)],
        place,
    )
    ffn_last = after(ffn_last, ffn_first)
    grad_norm_one, ffn_last = lax.psum((grad_norm_part, ffn_last), "mp")
    grad_rows, grad_rank_qkv, gain_one = simple_pass(
        first_back_kernel,
        "first_back_pass",
        (grad_norm_one, tok_rows, gains_all, input_attn, grad_hidden),
        [
            ((row_count, model_width), BF16),
            ((row_count, 3 * rank), BF16),
            ((8, model_width), F32),
        ],
        place,
        LONG,
    )
    grad_input = relative(grad_rows, 1, dp_id, dp_count)
    grad_input_attn = product(normalized_rows, grad_rank_qkv, 0, 0).astype(BF16)

    quarter = part_width * kv_width // heads_width
    small = rank_part * kv_width // heads_width
    blocks = share_columns // heads_width
    mp_rows = 2 * blocks * rank_part + 2 * rank // heads_width * share_rows
    rest_rows = 2 * rank_part + small + mp_rows
    base_rows = 2 * part_width + quarter
    shares, shares_given, *rest = simple_pass(
        functools.partial(shares_kernel, dp_count, share_rows, share_columns),
        "shares_pass",
        (after(normalized_rows, grad_norm_part), grad_query, grad_kv, rank_rows, grad_branch, flat_heads)
        + (grad_rank_out, rank_out, normed_own, grad_rank_gu, rank_down, grad_ffn),
        [
            ((dp_count, base_rows, heads_width), BF16),
            ((dp_count, base_rows, heads_width), BF16),
            *[((rest_rows, heads_width), BF16)] * dp_count,
        ],
        place,
    )
    own = ()
    if dp_count == 4:
        own = weight_share([(0, 0, (), BF16), (0, 1, (), BF16)], grad_norm_part)
    shares_given = after(shares_given, *own)
    shares_got = after(partner(shares_given), grad_input_attn)

    def shared(p, dtype, *more):
        return add_pass(dtype, (shares, p), (shares_got, p), *more)

    far_share = shared(dp_count - 1, BF16)
    if dp_count == 4:
        mine = [(own[0], 0), (near_one, CHUNKS), (last_sent[1], 0)]
        theirs = sum_pass(
            own[1], (near_two, 1), after(last_sent[0], last_sent[1], far_share)
        )
        summed = after(grad_rank_qkv, theirs)
        theirs = partner(theirs)
    else:
        summed = grad_rank_qkv
        by_index = [
            weight_share([(p, 0, (), BF16), (p, 1, (), BF16)], None)
            for p in range(dp_count)
        ]
        mine = [(scatter_dp([b[0] for b in by_index]), 0)]
        theirs = partner(scatter_dp([b[1] for b in by_index]).astype(BF16))
    grad_w_gateup, grad_w_down, grad_lora_gateup, grad_lora_hidden = finish_pass(
        core, mine, theirs, part_width, rank_part, hidden
    )

    ffn_sum = jnp.concatenate([ffn_first[:, :model_width], ffn_last], axis=0)
    output = hidden_state + ffn_sum.astype(F32) + dot(rank_down, model_all[1])
    result_rows = relative(output.astype(BF16), 1, dp_id, dp_count)
    result_rows = after(result_rows, grad_w_down)
    grad_input = after(grad_input, grad_w_down)

    if dp_count == 4:
        near_share = trade(far_share, "dp", 1)
        near_rest = after(trade(after(rest[3], *own), "dp", 2), summed)
        share_one, rest_two = trade(after(shared(1, BF16), summed), "dp", 1), trade(after(rest[2], near_rest), "dp", 2)
        share_two = trade(shared(2, BF16, near_share), "dp", 2)
        rest_one = trade(add_pass(BF16, rest[1], near_rest), "dp", 1)
        share_own = shared(0, F32, after(share_one, grad_w_down), share_two)
        rest_own = add_pass(F32, rest[0], after(rest_one, grad_rank_qkv), rest_two)
    else:
        share_own = scatter_dp([shared(p, BF16) for p in range(dp_count)])
        rest_own = scatter_dp([rest[p] for p in range(dp_count)])

    share_own, rest_own = after(share_own, grad_rank_qkv), after(rest_own, grad_rank_qkv)

    def unfolded(block, width, heights):
        rows = heights
        columns = [block[at : at + rows, :width] for at in range(0, block.shape[0], rows)]
        return jnp.concatenate(columns, axis=1)

    def side_by_side(block, width):
        return jnp.concatenate(
            [block[:, at : at + width] for at in range(0, heads_width, width)], axis=0
        )

    grad_w_query = share_own[:part_width]
    grad_w_keyval = side_by_side(share_own[part_width : part_width + quarter], kv_width)
    grad_w_output = share_own[part_width + quarter :].T
    at = rank_part
    grad_lora_query = rest_own[:at][None]
    grad_lora_keyval = side_by_side(rest_own[at : at + small], kv_width)[None]
    at += small
    grad_lora_out = rest_own[at : at + rank_part][None]
    at += rank_part
    gathered = lax.all_gather(rest_own[at:].astype(BF16), "mp", axis=0, tiled=False).astype(F32)
    model_own, at = [], 0
    for _ in range(2):
        block = gathered[:, at : at + blocks * rank_part].reshape(-1, heads_width)
        model_own.append(unfolded(block, heads_width, rank_part))
        at += blocks * rank_part
    grad_lora_model = jnp.stack(model_own)[None]
    ffn_in_own = jnp.concatenate(
        [unfolded(gathered[z, at:], heads_width, share_rows) for z in range(mp_count)], axis=0
    )

    def by_dp(block):
        return block.reshape(dp_count, block.shape[0] // dp_count, block.shape[1])

    gain_grads = jnp.stack([gain_one[0], gain_two[0]]).astype(BF16)
    gain_grads = gain_grads.reshape(2, dp_count, slice_width)
    grad_input_attn = by_dp(grad_input_attn)
    attn_in_own = scatter_dp(
        [
            jnp.concatenate(
                [grad_input_attn[p], pad_rows(gain_grads[:, p], 16, 3 * rank)], axis=0
            )
            for p in range(dp_count)
        ],
        grad_w_down,
    )
    gain_grads = attn_in_own[slice_width : slice_width + 2, :slice_width]
    gain_first, gain_second = gain_grads[:, :part_width], gain_grads[:, part_width:]
    grad_w_gains = jnp.where(first_core, gain_first, gain_second) + partner(
        jnp.where(first_core, gain_second, gain_first)
    )
    input_own = jnp.concatenate([attn_in_own[:slice_width], ffn_in_own], axis=1)
    grad_lora_in = jnp.stack([input_own[:, k * rank : (k + 1) * rank] for k in range(5)])[None]

    mixed_rows = jnp.where(keep_own, result_rows, partner(result_rows))
    grad_tokens = jnp.where(keep_own, grad_input, partner(grad_input))
    return (
        mixed_rows,
        grad_tokens,
        grad_w_query,
        grad_w_keyval,
        grad_w_output,
        grad_w_gateup,
        grad_w_down,
        grad_w_gains,
        grad_lora_in,
        grad_lora_query,
        grad_lora_keyval,
        grad_lora_out,
        grad_lora_hidden,
        grad_lora_model,
        grad_lora_gateup,
    )


def solution(mesh):
    return jax.shard_map(
        local,
        mesh=mesh,
        in_specs=(
            P(("dp", "depth"), None),
            P(("dp", "depth"), None),
            P("dp", None, None),
            P("dp", None),
            P(("dp", "depth"), "mp"),
            P(("dp", "depth"), "mp"),
            P("mp", ("dp", "depth")),
            P(None, ("dp", "depth"), "mp"),
            P("mp", ("dp", "depth")),
            P(None, ("dp", "depth")),
            P("depth", None, "dp", None),
            P("depth", "dp", "mp"),
            P("depth", "dp", "mp"),
            P("depth", "dp", "mp"),
            P("depth", "dp", "mp"),
            P("depth", None, "dp", None),
            P("depth", None, "dp", "mp"),
        ),
        out_specs=(
            P(("dp", "depth"), None),
            P(("dp", "depth"), None),
            P(("dp", "depth"), "mp"),
            P(("dp", "depth"), "mp"),
            P("mp", ("dp", "depth")),
            P(None, ("dp", "depth"), "mp"),
            P("mp", ("dp", "depth")),
            P(None, ("dp", "depth")),
            P("depth", None, "dp", None),
            P("depth", "dp", "mp"),
            P("depth", "dp", "mp"),
            P("depth", "dp", "mp"),
            P("depth", "dp", "mp"),
            P("depth", None, "dp", None),
            P("depth", None, "dp", "mp"),
        ),
        check_vma=False,
    )
```

```python
import functools

import jax
import jax.numpy as jnp
from jax import lax
from jax.experimental import pallas as pl
from jax.experimental.pallas import tpu as pltpu
from jax.sharding import PartitionSpec as P

HEAD_SIZE = 256


EPS = 1e-06
THETA = 10000.0
NEGATIVE = -1e30


def product(left_op, right_op, left_dim, right_dim):
    return lax.dot_general(
        left_op,
        right_op,
        (((left_dim,), (right_dim,)), ((), ())),
        preferred_element_type=jnp.float32,
    )


def layout(seq_lens, row_count):
    seq_ends = jnp.cumsum(seq_lens)
    places = jnp.arange(row_count, dtype=jnp.int32)
    passed = (places[:, None] >= seq_ends[None, :]).astype(jnp.int32)
    segment = jnp.sum(passed, axis=1)
    starts = jnp.sum(passed * seq_lens[None, :], axis=1)
    valid_rows = (places < seq_ends[-1]).astype(jnp.float32)
    within = (places - starts).astype(jnp.float32)
    return (places, segment, within, valid_rows)


def rotary(within, head_width):
    half_width = head_width // 2
    frequency = THETA ** (-2.0 * jnp.arange(half_width, dtype=jnp.float32) / head_width)
    angles = within[:, None] * frequency[None, :]
    return (jnp.cos(angles), jnp.sin(angles))


def rotate(vector, cosine, sine_part):
    half_width = vector.shape[-1] // 2
    former = vector[..., :half_width]
    latter = vector[..., half_width:]
    return jnp.concatenate(
        [former * cosine - latter * sine_part, latter * cosine + former * sine_part], axis=-1
    )


def rotate_back(vector, cosine, sine_part):
    half_width = vector.shape[-1] // 2
    former = vector[..., :half_width]
    latter = vector[..., half_width:]
    return jnp.concatenate(
        [former * cosine + latter * sine_part, latter * cosine - former * sine_part], axis=-1
    )


def rms_forward(values, gain_row):
    inverse = lax.rsqrt(jnp.mean(values * values, axis=-1, keepdims=True) + EPS)
    return (values * inverse * gain_row, inverse)


def rms_backward(values, inverse, gain_row, grad_norm):
    weighted = grad_norm * gain_row
    grad_values = inverse * weighted - values * inverse**3 * jnp.mean(
        weighted * values, axis=-1, keepdims=True
    )
    grad_gain = jnp.sum(grad_norm * values * inverse, axis=0)
    return (grad_values, grad_gain)


def gelu_tanh(values):
    return jax.nn.gelu(values, approximate=True)


def block_mask(places, segment):
    return (segment[:, None] == segment[None, :]) & (places[None, :] <= places[:, None])


CHUNKS = 4
GROUPS = 2
BF16 = jnp.bfloat16
F32 = jnp.float32


def trade(block, axis, mask):
    count = lax.axis_size(axis)
    return lax.ppermute(block, axis, [(i, i ^ mask) for i in range(count)])


def gather_dp(piece, *hold):
    count = lax.axis_size("dp")
    if count == 4:
        half = piece.shape[0] // 2
        from_one = trade(piece, "dp", 1)
        from_two = trade(piece, "dp", 2)
        far = jnp.concatenate(
            [
                trade(after(from_two[:half], *hold), "dp", 1),
                trade(after(from_one[half:], *hold), "dp", 2),
            ],
            axis=0,
        )
        return [piece, from_one, from_two, far]
    pieces, mask = [piece], 1
    while mask < count:
        pieces = pieces + [trade(held, "dp", mask) for held in pieces]
        mask *= 2
    return pieces


def gather_pair(one, two, *early):
    count = lax.axis_size("dp")
    if count == 4:
        first_one, first_two = trade(one, "dp", 1), trade(one, "dp", 2)
        second_one, second_two = trade(two, "dp", 1), trade(two, "dp", 2)
        far = trade(after(first_two, *early), "dp", 1), trade(second_one, "dp", 2)
        pieces = [(one, two), (first_one, second_one), (first_two, second_two), far]
        return pieces, (first_two, second_one)
    ones, twos = gather_dp(one), gather_dp(two)
    return list(zip(ones, twos)), (ones[-1], twos[-1])


def gather_near(bundle):
    count = lax.axis_size("dp")
    pieces, mask = [bundle], 1
    while mask < count:
        first = pieces if count != 4 else pieces[:1]
        pieces = pieces + [trade(held, "dp", mask) for held in first]
        mask *= 2
    return pieces


def gather_far(near, hold, height):
    chunks = [[((b, c), (b, CHUNKS + c)) for b in near] for c in range(CHUNKS)]
    cut = []
    if lax.axis_size("dp") == 4:
        size = CHUNKS // GROUPS
        for group in range(GROUPS):
            rows = (size * group * height, size * (group + 1) * height)
            one = lax.slice_in_dim(after(near[2], hold), *rows, axis=0)
            two = lax.slice_in_dim(
                after(near[1], hold), *[CHUNKS * height + r for r in rows], axis=0
            )
            cut += [one, two]
            one, two = trade(one, "dp", 1), trade(two, "dp", 2)
            for n in range(size):
                chunks[group * size + n].append(((one, n), (two, n)))
    return chunks, cut


def scatter_dp(parts, *last):
    count = lax.axis_size("dp")
    if count == 4:
        half = parts[3].shape[0] // 2
        near_one = trade(parts[3][:half], "dp", 1)
        near_two = trade(parts[3][half:], "dp", 2)
        for_two = jnp.concatenate([add_rounded(parts[2][:half], near_one), parts[2][half:]], axis=0)
        for_one = jnp.concatenate([parts[1][:half], add_rounded(parts[1][half:], near_two)], axis=0)
        got_one = trade(for_one, "dp", 1)
        got_two = after(trade(for_two, "dp", 2), *last)
        return parts[0].astype(F32) + got_one.astype(F32) + got_two.astype(F32)
    mask = count // 2
    while mask:
        parts = [
            add_rounded(parts[p], trade(parts[p + mask], "dp", mask)) for p in range(mask)
        ]
        mask //= 2
    return parts[0].astype(F32)


def add_rounded(one, two):
    return (one.astype(F32) + two.astype(F32)).astype(BF16)


def relative(block, axis, index, count):
    width = block.shape[axis] // count
    mask = 1
    while mask < count:
        flipped = jnp.concatenate(
            [
                lax.slice_in_dim(block, (b ^ mask) * width, ((b ^ mask) + 1) * width, axis=axis)
                for b in range(count)
            ],
            axis=axis,
        )
        block = jnp.where((index & mask) > 0, flipped, block)
        mask *= 2
    return block


VMEM_LIMIT = 50 * 1024 * 1024
GELU_SCALE = 0.7978845608028654
LONG = pl.CostEstimate(flops=10**14, bytes_accessed=1, transcendentals=0)
BRIEF = pl.CostEstimate(flops=1, bytes_accessed=1, transcendentals=0)


def after(block, *earlier):
    return lax.optimization_barrier((block, *earlier))[0]


def whole_spec(shape):
    return pl.BlockSpec(shape, lambda *_: (0,) * len(shape), pipeline_mode=pl.Buffered(1))


def params():
    return pltpu.CompilerParams(vmem_limit_bytes=VMEM_LIMIT)


def nn(left_op, right_op):
    return product(left_op, right_op, 1, 0)


def nt(left_op, right_op):
    return product(left_op, right_op, 1, 1)


def late_split(height):
    return -(-height // 48) * 16


def pack_kernel(part, rank_part, rank, mp, *refs):
    query, key_value, output, gains, query_up, key_value_up, output_down = refs[:7]
    inputs, input_share, model_share, attn, one, late = refs[7:]
    heads = query.shape[1]
    one[...] = jnp.zeros_like(one)
    one[:part, :heads] = query[...]
    one[:part, heads:] = key_value[...]
    one[part : 2 * part, :heads] = output[...].T
    one[2 * part : 2 * part + 2, :part] = gains[...]
    first = 2 * part + 16
    one[first : first + rank_part, :heads] = query_up[0]
    one[first : first + rank_part, heads:] = key_value_up[0]
    one[first + rank_part :, :heads] = output_down[0]
    wide = inputs.shape[2]
    attn[wide:, :] = jnp.zeros_like(attn[wide:, :])
    for k in range(3):
        attn[:wide, k * rank : (k + 1) * rank] = inputs[0, k]
    row = 0
    for at in range(0, model_share.shape[3], rank):
        for k in range(2):
            late[row : row + rank_part, :] = model_share[0, k, :, at : at + rank]
            row += rank_part
    height = input_share.shape[2]
    for k in range(2):
        late[row : row + height, :] = input_share[0, 3 + k]
        row += height
    split = late_split(row)
    for k in range(3):
        rows = min(split, row - k * split)
        attn[wide : wide + rows, k * rank : (k + 1) * rank] = late[
            k * split : k * split + rows, :
        ]


def pack_pass(mp, arrays, mp_count, rank):
    query, key_value, output, gains, query_up, _, _, inputs, model_up = arrays
    part, rank_part = query.shape[0], query_up.shape[1]
    slice_width, columns = inputs.shape[2], model_up.shape[3] // mp_count
    rows = slice_width // mp_count
    late_rows = 2 * rank_part * (columns // rank) + 2 * rows
    shapes = [
        (slice_width + late_split(late_rows), 3 * rank),
        (2 * part + 16 + 2 * rank_part, query.shape[1] + key_value.shape[1]),
    ]

    def whole(shape):
        return pl.BlockSpec(shape, lambda s, mp: (0,) * len(shape))

    return pl.pallas_call(
        functools.partial(pack_kernel, part, rank_part, rank),
        grid_spec=pltpu.PrefetchScalarGridSpec(
            num_scalar_prefetch=1,
            grid=(1,),
            in_specs=[whole(a.shape) for a in arrays[:8]]
            + [
                pl.BlockSpec((1, 5, rows, rank), lambda s, mp: (0, 0, mp[0], 0)),
                pl.BlockSpec((1, 2, rank_part, columns), lambda s, mp: (0, 0, 0, mp[0])),
            ],
            out_specs=[whole(s) for s in shapes],
            scratch_shapes=[pltpu.VMEM((late_rows, rank), BF16)],
        ),
        out_shape=[jax.ShapeDtypeStruct(s, BF16) for s in shapes],
        compiler_params=params(),
        cost_estimate=BRIEF,
        name="pack_pass",
    )(mp, *arrays[:7], inputs, inputs, model_up)


def unpack_kernel(count, part, rank_part, *refs):
    pieces, (shared, inputs, late, lifted, out_down) = refs[: 2 * count], refs[2 * count :]
    rows = shared.shape[0] // count
    wide, rank = 2 * part, late.shape[2]
    heads = out_down.shape[1]
    height = late.shape[1]
    split = late_split(height)
    for p in range(count):
        attn, one = pieces[2 * p : 2 * p + 2]
        shared[p * rows : (p + 1) * rows, :] = one[:rows, :]
        here = slice(p * rank_part, (p + 1) * rank_part)
        lifted[here, :] = one[rows : rows + rank_part, :]
        out_down[here, :] = one[rows + rank_part :, :heads]
        inputs[p * wide : (p + 1) * wide, :] = attn[:wide, :]
        for k in range(3):
            number = min(split, height - k * split)
            late[p, k * split : k * split + number, :] = attn[
                wide : wide + number, k * rank : (k + 1) * rank
            ]


def unpack_pass(pieces, part, rank_part, rank, rows, columns, heads):
    count = len(pieces)
    joint = pieces[0][1].shape[1]
    late_rows = 2 * rank_part * (columns // rank) + 2 * rows
    flat = [b for pair in pieces for b in pair]
    shapes = [
        (count * (2 * part + 16), joint),
        (count * 2 * part, 3 * rank),
        (count, late_rows, rank),
        (count * rank_part, joint),
        (count * rank_part, heads),
    ]
    return pl.pallas_call(
        functools.partial(unpack_kernel, count, part, rank_part),
        grid=(1,),
        in_specs=[whole_spec(b.shape) for b in flat],
        out_specs=[whole_spec(s) for s in shapes],
        out_shape=[jax.ShapeDtypeStruct(s, BF16) for s in shapes],
        compiler_params=params(),
        cost_estimate=BRIEF,
        name="unpack_pass",
    )(*flat)


def shared_kernel(count, part, core, own, other, joint, output, gains):
    rows = own.shape[0] // count
    heads = output.shape[1]
    gains[...] = jnp.zeros_like(gains)
    for e in range(2):

        @pl.when(core[0] == e)
        def _(e=e):
            for side, source in ((e, own), (1 - e, other)):
                for p in range(count):
                    here = slice((2 * p + side) * part, (2 * p + side + 1) * part)
                    first = p * rows
                    joint[here, :] = source[first : first + part, :]
                    output[here, :] = source[first + part : first + 2 * part, :heads]
                    gains[:2, here] = source[first + 2 * part : first + 2 * part + 2, :part]


def shared_pass(core, own, other, count, part, heads):
    shapes = [(count * 2 * part, own.shape[1]), (count * 2 * part, heads), (16, count * 2 * part)]
    return pl.pallas_call(
        functools.partial(shared_kernel, count, part),
        grid=(1,),
        in_specs=[pl.BlockSpec(memory_space=pltpu.SMEM)] + [whole_spec(own.shape)] * 2,
        out_specs=[whole_spec(s) for s in shapes],
        out_shape=[jax.ShapeDtypeStruct(s, BF16) for s in shapes],
        compiler_params=params(),
        cost_estimate=BRIEF,
        name="shared_pass",
    )(core, own, other)


def late_kernel(rank_part, rows, count, late, model, inputs):
    rank = late.shape[3]
    for p in range(count):
        for n in range(model.shape[2] // rank):
            for k in range(2):
                first = (2 * n + k) * rank_part
                model[k, p * rank_part : (p + 1) * rank_part, n * rank : (n + 1) * rank] = late[
                    0, p, first : first + rank_part, :
                ]
        first = 2 * rank_part * (model.shape[2] // rank)
        for k in range(2):
            inputs[p, 0, :, k * rank : (k + 1) * rank] = late[
                0, p, first + k * rows : first + (k + 1) * rows, :
            ]


def late_pass(late, rows, columns, rank_part):
    mp_count, count, height, rank = late.shape
    model, inputs = pl.pallas_call(
        functools.partial(late_kernel, rank_part, rows, count),
        grid=(mp_count,),
        in_specs=[pl.BlockSpec((1, count, height, rank), lambda z: (z, 0, 0, 0))],
        out_specs=[
            pl.BlockSpec((2, rank, columns), lambda z: (0, 0, z)),
            pl.BlockSpec((count, 1, rows, 2 * rank), lambda z: (0, z, 0, 0)),
        ],
        out_shape=[
            jax.ShapeDtypeStruct((2, rank, mp_count * columns), BF16),
            jax.ShapeDtypeStruct((count, mp_count, rows, 2 * rank), BF16),
        ],
        compiler_params=params(),
        cost_estimate=BRIEF,
        name="late_pass",
    )(late)
    return model, inputs.reshape(count * mp_count * rows, 2 * rank)


def ffn_blocks(arrays, chunk, side):
    gate_up, down, lora_gate_up, lora_hidden = arrays

    def column(s, core):
        return side(core[0]) * CHUNKS + s

    return [
        pl.BlockSpec((2, gate_up.shape[1], chunk), lambda s, core: (0, 0, column(s, core))),
        pl.BlockSpec((chunk, down.shape[1]), lambda s, core: (column(s, core), 0)),
        pl.BlockSpec(
            (1, 2, lora_gate_up.shape[2], chunk), lambda s, core: (0, 0, 0, column(s, core))
        ),
        pl.BlockSpec((1, lora_hidden.shape[1], chunk), lambda s, core: (0, 0, column(s, core))),
    ]


def ffn_rows(gate_up, down, lora_gate_up, lora_hidden):
    return [
        gate_up[0],
        gate_up[1],
        down[...].T,
        jnp.concatenate([lora_gate_up[0, 0], lora_gate_up[0, 1], lora_hidden[0]], axis=0),
    ]


def give_kernel(core, gate_up, down, lora_gate_up, lora_hidden, given):
    first = 0
    for block in ffn_rows(gate_up, down, lora_gate_up, lora_hidden):
        given[first : first + block.shape[0], :] = block
        first += block.shape[0]


def give_pass(core, arrays, chunk):
    part, rank_part = arrays[0].shape[1], arrays[3].shape[1]
    height = 3 * (part + rank_part)
    return pl.pallas_call(
        give_kernel,
        grid_spec=pltpu.PrefetchScalarGridSpec(
            num_scalar_prefetch=1,
            grid=(CHUNKS,),
            in_specs=ffn_blocks(arrays, chunk, lambda me: 1 - me),
            out_specs=pl.BlockSpec((height, chunk), lambda s, core: (s, 0)),
        ),
        out_shape=jax.ShapeDtypeStruct((CHUNKS * height, chunk), BF16),
        compiler_params=params(),
        cost_estimate=BRIEF,
        name="give_pass",
    )(core, *arrays)


def bundle_kernel(part, core, gate_up, down, lora_gate_up, lora_hidden, taken, bundle):
    own_first = core[0] == 0
    one, two = bundle.at[0], bundle.at[1]
    gate, upper, lower, lifted = ffn_rows(gate_up, down, lora_gate_up, lora_hidden)

    def pair(own, start):
        other = taken[start : start + part, :]
        return jnp.where(own_first, own, other), jnp.where(own_first, other, own)

    one[:part, :], one[part : 2 * part, :] = pair(gate, 0)
    two[:part, :], two[part : 2 * part, :] = pair(upper, part)
    one[2 * part : 3 * part, :], two[2 * part : 3 * part, :] = pair(lower, 2 * part)
    one[3 * part :, :] = lifted
    two[3 * part :, :] = taken[3 * part :, :]


def bundle_pass(core, arrays, taken, chunk):
    part = arrays[0].shape[1]
    height = taken.shape[0] // CHUNKS
    out = pl.pallas_call(
        functools.partial(bundle_kernel, part),
        grid_spec=pltpu.PrefetchScalarGridSpec(
            num_scalar_prefetch=1,
            grid=(CHUNKS,),
            in_specs=ffn_blocks(arrays, chunk, lambda me: me)
            + [pl.BlockSpec((height, chunk), lambda s, core: (s, 0))],
            out_specs=pl.BlockSpec((2, height, chunk), lambda s, core: (0, s, 0)),
        ),
        out_shape=jax.ShapeDtypeStruct((2, CHUNKS * height, chunk), BF16),
        compiler_params=params(),
        cost_estimate=BRIEF,
        name="bundle_pass",
    )(core, *arrays, taken)
    return out.reshape(2 * CHUNKS * height, chunk)


def simple_pass(kernel, name, inputs, shapes, scalars=None, cost=BRIEF):
    specs = [whole_spec(a.shape) for a in inputs]
    if scalars is not None:
        inputs = (scalars, *inputs)
        specs = [pl.BlockSpec(memory_space=pltpu.SMEM)] + specs
    return pl.pallas_call(
        kernel,
        grid=(1,),
        in_specs=specs,
        out_specs=[whole_spec(shape) for shape, _ in shapes],
        out_shape=[jax.ShapeDtypeStruct(shape, dtype) for shape, dtype in shapes],
        compiler_params=params(),
        cost_estimate=cost,
        name=name,
    )(*inputs)


def tn(left_op, right_op):
    return product(left_op, right_op, 0, 0)


def rank_order(block, rank, shift):
    row = lax.broadcasted_iota(jnp.int32, (rank, rank), 0)
    column = lax.broadcasted_iota(jnp.int32, (rank, rank), 1)
    swap = (jnp.bitwise_xor(row, shift) == column).astype(F32).astype(BF16)
    parts = [
        nn(block[:, at : at + rank], swap).astype(BF16)
        for at in range(0, block.shape[1], rank)
    ]
    return jnp.concatenate(parts, axis=1)


def inverse_rms(values):
    return lax.rsqrt(jnp.mean(values * values, axis=-1, keepdims=True) + EPS)


def project_kernel(place, rows, gains, inputs, joint, lifted, cosine, sine, *outs):
    normed, ranks, query, joint_part = outs
    heads = query.shape[1]
    rank = inputs.shape[1] // 3
    values = rows[...].astype(F32)
    gain = gains[0:1, :].astype(F32)
    normed[...] = (values * inverse_rms(values) * gain).astype(BF16)
    ranks[...] = rank_order(nn(normed[...], inputs[...]).astype(BF16), rank, place[0])
    raw = nn(normed[...], joint[...])
    query_raw = raw[:, :heads] + nn(ranks[:, :rank], lifted[:, :heads])
    for at in range(0, heads, HEAD_SIZE):
        here = slice(at, at + HEAD_SIZE)
        query[:, here] = rotate(query_raw[:, here], cosine[...], sine[...]).astype(BF16)
    pick = jnp.where(place[1] == 1, ranks[:, rank : 2 * rank], ranks[:, 2 * rank :])
    joint_part[...] = (raw[:, heads:] + nn(pick, lifted[:, heads:])).astype(BF16)


def beside(blocks):
    return jnp.concatenate([blocks[n] for n in range(blocks.shape[0])], axis=1)


def head_probs(query, keys, rows_segment, columns_segment):
    count = query.shape[0]
    scores = nt(query, keys) * HEAD_SIZE ** (-0.5)
    row = lax.broadcasted_iota(jnp.int32, (count, count), 0)
    column = lax.broadcasted_iota(jnp.int32, (count, count), 1)
    allowed = (rows_segment == columns_segment) & (column <= row)
    scores = jnp.where(allowed, scores, NEGATIVE)
    powers = jnp.exp(scores - jnp.max(scores, axis=-1, keepdims=True))
    return powers / jnp.sum(powers, axis=-1, keepdims=True)


def attend_kernel(query, joint, cosine, sine, row_seg, column_seg, output, down, *outs):
    keys, flat, branch = outs
    width = output.shape[0]
    both = beside(joint)
    keys[...] = rotate(both[:, :HEAD_SIZE].astype(F32), cosine[...], sine[...]).astype(BF16)
    for at in range(0, flat.shape[1], HEAD_SIZE):
        here = slice(at, at + HEAD_SIZE)
        probs = head_probs(query[:, here], keys[...], row_seg[...], column_seg[...])
        flat[:, here] = nn(probs.astype(BF16), both[:, HEAD_SIZE:]).astype(BF16)
    branch[:, :width] = nt(flat[...], output[...]).astype(BF16)
    branch[:, width:] = nt(flat[...], down[...]).astype(BF16)


def second_kernel(place, rows, branch, model, gains, inputs, hidden, normed):
    width = rows.shape[1]
    rank = model.shape[1]
    hidden[...] = (
        rows[...].astype(F32)
        + branch[:, :width].astype(F32)
        + nn(branch[:, width:], model[0])
    )
    values = hidden[...]
    gain = gains[1:2, :].astype(F32)
    normed[:, :width] = (values * inverse_rms(values) * gain).astype(BF16)
    normed[:, width:] = rank_order(
        nn(normed[:, :width], inputs[...]).astype(BF16), rank, place[0]
    )


def early_kernel(block, early, late):
    rows, columns = early.shape[0], block.shape[1]
    early[:, :columns] = block[:rows, :]
    early[:, columns:] = block[rows:, columns - (early.shape[1] - columns) :]
    late[...] = block[rows:, : late.shape[1]]


def grad_kernel(rows, model, grad):
    width = rows.shape[1]
    grad[:, :width] = rows[...]
    grad[:, width:] = nt(rows[...], model[1]).astype(BF16)


def norm_back(values, gain, grad_norm):
    inverse = inverse_rms(values)
    weighted = grad_norm * gain
    grad_values = inverse * weighted - values * inverse**3 * jnp.mean(
        weighted * values, axis=-1, keepdims=True
    )
    return grad_values, jnp.sum(grad_norm * values * inverse, axis=0, keepdims=True)


def attend_back_kernel(place, summed, hidden, gains, inputs, grad_ffn, model, *refs):
    output, down, query, keys, joint, cosine, sine, row_seg, column_seg = refs[:9]
    grad_hidden, branch, rank_gu, rank_out, grad_query, grad_joint, grad_gain = refs[9:]
    width = hidden.shape[1]
    rank = down.shape[0]
    factor = HEAD_SIZE ** (-0.5)
    rank_gu[...] = rank_order(summed[:, width:], rank, place[0])
    grad_norm = summed[:, :width].astype(F32) + nt(rank_gu[...], inputs[...])
    values, gain_row = norm_back(hidden[...], gains[1:2, :].astype(F32), grad_norm)
    grad_gain[...] = jnp.broadcast_to(gain_row, grad_gain.shape)
    grad_hidden[...] = values + grad_ffn[...].astype(F32)
    branch[...] = grad_hidden[...].astype(BF16)
    rank_out[...] = nt(branch[...], model[0]).astype(BF16)
    grad_flat = (nn(branch[...], output[...]) + nn(rank_out[...], down[...])).astype(BF16)
    values_here = beside(joint)[:, HEAD_SIZE:]
    grad_keys = grad_values = 0.0
    for at in range(0, query.shape[1], HEAD_SIZE):
        here = slice(at, at + HEAD_SIZE)
        probs = head_probs(query[:, here], keys[...], row_seg[...], column_seg[...])
        grad_probs = nt(grad_flat[:, here], values_here)
        grad_values += tn(probs.astype(BF16), grad_flat[:, here])
        centre = jnp.sum(grad_probs * probs, axis=-1, keepdims=True)
        grad_scores = (probs * (grad_probs - centre)).astype(BF16)
        turned = rotate_back(nn(grad_scores, keys[...]) * factor, cosine[...], sine[...])
        grad_query[:, here] = turned.astype(BF16)
        grad_keys += tn(grad_scores, query[:, here]) * factor
    both = jnp.concatenate([rotate_back(grad_keys, cosine[...], sine[...]), grad_values], axis=1)
    kv = grad_joint.shape[2]
    for n in range(grad_joint.shape[0]):
        grad_joint[n] = both[:, n * kv : (n + 1) * kv].astype(BF16)


def project_back_kernel(place, grad_query, grad_kv, joint, lifted, out):
    heads = grad_query.shape[1]
    width, rank = joint.shape[0], lifted.shape[0]
    out[:, :width] = (
        nt(grad_query[...], joint[:, :heads]) + nt(grad_kv[...], joint[:, heads:])
    ).astype(BF16)
    pick = nt(grad_kv[...], lifted[:, heads:]).astype(BF16)
    none = jnp.zeros_like(pick)
    out[:, width : width + rank] = nt(grad_query[...], lifted[:, :heads]).astype(BF16)
    out[:, width + rank : width + 2 * rank] = jnp.where(place[1] == 1, pick, none)
    out[:, width + 2 * rank :] = jnp.where(place[1] == 1, none, pick)


def first_back_kernel(place, summed, rows, gains, inputs, grad_hidden, *outs):
    grad_rows, ranks, grad_gain = outs
    width = rows.shape[1]
    ranks[...] = rank_order(summed[:, width:], inputs.shape[1] // 3, place[0])
    grad_norm = summed[:, :width].astype(F32) + nt(ranks[...], inputs[...])
    values, gain_row = norm_back(rows[...].astype(F32), gains[0:1, :].astype(F32), grad_norm)
    grad_gain[...] = jnp.broadcast_to(gain_row, grad_gain.shape)
    grad_rows[...] = (values + grad_hidden[...]).astype(BF16)


def folded(block, width):
    blocks = [block[:, at : at + width] for at in range(0, block.shape[1], width)]
    return blocks[0] if len(blocks) == 1 else jnp.concatenate(blocks, axis=0)


def share_of(block, first, rows):
    total = jnp.zeros((rows, block.shape[1]), block.dtype)
    for at in range(0, block.shape[0], rows):
        total = jnp.where(first == at, block[at : at + rows], total)
    return total


def shares_kernel(count, share_rows, share_columns, place, normed, grad_query, grad_kv, ranks, branch, flat, *refs):
    rank_out, out_sum, second, rank_gu, down_sum, grad_ffn = refs[:6]
    mine, theirs, *rest = refs[6:]
    heads, kv = grad_query.shape[1], grad_kv.shape[1]
    width = normed.shape[1]
    rank = rank_out.shape[1]
    part, rank_part = width // (2 * count), rank // count
    own_first = place[2] == 0
    pick = jnp.where(place[1] == 1, ranks[:, rank : 2 * rank], ranks[:, 2 * rank : 3 * rank])

    def put(target, p, start, block):
        target[p, start : start + block.shape[0], :] = block.astype(BF16)
        return start + block.shape[0]

    def put_rest(p, start, block):
        rest[p][start : start + block.shape[0], :] = block.astype(BF16)
        return start + block.shape[0]

    lift_query = tn(ranks[:, :rank], grad_query[...])
    lift_kv = tn(pick, grad_kv[...])
    out_down = tn(rank_out[...], flat[...])
    for p in range(count):
        columns = slice(2 * p * part, 2 * (p + 1) * part)
        here = slice(p * rank_part, (p + 1) * rank_part)
        query = tn(normed[:, columns], grad_query[...])
        joint = tn(normed[:, columns], grad_kv[...])
        output = tn(branch[:, columns], flat[...])
        quarter = part * kv // heads
        for side, target in ((0, mine), (1, theirs)):
            first = [jnp.where(own_first, b[:part], b[part:]) for b in (query, joint, output)]
            other = [jnp.where(own_first, b[part:], b[:part]) for b in (query, joint, output)]
            blocks = first if side == 0 else other
            put(target, p, 0, blocks[0])
            for n in range(part // quarter):
                target[p, part : part + quarter, n * kv : (n + 1) * kv] = blocks[1][
                    n * quarter : (n + 1) * quarter
                ].astype(BF16)
            put(target, p, part + quarter, blocks[2])
        at = put_rest(p, 0, lift_query[here])
        small = rank_part * kv // heads
        for n in range(rank_part // small):
            rest[p][at : at + small, n * kv : (n + 1) * kv] = lift_kv[
                p * rank_part + n * small : p * rank_part + (n + 1) * small
            ].astype(BF16)
        at = put_rest(p, at + small, out_down[here])
        here_columns = pl.multiple_of(place[4], 128)
        for ranks_of, rows_of in ((out_sum, branch), (down_sum, grad_ffn)):
            value = tn(ranks_of[:, here], rows_of[:, pl.ds(here_columns, share_columns)])
            for block in range(0, share_columns, heads):
                at = put_rest(p, at, value[:, block : block + heads])
        if share_rows % 128 == 0:
            first = pl.multiple_of(2 * p * part + place[5], 128)
            value = tn(second[:, pl.ds(first, share_rows)], rank_gu[...])
        else:
            value = share_of(tn(second[:, columns], rank_gu[...]), place[5], share_rows)
        for block in range(0, value.shape[1], heads):
            at = put_rest(p, at, value[:, block : block + heads])


def add_kernel(*refs):
    total = 0.0
    for ref in refs[:-1]:
        total += ref[...].astype(F32).reshape(refs[-1].shape)
    refs[-1][...] = total.astype(refs[-1].dtype)


def add_pass(dtype, *blocks):
    inputs, specs = [], []
    for block in blocks:
        if isinstance(block, tuple):
            block, at = block
            specs.append(
                pl.BlockSpec(
                    (1, *block.shape[1:]), functools.partial(lambda at, t: (at, 0, 0), at)
                )
            )
            shape = block.shape[1:]
        else:
            specs.append(whole_spec(block.shape))
            shape = block.shape
        inputs.append(block)
    return pl.pallas_call(
        add_kernel,
        grid=(1,),
        in_specs=specs,
        out_specs=whole_spec(shape),
        out_shape=jax.ShapeDtypeStruct(shape, dtype),
        compiler_params=params(),
        cost_estimate=BRIEF,
        name="add_pass",
    )(*inputs)


def gate_kernel(count, width, rank_part, has_base, *refs):
    blocks, refs = refs[:4], refs[4:]
    pieces = [(refs[2 * p], refs[2 * p + 1]) for p in range(count)]
    refs = refs[2 * count :]
    bases, refs = (refs[:2], refs[2:]) if has_base else ((), refs)
    gated_ref, gate_ref, upper_ref, *outs = refs[:5]
    adapters = refs[5]
    start = pl.program_id(0) == 0
    rows = blocks[0].shape[0]
    part = width // 2
    rank = count * rank_part
    model_width = count * width
    for b in range(2):
        for k in range(3):
            first = 3 * part + k * rank_part
            for p in range(count):
                adapters[3 * b + k, p * rank_part : (p + 1) * rank_part, :] = pieces[p][b][
                    first : first + rank_part, :
                ]
    for b in range(2):
        normed, grad = blocks[b], blocks[2 + b]
        span = slice(b * rows, (b + 1) * rows)
        gate = nn(normed[:, model_width : model_width + rank], adapters[3 * b])
        upper = nn(normed[:, model_width + rank :], adapters[3 * b + 1])
        grad_gated = nn(grad[:, model_width:], adapters[3 * b + 2])
        for p in range(count):
            columns = slice(p * width, (p + 1) * width)
            gate += nn(normed[:, columns], pieces[p][0][:width, :])
            upper += nn(normed[:, columns], pieces[p][1][:width, :])
            for e in range(2):
                columns = slice(p * width + e * part, p * width + (e + 1) * part)
                grad_gated += nn(grad[:, columns], pieces[p][e][width : width + part, :])
        square = gate * gate
        bent = jnp.tanh(GELU_SCALE * gate * (1.0 + 0.044715 * square))
        half = 0.5 * (1.0 + bent)
        active = gate * half
        slope = half + 0.5 * gate * (1.0 - bent * bent) * GELU_SCALE * (
            1.0 + 3.0 * 0.044715 * square
        )
        gated_ref[span, :] = (active * upper).astype(BF16)
        gate_ref[span, :] = (grad_gated * upper * slope).astype(BF16)
        upper_ref[span, :] = (grad_gated * active).astype(BF16)

    def put(b, first, value):
        columns = slice(first, first + value.shape[1])
        before = outs[b][:, columns].astype(F32)
        base = bases[b][:, columns].astype(F32) if bases else jnp.zeros_like(before)
        value = value + jnp.where(start, base, before)
        outs[b][:, columns] = value.astype(outs[b].dtype)

    for p in range(count):
        value = nt(gate_ref[...], pieces[p][0][:width, :]) + nt(
            upper_ref[...], pieces[p][1][:width, :]
        )
        for b in range(2):
            put(b, p * width, value[b * rows : (b + 1) * rows])
    for b in range(2):
        span = slice(b * rows, (b + 1) * rows)
        put(b, model_width, nt(gate_ref[span, :], adapters[3 * b]))
        put(b, model_width + rank, nt(upper_ref[span, :], adapters[3 * b + 1]))


def gate_pass(normed_pair, grad_pair, chunks, width, rank_part, bases, last):
    blocks = (*normed_pair, *grad_pair)
    rows, columns = blocks[0].shape
    both_rows, size = 2 * rows, len(chunks)
    pairs = [block for pair in chunks[0] for block in pair]
    height = 3 * (width // 2 + rank_part)
    chunk = pairs[0][0].shape[1]
    tiled = pl.BlockSpec((both_rows, chunk), lambda t: (0, t))
    return pl.pallas_call(
        functools.partial(gate_kernel, len(chunks[0]), width, rank_part, bool(bases)),
        grid=(size,),
        in_specs=[whole_spec(a.shape) for a in blocks]
        + [
            pl.BlockSpec((height, chunk), functools.partial(lambda at, t: (at + t, 0), at))
            for _, at in pairs
        ]
        + [whole_spec(a.shape) for a in bases],
        out_specs=[tiled] * 3 + [whole_spec((rows, columns))] * 2,
        out_shape=[jax.ShapeDtypeStruct((both_rows, size * chunk), BF16)] * 3
        + [
            jax.ShapeDtypeStruct((rows, columns), F32 if last else BF16),
            jax.ShapeDtypeStruct((rows, columns), BF16),
        ],
        scratch_shapes=[pltpu.VMEM((6, len(chunks[0]) * rank_part, chunk), BF16)],
        compiler_params=pltpu.CompilerParams(vmem_limit_bytes=60 * 1024 * 1024),
        cost_estimate=BRIEF,
        name="gate_pass",
    )(*blocks, *[block for block, _ in pairs], *bases)


def down_kernel(count, rows, width, rank_part, chunks, *refs):
    acts, refs = refs[:chunks], refs[chunks:]
    outs, adapters = refs[-3:-1], refs[-1]
    part = width // 2
    pieces = [
        [refs[2 * (q * count + p) : 2 * (q * count + p) + 2] for p in range(count)]
        for q in range(chunks)
    ]
    for b in range(2):
        span = slice(b * rows, (b + 1) * rows)
        for p in range(count):
            for e in range(2):
                value = nt(acts[0][span, :], pieces[0][p][e][width : width + part, :])
                for q in range(1, chunks):
                    value += nt(acts[q][span, :], pieces[q][p][e][width : width + part, :])
                first = p * width + e * part
                outs[b][:, first : first + part] = value.astype(outs[b].dtype)
        value = 0.0
        first = 3 * part + 2 * rank_part
        for q in range(chunks):
            for p in range(count):
                adapters[p * rank_part : (p + 1) * rank_part, :] = pieces[q][p][b][
                    first : first + rank_part, :
                ]
            value += nt(acts[q][span, :], adapters[...])
        outs[b][:, count * width :] = value.astype(outs[b].dtype)


def down_pass(acts, chunks, width, rank_part):
    count = len(chunks[0])
    both_rows = acts[0][0].shape[0]
    chunk = chunks[0][0][0][0].shape[1]
    rows = both_rows // 2
    columns = count * (width + rank_part)
    height = 3 * (width // 2 + rank_part)
    pairs = [block for pieces in chunks for pair in pieces for block in pair]
    shapes = [
        jax.ShapeDtypeStruct((rows, columns), F32),
        jax.ShapeDtypeStruct((rows, columns), BF16),
    ]
    return pl.pallas_call(
        functools.partial(down_kernel, count, rows, width, rank_part, len(chunks)),
        grid=(1,),
        in_specs=[
            pl.BlockSpec(
                (both_rows, chunk),
                functools.partial(lambda n, t: (0, n), n),
                pipeline_mode=pl.Buffered(1),
            )
            for _, n in acts
        ]
        + [
            pl.BlockSpec(
                (height, chunk),
                functools.partial(lambda at, t: (at, 0), at),
                pipeline_mode=pl.Buffered(1),
            )
            for _, at in pairs
        ],
        out_specs=[whole_spec(s.shape) for s in shapes],
        out_shape=shapes,
        scratch_shapes=[pltpu.VMEM((count * rank_part, chunk), BF16)],
        compiler_params=params(),
        cost_estimate=BRIEF,
        name="down_pass",
    )(*[a for a, _ in acts], *[block for block, _ in pairs])


def sum_kernel(*refs):
    total = refs[0][...].astype(F32)
    for other in refs[1:-1]:
        total = total + other[...].astype(F32)
    refs[-1][...] = total.astype(BF16)


def sum_pass(*blocks):
    blocks = [b if isinstance(b, tuple) else (b, 0) for b in blocks]
    rows, columns = min((b.shape for b, _ in blocks), key=lambda shape: shape[0])
    steps = 4
    return pl.pallas_call(
        sum_kernel,
        grid=(steps,),
        in_specs=[
            pl.BlockSpec(
                (rows // steps, columns), functools.partial(lambda at, t: (at * steps + t, 0), at)
            )
            for _, at in blocks
        ],
        out_specs=pl.BlockSpec((rows // steps, columns), lambda t: (t, 0)),
        out_shape=jax.ShapeDtypeStruct((rows, columns), BF16),
        compiler_params=params(),
        cost_estimate=BRIEF,
        name="sum_pass",
    )(*[b for b, _ in blocks])


def turn_kernel(own, other, turned):
    rows = own.shape[0]
    turned[:, :rows] = own[...].T
    turned[:, rows:] = other[...].T


def turn_pass(own, other):
    rows, columns = own.shape
    tile = 256
    source = pl.BlockSpec((rows, tile), lambda t: (0, t))
    return pl.pallas_call(
        turn_kernel,
        grid=(columns // tile,),
        in_specs=[source, source],
        out_specs=pl.BlockSpec((tile, 2 * rows), lambda t: (t, 0)),
        out_shape=jax.ShapeDtypeStruct((columns, 2 * rows), own.dtype),
        compiler_params=params(),
        cost_estimate=BRIEF,
        name="turn_pass",
    )(own, other)


def weight_kernel(part, rank_part, sides, adds, aliased, core, *refs):
    gate, upper, gated = refs[:3]
    refs = refs[3:]
    rows = gate.shape[0] // 2
    outs = refs[-len(sides) :]
    for side, number, out in zip(sides, adds, outs):
        normed, grad, *ranks = refs[:5]
        added = refs[5 : 5 + number]
        refs = refs[5 + number :]

        def store(start, value):
            here = slice(start, start + value.shape[0])
            for other in added:
                value = value + other[here, :].astype(F32)
            out[here, :] = value.astype(out.dtype)

        for n, (columns, act) in enumerate(((normed, gate), (normed, upper), (grad, gated))):
            store(n * part, nn(columns[...], act[...]))
        span = slice(side * rows, (side + 1) * rows)
        for n, act in enumerate((gate, upper, gated)):
            store(3 * part + n * rank_part, nn(ranks[n][:, span], act[span, :]))


def weight_pass(core, normed_t, grad_t, width, rank_part, acts, chunk, at, count, items, held=()):
    both_rows = normed_t.shape[1]
    part = width // 2
    height = 3 * (part + rank_part)
    tile = min(256, chunk)
    model_blocks = (2 * grad_t.shape[0] - normed_t.shape[0]) // rank_part
    rank_blocks = (normed_t.shape[0] - grad_t.shape[0]) // rank_part

    def rows_of(index, side):
        return pl.BlockSpec(
            (part, both_rows),
            lambda t, core: (2 * index + (core[0] ^ side), 0),
            pipeline_mode=pl.Buffered(1),
        )

    def ranks_of(block):
        return pl.BlockSpec(
            (rank_part, both_rows), lambda t, core: (block, 0), pipeline_mode=pl.Buffered(1)
        )

    tiled = pl.BlockSpec((height, tile), lambda t, core: (at, t))
    inputs = [a for a, _ in acts]
    specs = [
        pl.BlockSpec(
            (both_rows, tile),
            functools.partial(lambda n, t, core: (0, n * (chunk // tile) + t), n),
        )
        for _, n in acts
    ]
    for index, side, added, _ in items:
        inputs += [normed_t, grad_t, normed_t, normed_t, grad_t, *[block for block, _ in added]]
        specs += [rows_of(index, side)] * 2
        specs += [ranks_of(model_blocks + n * rank_blocks + index) for n in (0, 1, 0)]
        specs += [
            pl.BlockSpec((height, tile), functools.partial(lambda n, t, core: (n, t), n))
            for _, n in added
        ]
    aliases = {1 + len(inputs) + n: n for n in range(len(held))}
    return pl.pallas_call(
        functools.partial(
            weight_kernel,
            part,
            rank_part,
            tuple(item[1] for item in items),
            tuple(len(item[2]) for item in items),
            len(held),
        ),
        grid_spec=pltpu.PrefetchScalarGridSpec(
            num_scalar_prefetch=1,
            grid=(chunk // tile,),
            in_specs=specs + [pl.BlockSpec(memory_space=pl.ANY) for _ in held],
            out_specs=[tiled] * len(items),
        ),
        out_shape=[jax.ShapeDtypeStruct((count * height, chunk), item[3]) for item in items],
        input_output_aliases=aliases,
        compiler_params=params(),
        cost_estimate=BRIEF,
        name="weight_pass",
    )(core, *inputs, *held)


def finish_kernel(part, rank_part, core, *refs):
    *mine, other = refs[:-4]
    gate_up, down, lora_gate_up, lora_hidden = refs[-4:]
    for side, sources in enumerate((mine, [other])):

        @pl.when(pl.program_id(0) == side)
        def _(sources=sources):
            def rows(start, height):
                total = sources[0][start : start + height, :].astype(F32)
                for source in sources[1:]:
                    total = total + source[start : start + height, :].astype(F32)
                return total

            gate_up[0] = rows(0, part)
            gate_up[1] = rows(part, part)
            down[...] = rows(2 * part, part).T
            lora_gate_up[0, 0] = rows(3 * part, rank_part)
            lora_gate_up[0, 1] = rows(3 * part + rank_part, rank_part)
            lora_hidden[0] = rows(3 * part + 2 * rank_part, rank_part)


def finish_pass(core, mine, other, part, rank_part, hidden):
    chunk = other.shape[1]
    height = other.shape[0] // CHUNKS

    def source(side, first=0):
        return pl.BlockSpec(
            (height, chunk),
            lambda s, q, core: (first + jnp.where(s == side, q, (CHUNKS - 1) * (1 - side)), 0),
        )

    def column(s, q, core):
        return (core[0] ^ s) * CHUNKS + q

    shapes = [
        jax.ShapeDtypeStruct(s, F32)
        for s in (
            (2, part, hidden),
            (hidden, part),
            (1, 2, rank_part, hidden),
            (1, rank_part, hidden),
        )
    ]
    grid_spec = pltpu.PrefetchScalarGridSpec(
        num_scalar_prefetch=1,
        grid=(2, CHUNKS),
        in_specs=[source(0, first) for _, first in mine] + [source(1)],
        out_specs=[
            pl.BlockSpec((2, part, chunk), lambda s, q, core: (0, 0, column(s, q, core))),
            pl.BlockSpec((chunk, part), lambda s, q, core: (column(s, q, core), 0)),
            pl.BlockSpec(
                (1, 2, rank_part, chunk), lambda s, q, core: (0, 0, 0, column(s, q, core))
            ),
            pl.BlockSpec((1, rank_part, chunk), lambda s, q, core: (0, 0, column(s, q, core))),
        ],
    )
    return pl.pallas_call(
        functools.partial(finish_kernel, part, rank_part),
        grid_spec=grid_spec,
        out_shape=shapes,
        compiler_params=params(),
        cost_estimate=BRIEF,
        name="finish_pass",
    )(core, *[block for block, _ in mine], other)


def dot(left_op, right_op):
    return jnp.dot(left_op, right_op, preferred_element_type=F32)


def pad_rows(block, rows, width):
    return jnp.pad(block, ((0, rows - block.shape[0]), (0, width - block.shape[1])))


def local(
    tokens,
    cotangent,
    lengths,
    bucket_loop_index,
    query_weight,
    key_value_weight,
    output_weight,
    gate_up_weight,
    down_weight,
    gains,
    adapter_input_down,
    adapter_query_up,
    adapter_key_value,
    adapter_output_down,
    adapter_hidden_down,
    adapter_model_up,
    adapter_gate_up,
):
    dp_count = lax.axis_size("dp")
    dp_id = lax.axis_index("dp")
    depth_id = lax.axis_index("depth")
    mp_index = lax.axis_index("mp")
    first_core = depth_id == 0
    row_count, model_width = tokens.shape
    slice_width = model_width // dp_count
    part_width = slice_width // 2
    heads_width = query_weight.shape[1]
    heads_here = heads_width // HEAD_SIZE
    kv_width = key_value_weight.shape[1]
    joint_width = heads_width + kv_width
    rank_part = adapter_query_up.shape[1]
    rank = rank_part * dp_count
    hidden = down_weight.shape[0]
    half_hidden = hidden // 2
    chunk = half_hidden // CHUNKS

    def partner(block):
        return trade(block, "depth", 1)

    def in_core_order(own, other):
        return jnp.where(first_core, own, other), jnp.where(first_core, other, own)

    keep_own = bucket_loop_index[0, depth_id] == depth_id
    tok_swap, grad_swap = partner(tokens), partner(cotangent)
    slot_id = jnp.where(keep_own, depth_id, 1 - depth_id)
    seq_lens = lengths[0, slot_id]
    places, segment, within, valid_rows = layout(seq_lens, row_count)
    cosine, sine_part = rotary(within, HEAD_SIZE)
    tok_rows = relative(jnp.where(keep_own, tokens, tok_swap), 1, dp_id, dp_count)
    grad_rows = relative(jnp.where(keep_own, cotangent, grad_swap), 1, dp_id, dp_count)
    grad_ffn = (grad_rows.astype(F32) * valid_rows[:, None]).astype(BF16)

    mp_count = lax.axis_size("mp")
    share_rows = slice_width // mp_count
    share_columns = model_width // mp_count
    core = depth_id[None].astype(jnp.int32)
    ffn_arrays = (gate_up_weight, down_weight, adapter_gate_up, adapter_hidden_down)
    taken = partner(give_pass(core, ffn_arrays, chunk))
    bundles = pack_pass(
        mp_index[None].astype(jnp.int32),
        (query_weight, key_value_weight, output_weight, gains)
        + (adapter_query_up, adapter_key_value, adapter_output_down)
        + (adapter_input_down, adapter_model_up),
        mp_count,
        rank,
    )
    bundle = bundle_pass(core, ffn_arrays, taken, chunk)
    pieces, hold = gather_pair(*bundles, bundle, tok_rows, grad_ffn)
    shared_own, input_attn, late, joint_lifted, out_down = unpack_pass(
        pieces, part_width, rank_part, rank, share_rows, share_columns, heads_width
    )
    joint_weight, out_weight, gains_all = shared_pass(
        core, shared_own, partner(shared_own), dp_count, part_width, heads_width
    )
    model_all, input_ffn = late_pass(
        lax.all_gather(late, "mp", axis=0, tiled=False),
        share_rows,
        share_columns,
        rank_part,
    )
    model_all = relative(model_all, 2, dp_id, dp_count)

    near = gather_near(after(bundle, *hold))
    height = 3 * (part_width + rank_part)

    is_key = mp_index * kv_width < HEAD_SIZE
    place = jnp.stack([dp_id * rank_part, is_key.astype(jnp.int32), depth_id, dp_id]
        + [((mp_index * share_columns // slice_width) ^ dp_id) * slice_width + mp_index * share_columns % slice_width, mp_index * share_rows]).astype(jnp.int32)
    row_segment, column_segment = segment[:, None], segment[None, :]
    normalized_rows, rank_rows, query_rows, joint_part = simple_pass(
        project_kernel,
        "project_pass",
        (tok_rows, gains_all, input_attn, joint_weight, joint_lifted, cosine, sine_part),
        [
            ((row_count, model_width), BF16),
            ((row_count, 3 * rank), BF16),
            ((row_count, heads_width), BF16),
            ((row_count, kv_width), BF16),
        ],
        place,
    )
    joint_key_value = lax.all_gather(joint_part, "mp", axis=0, tiled=False)
    key_rows, flat_heads, branch_part = simple_pass(
        attend_kernel,
        "attend_pass",
        (query_rows, joint_key_value, cosine, sine_part, row_segment, column_segment)
        + (out_weight, out_down),
        [
            ((row_count, HEAD_SIZE), BF16),
            ((row_count, heads_width), BF16),
            ((row_count, model_width + rank), BF16),
        ],
    )
    chunks, cut = gather_far(near, flat_heads, height)
    branch_sum = lax.psum(branch_part, "mp")
    branch_sum = after(branch_sum, *cut)
    rank_out = branch_sum[:, model_width:]

    hidden_state, normed_own = simple_pass(
        second_kernel,
        "second_pass",
        (tok_rows, branch_sum, model_all, gains_all, input_ffn),
        [((row_count, model_width), F32), ((row_count, model_width + 2 * rank), BF16)],
        place,
    )
    (grad_own,) = simple_pass(
        grad_kernel,
        "grad_pass",
        (grad_ffn, model_all),
        [((row_count, model_width + rank), BF16)],
    )
    grad_pair = (grad_own, partner(grad_own))
    grad_t = turn_pass(*grad_pair)
    normed_pair = (after(normed_own, grad_t), partner(normed_own))

    acts, sums = [], ()
    size = CHUNKS // GROUPS
    for group in range(GROUPS):
        *act, own_sum, other_sum = gate_pass(
            normed_pair,
            grad_pair,
            chunks[group * size : (group + 1) * size],
            slice_width,
            rank_part,
            sums,
            group == GROUPS - 1,
        )
        acts += [[(a, n) for a in act] for n in range(size)]
        sums = (own_sum, other_sum)
    normed_t = turn_pass(after(normed_own, sums[1]), normed_pair[1])
    grad_norm_ready = sum_pass(sums[0], partner(sums[1]))
    first_space = partner(grad_norm_ready[:16])
    grad_norm_sum = lax.psum(grad_norm_ready, "mp")

    def weight_share(items, hold, held=(), start=0, count=CHUNKS):
        for c in range(CHUNKS):
            gated, grad_gate, grad_upper = acts[c]
            if hold is not None:
                grad_gate = (after(grad_gate[0], hold), grad_gate[1])
            held = weight_pass(
                core,
                normed_t,
                grad_t,
                slice_width,
                rank_part,
                (grad_gate, grad_upper, gated),
                chunk,
                start + c,
                count,
                items,
                held,
            )
        return held

    sends, held, last_sent = (), (), ()
    if dp_count == 4:
        sends = weight_share(
            [(3, 0, (), BF16), (3, 1, (), BF16)], first_space, count=2 * CHUNKS
        )
        sends = weight_share(
            [(1, 0, (), BF16), (2, 1, (), BF16)], first_space, sends, CHUNKS, 2 * CHUNKS
        )
        near_one, near_two = trade(sends[0], "dp", 1), trade(sends[1], "dp", 2)
        held = weight_share([(1, 1, (), BF16), (2, 0, (), BF16)], sends[0])

    acts_down = [(after(a[0][0], first_space, *sends), a[0][1]) for a in acts]
    ffn_own, ffn_given = down_pass(acts_down, chunks, slice_width, rank_part)
    ffn_ready = sum_pass(ffn_own, partner(ffn_given))
    grad_norm_sum = after(grad_norm_sum, ffn_ready)
    if dp_count == 4:
        grad_norm_sum = after(grad_norm_sum, *held)
    half_rows = row_count // 2
    ffn_first, ffn_last = simple_pass(
        early_kernel,
        "early_pass",
        (ffn_ready,),
        [((half_rows, model_width + 2 * rank), BF16), ((half_rows, model_width), BF16)],
    )
    ffn_first = after(ffn_first, grad_norm_sum)
    grad_norm_sum = after(grad_norm_sum, partner(ffn_first))
    ffn_first = lax.psum(ffn_first, "mp")
    rank_down = jnp.concatenate(
        [ffn_first[:, model_width : model_width + rank], ffn_first[:, model_width + rank :]],
        axis=0,
    )

    grad_hidden, grad_branch, grad_rank_gu, grad_rank_out, grad_query, grad_joint, gain_two = (
        simple_pass(
            attend_back_kernel,
            "attend_back_pass",
            (grad_norm_sum, hidden_state, gains_all, input_ffn, grad_ffn, model_all)
            + (out_weight, out_down, query_rows, key_rows, joint_key_value)
            + (cosine, sine_part, row_segment, column_segment),
            [
                ((row_count, model_width), F32),
                ((row_count, model_width), BF16),
                ((row_count, 2 * rank), BF16),
                ((row_count, rank), BF16),
                ((row_count, heads_width), BF16),
                ((mp_count, row_count, kv_width), BF16),
                ((8, model_width), F32),
            ],
            place,
            LONG,
        )
    )
    grad_kv = lax.psum_scatter(after(grad_joint, ffn_first), "mp", scatter_dimension=0, tiled=False)
    if dp_count == 4:
        near_one, near_two = after(near_one, grad_query), after(near_two, grad_query)
        last_one = sum_pass(held[0], (near_two, 0))
        last_two = sum_pass(held[1], (near_one, 0))
        last_sent = (trade(last_one, "dp", 1), trade(last_two, "dp", 2))
    (grad_norm_part,) = simple_pass(
        project_back_kernel,
        "project_back_pass",
        (grad_query, grad_kv, joint_weight, joint_lifted),
        [((row_count, model_width + 3 * rank), BF16)],
        place,
    )
    ffn_last = after(ffn_last, ffn_first)
    grad_norm_one, ffn_last = lax.psum((grad_norm_part, ffn_last), "mp")
    grad_rows, grad_rank_qkv, gain_one = simple_pass(
        first_back_kernel,
        "first_back_pass",
        (grad_norm_one, tok_rows, gains_all, input_attn, grad_hidden),
        [
            ((row_count, model_width), BF16),
            ((row_count, 3 * rank), BF16),
            ((8, model_width), F32),
        ],
        place,
        LONG,
    )
    grad_input = relative(grad_rows, 1, dp_id, dp_count)
    grad_input_attn = product(normalized_rows, grad_rank_qkv, 0, 0).astype(BF16)

    quarter = part_width * kv_width // heads_width
    small = rank_part * kv_width // heads_width
    blocks = share_columns // heads_width
    mp_rows = 2 * blocks * rank_part + 2 * rank // heads_width * share_rows
    rest_rows = 2 * rank_part + small + mp_rows
    base_rows = 2 * part_width + quarter
    shares, shares_given, *rest = simple_pass(
        functools.partial(shares_kernel, dp_count, share_rows, share_columns),
        "shares_pass",
        (after(normalized_rows, grad_norm_part), grad_query, grad_kv, rank_rows, grad_branch, flat_heads)
        + (grad_rank_out, rank_out, normed_own, grad_rank_gu, rank_down, grad_ffn),
        [
            ((dp_count, base_rows, heads_width), BF16),
            ((dp_count, base_rows, heads_width), BF16),
            *[((rest_rows, heads_width), BF16)] * dp_count,
        ],
        place,
    )
    own = ()
    if dp_count == 4:
        own = weight_share([(0, 0, (), BF16), (0, 1, (), BF16)], grad_norm_part)
    shares_given = after(shares_given, *own)
    shares_got = after(partner(shares_given), grad_input_attn)

    def shared(p, dtype, *more):
        return add_pass(dtype, (shares, p), (shares_got, p), *more)

    far_share = shared(dp_count - 1, BF16)
    if dp_count == 4:
        mine = [(own[0], 0), (near_one, CHUNKS), (last_sent[1], 0)]
        theirs = sum_pass(
            own[1], (near_two, 1), after(last_sent[0], last_sent[1], far_share)
        )
        summed = after(grad_rank_qkv, theirs)
        theirs = partner(theirs)
    else:
        summed = grad_rank_qkv
        by_index = [
            weight_share([(p, 0, (), BF16), (p, 1, (), BF16)], None)
            for p in range(dp_count)
        ]
        mine = [(scatter_dp([b[0] for b in by_index]), 0)]
        theirs = partner(scatter_dp([b[1] for b in by_index]).astype(BF16))
    grad_w_gateup, grad_w_down, grad_lora_gateup, grad_lora_hidden = finish_pass(
        core, mine, theirs, part_width, rank_part, hidden
    )

    ffn_sum = jnp.concatenate([ffn_first[:, :model_width], ffn_last], axis=0)
    output = hidden_state + ffn_sum.astype(F32) + dot(rank_down, model_all[1])
    result_rows = relative(output.astype(BF16), 1, dp_id, dp_count)
    result_rows = after(result_rows, grad_w_down)
    grad_input = after(grad_input, grad_w_down)

    if dp_count == 4:
        near_share = trade(far_share, "dp", 1)
        near_rest = after(trade(after(rest[3], *own), "dp", 2), summed)
        share_one, rest_two = trade(after(shared(1, BF16), summed), "dp", 1), trade(after(rest[2], near_rest), "dp", 2)
        share_two = trade(shared(2, BF16, near_share), "dp", 2)
        rest_one = trade(add_pass(BF16, rest[1], near_rest), "dp", 1)
        share_own = shared(0, F32, after(share_one, grad_w_down), share_two)
        rest_own = add_pass(F32, rest[0], after(rest_one, grad_rank_qkv), rest_two)
    else:
        share_own = scatter_dp([shared(p, BF16) for p in range(dp_count)])
        rest_own = scatter_dp([rest[p] for p in range(dp_count)])

    share_own, rest_own = after(share_own, grad_rank_qkv), after(rest_own, grad_rank_qkv)

    def unfolded(block, width, heights):
        rows = heights
        columns = [block[at : at + rows, :width] for at in range(0, block.shape[0], rows)]
        return jnp.concatenate(columns, axis=1)

    def side_by_side(block, width):
        return jnp.concatenate(
            [block[:, at : at + width] for at in range(0, heads_width, width)], axis=0
        )

    grad_w_query = share_own[:part_width]
    grad_w_keyval = side_by_side(share_own[part_width : part_width + quarter], kv_width)
    grad_w_output = share_own[part_width + quarter :].T
    at = rank_part
    grad_lora_query = rest_own[:at][None]
    grad_lora_keyval = side_by_side(rest_own[at : at + small], kv_width)[None]
    at += small
    grad_lora_out = rest_own[at : at + rank_part][None]
    at += rank_part
    gathered = lax.all_gather(rest_own[at:].astype(BF16), "mp", axis=0, tiled=False).astype(F32)
    model_own, at = [], 0
    for _ in range(2):
        block = gathered[:, at : at + blocks * rank_part].reshape(-1, heads_width)
        model_own.append(unfolded(block, heads_width, rank_part))
        at += blocks * rank_part
    grad_lora_model = jnp.stack(model_own)[None]
    ffn_in_own = jnp.concatenate(
        [unfolded(gathered[z, at:], heads_width, share_rows) for z in range(mp_count)], axis=0
    )

    def by_dp(block):
        return block.reshape(dp_count, block.shape[0] // dp_count, block.shape[1])

    gain_grads = jnp.stack([gain_one[0], gain_two[0]]).astype(BF16)
    gain_grads = gain_grads.reshape(2, dp_count, slice_width)
    grad_input_attn = by_dp(grad_input_attn)
    attn_in_own = scatter_dp(
        [
            jnp.concatenate(
                [grad_input_attn[p], pad_rows(gain_grads[:, p], 16, 3 * rank)], axis=0
            )
            for p in range(dp_count)
        ],
        grad_w_down,
    )
    gain_grads = attn_in_own[slice_width : slice_width + 2, :slice_width]
    gain_first, gain_second = gain_grads[:, :part_width], gain_grads[:, part_width:]
    grad_w_gains = jnp.where(first_core, gain_first, gain_second) + partner(
        jnp.where(first_core, gain_second, gain_first)
    )
    input_own = jnp.concatenate([attn_in_own[:slice_width], ffn_in_own], axis=1)
    grad_lora_in = jnp.stack([input_own[:, k * rank : (k + 1) * rank] for k in range(5)])[None]

    mixed_rows = jnp.where(keep_own, result_rows, partner(result_rows))
    grad_tokens = jnp.where(keep_own, grad_input, partner(grad_input))
    return (
        mixed_rows,
        grad_tokens,
        grad_w_query,
        grad_w_keyval,
        grad_w_output,
        grad_w_gateup,
        grad_w_down,
        grad_w_gains,
        grad_lora_in,
        grad_lora_query,
        grad_lora_keyval,
        grad_lora_out,
        grad_lora_hidden,
        grad_lora_model,
        grad_lora_gateup,
    )


def solution(mesh):
    return jax.shard_map(
        local,
        mesh=mesh,
        in_specs=(
            P(("dp", "depth"), None),
            P(("dp", "depth"), None),
            P("dp", None, None),
            P("dp", None),
            P(("dp", "depth"), "mp"),
            P(("dp", "depth"), "mp"),
            P("mp", ("dp", "depth")),
            P(None, ("dp", "depth"), "mp"),
            P("mp", ("dp", "depth")),
            P(None, ("dp", "depth")),
            P("depth", None, "dp", None),
            P("depth", "dp", "mp"),
            P("depth", "dp", "mp"),
            P("depth", "dp", "mp"),
            P("depth", "dp", "mp"),
            P("depth", None, "dp", None),
            P("depth", None, "dp", "mp"),
        ),
        out_specs=(
            P(("dp", "depth"), None),
            P(("dp", "depth"), None),
            P(("dp", "depth"), "mp"),
            P(("dp", "depth"), "mp"),
            P("mp", ("dp", "depth")),
            P(None, ("dp", "depth"), "mp"),
            P("mp", ("dp", "depth")),
            P(None, ("dp", "depth")),
            P("depth", None, "dp", None),
            P("depth", "dp", "mp"),
            P("depth", "dp", "mp"),
            P("depth", "dp", "mp"),
            P("depth", "dp", "mp"),
            P("depth", None, "dp", None),
            P("depth", None, "dp", "mp"),
        ),
        check_vma=False,
    )
```
